32 devices in a mesh: items: 2 (over core), seq: 16 (over z, y, x).
Axes of the slice: x: 2, y: 2, z: 4, core: 2. Of those that a mesh axis runs over, the one named last changes fastest.
Arguments:
- frames: bfloat16 [2, 4096, 1024], P('items', 'seq'), may hold values from -6 to 6
- lengths: int32 [2, 3], P('items'), may hold values from 128 to 3712, as said below
- w_qkv: bfloat16 [1024, 3072], replicated, may hold values from -0.1875 to 0.1875
- w_out: bfloat16 [1024, 1024], replicated, may hold values from -3 to 3
- w_up: bfloat16 [1024, 4096], replicated, may hold values from -0.1875 to 0.1875
- w_down: bfloat16 [4096, 1024], replicated, may hold values from -0.09375 to 0.09375
- gain_one: float32 [1024], replicated, may hold values from 0.1 to 1.9
- gain_two: float32 [1024], replicated, may hold values from 0.1 to 1.9
- cotangent: bfloat16 [2, 4096, 1024], P('items', 'seq'), may hold values from -6 to 6
Outputs:
- output: bfloat16 [2, 4096, 1024], P('items', 'seq')
- grad_frames: float32 [2, 4096, 1024], P('items', 'seq')
- grad_qkv: float32 [1024, 3072], P('seq')
- grad_out: float32 [1024, 1024], P('seq')
- grad_up: float32 [1024, 4096], P('seq')
- grad_down: float32 [4096, 1024], P('seq')
- grad_gain_one: float32 [1024], P('seq')
- grad_gain_two: float32 [1024], P('seq')
The draws below stay inside these ranges and needn't reach their ends.
Inputs may be any that keep to these rules, and one draw needn't show every extreme that they name: Each row holds a first utterance of more than 128 and fewer than 256 frames, then one of exactly 3712 frames, then one of exactly 128 frames; the lengths sum to less than 4096 and the frames after their sum are padding.
All inputs are finite; a program needn't handle non-finite values.
Results may differ from the reference program's by a relative error of at most 0.023.
Values may be sent and summed in bfloat16 or wider, within the bound.
No kernel may reach another device: no remote copies, remote signals or barrier semaphores. Data moves between devices by JAX's collectives and lax.ppermute only.
A program may use at most 320 MiB of HBM per device.

```python
import math
import jax
import jax.numpy as jnp
from jax import lax

D = 1024
HEADS = 16
HEAD_DIM = 64
FF = 4096
TOK_DEV = 256
UTT = 3
GROUPS = 2
GRP = 4096


def draw_lengths(key, part):
    key = jax.random.fold_in(key, 7)
    first_length = jax.random.randint(key, (GROUPS, 1), TOK_DEV // 2 + 1, TOK_DEV)
    long_length = jnp.full((GROUPS, 1), GRP - 3 * TOK_DEV // 2, jnp.int32)
    last_length = jnp.full((GROUPS, 1), TOK_DEV // 2, jnp.int32)
    rows_out = jnp.concatenate([first_length.astype(jnp.int32), long_length, last_length], axis=1)
    return rows_out.astype(jnp.int32)


def shard_levels(stream_key, shape, cuts, smallest, largest):
    def one(position, blocks):
        heights = jax.random.uniform(jax.random.fold_in(jax.random.fold_in(stream_key, 6), position), (blocks,), jnp.float32, smallest / len(cuts), largest / len(cuts))
        return jnp.repeat(jnp.exp(heights), shape[position] // blocks).reshape((-1,) + (1,) * (len(shape) - position - 1))

    level = one(*cuts[0])
    for cut in cuts[1:]:
        level = level * one(*cut)
    return level


def gaussian(own_key, extent, scale, reach, cuts=(), kind=jnp.bfloat16):
    array = jax.random.normal(own_key, extent, jnp.float32) * scale
    if len(cuts) > 0:
        array = shard_levels(own_key, extent, cuts, -0.22, 0.18) * array
    return jnp.clip(array, min=-reach, max=reach).astype(kind)


def setup_inputs(seed: int = 0) -> dict:
    splits = jax.random.split(jax.random.key(seed), 10)
    return {
        "frames": gaussian(splits[0], (GROUPS, GRP, D), 1.0, 6.0, ((0, 2), (1, 16))),
        "lengths": draw_lengths(jax.random.fold_in(splits[9], 71), 0),
        "w_qkv": gaussian(splits[2], (D, 3 * D), D ** -0.5, 0.1875),
        "w_out": gaussian(splits[3], (D, D), 4 ** -0.5, 3.0),
        "w_up": gaussian(splits[4], (D, FF), D ** -0.5, 0.1875),
        "w_down": gaussian(splits[5], (FF, D), FF ** -0.5, 0.09375),
        "gain_one": jnp.clip(1.0 + 0.18 * jax.random.normal(splits[6], (D,), jnp.float32), 0.1, 1.9),
        "gain_two": jnp.clip(1.0 + 0.18 * jax.random.normal(splits[7], (D,), jnp.float32), 0.1, 1.9),
        "cotangent": gaussian(splits[8], (GROUPS, GRP, D), 1.0, 6.0, ((0, 2), (1, 16))),
    }


@jax.custom_vjp
def low(v):
    return lax.optimization_barrier(v.astype(jnp.bfloat16)).astype(jnp.float32)

@jax.custom_vjp
def low_back(v):
    return v

def low_keep(v):
    return (low(v), None)

def low_pass(kept, grad):
    return (grad,)

def back_keep(v):
    return (v, None)

def back_low(kept, grad):
    return (low(grad),)
low.defvjp(low_keep, low_pass)
low_back.defvjp(back_keep, back_low)
eps = 1e-05
masked = -1e+30
precise = lax.Precision.HIGHEST

def norm_scaled(inputs, gain):
    centred = inputs - lax.optimization_barrier(jnp.mean(inputs, axis=-1, keepdims=True))
    spread = lax.optimization_barrier(jnp.mean(centred * centred, axis=-1, keepdims=True))
    return centred * lax.rsqrt(spread + eps) * gain

def frame_ids(lengths):
    utter_ends = jnp.cumsum(lengths, axis=1).astype(jnp.int32)
    places = jnp.arange(GRP, dtype=jnp.int32)
    labels = lax.optimization_barrier(jnp.sum((places[None, :, None] >= utter_ends[:, None, :]).astype(jnp.int32), axis=2)).astype(jnp.int32)
    return (labels, places)

def attention(queries, key_rows, value_rows, labels, places):
    block_rows = math.gcd(GRP, 512)
    block_count = GRP // block_rows
    score_scale = HEAD_DIM ** (-0.5)
    key_heads = key_rows.reshape(GRP, HEADS, HEAD_DIM)
    value_heads = value_rows.reshape(GRP, HEADS, HEAD_DIM)

    def one_block(block_parts):
        block_query, row_labels, row_places = block_parts
        raw_scores = jnp.einsum('qhd,khd->qhk', block_query, key_heads, precision=precise) * score_scale
        scores = low_back(raw_scores)
        allowed = ((row_labels[:, None] == labels[None, :]) & (row_places[:, None] >= places[None, :]))[:, None, :]
        scores = jnp.where(allowed, scores, masked)
        row_peak = lax.optimization_barrier(jnp.max(scores, axis=-1, keepdims=True))
        weights = jnp.where(allowed, jnp.exp(scores - row_peak), 0.0)
        attn_probs = weights / lax.optimization_barrier(jnp.sum(weights, axis=-1, keepdims=True))
        return jnp.einsum('qhk,khd->qhd', low(attn_probs), value_heads, precision=precise)
    attended = lax.map(jax.checkpoint(one_block), (queries.reshape(block_count, block_rows, HEADS, HEAD_DIM), labels.reshape(block_count, block_rows), places.reshape(block_count, block_rows)))
    return attended.reshape(GRP, HEADS * HEAD_DIM)

def group_forward(weights, inputs, labels, present, places):
    w_qkv, w_out, w_up, w_down, gain_one, gain_two = weights
    feature_count = HEADS * HEAD_DIM
    normed_one = low(norm_scaled(inputs, gain_one))
    packed = low(low_back(jnp.dot(normed_one, w_qkv, precision=precise)))
    attended = attention(packed[:, :feature_count], packed[:, feature_count:2 * feature_count], packed[:, 2 * feature_count:], labels, places)
    attended = low(low_back(attended * present[:, None]))
    middle = inputs + low_back(jnp.dot(attended, w_out, precision=precise))
    normed_two = low(norm_scaled(middle, gain_two))
    hidden = low_back(jnp.dot(normed_two, w_up, precision=precise))
    mixed = low_back(jnp.dot(low(jax.nn.gelu(hidden)), w_down, precision=precise))
    return present[:, None] * (middle + mixed)

def reference(frames, lengths, w_qkv, w_out, w_up, w_down, gain_one, gain_two, cotangent):
    labels, places = frame_ids(lengths)
    present = (labels < UTT).astype(jnp.float32)
    weights = (w_qkv.astype(jnp.float32), w_out.astype(jnp.float32), w_up.astype(jnp.float32), w_down.astype(jnp.float32), gain_one.astype(jnp.float32), gain_two.astype(jnp.float32))

    def forward(inputs, params):

        def one_group(group_parts):
            return group_forward(params, group_parts[0], group_parts[1], group_parts[2], places)
        return lax.map(one_group, (inputs, labels, present))
    result, pull = jax.vjp(forward, frames.astype(jnp.float32), weights)
    grad_inputs, grads = pull(cotangent.astype(jnp.float32))
    return (result.astype(jnp.bfloat16), grad_inputs, grads[0], grads[1], grads[2], grads[3], grads[4], grads[5])
```

```python
import functools

import jax
import jax.numpy as jnp
from jax import lax
from jax.experimental import pallas as pl
from jax.experimental.pallas import tpu as pltpu
from jax.sharding import PartitionSpec as P

HEADS = 16
HEAD_DIM = 64
eps = 1e-05
masked = -1e30
log2e = 1.4426950408889634
vmem_bytes = 56 * 2**20
GAIN_ROWS = 16
low = jnp.bfloat16
full = jnp.float32


def lane_labels(ends_ref, utterances, start, rows, count):
    place = start + lax.broadcasted_iota(jnp.int32, (rows, count), 1)
    label = jnp.zeros((rows, count), jnp.int32)
    for u in range(utterances):
        label = label + (place >= ends_ref[u]).astype(jnp.int32)
    return label


def stage_scores(ends_ref, rows_ref, source, utterances, query_s, key_s):
    frames = rows_ref.shape[2]
    label = lane_labels(ends_ref, utterances, source * frames, HEAD_DIM, frames)
    row = lax.broadcasted_iota(jnp.int32, (HEAD_DIM, frames), 0)
    own = jnp.where(row == label, 1.0, 0.0).astype(low)
    barred = jnp.where((row != label) & (row <= utterances), masked, 0.0).astype(low)
    span = pl.ds(source * frames, frames)
    query_s[0:HEAD_DIM, span] = rows_ref[source, 0:HEAD_DIM, :]
    query_s[HEAD_DIM:, span] = own
    key_s[span, :] = jnp.concatenate([rows_ref[source, HEAD_DIM : 2 * HEAD_DIM, :], barred], axis=0).T


def causal(scores, key_start, query_start):
    key_place = key_start + lax.broadcasted_iota(jnp.int32, scores.shape, 0)
    query_place = query_start + lax.broadcasted_iota(jnp.int32, scores.shape, 1)
    return jnp.where(key_place <= query_place, scores, masked)


def forward_kernel(ends_ref, rows_ref, out_ref, mass_ref, query_s, key_s, value_s, *, block, copies):
    sources, _, frames = rows_ref.shape
    utterances = ends_ref.shape[0] - 1
    share = ends_ref[utterances]
    power = HEAD_DIM**-0.5 * log2e
    total = sources * frames
    for source in range(sources):
        stage_scores(ends_ref, rows_ref, source, utterances, query_s, key_s)
        span = pl.ds(source * frames, frames)
        value_s[0:HEAD_DIM, span] = rows_ref[source, 2 * HEAD_DIM :, :]
        row = lax.broadcasted_iota(jnp.int32, (value_s.shape[0] - HEAD_DIM, frames), 0)
        value_s[HEAD_DIM:, span] = jnp.where(row == 0, 1.0, 0.0).astype(low)
    if copies > 1:
        out_ref[...] = jnp.zeros_like(out_ref)
        mass_ref[...] = jnp.zeros_like(mass_ref)

    def query_block(turn, _):
        i = turn * copies + share if copies > 1 else turn
        span = pl.ds(pl.multiple_of(i * block, block), block)
        query = query_s[:, span]

        def step(j, current, diagonal):
            peak, sums = current
            keys = pl.ds(pl.multiple_of(j * block, block), block)
            scores = jnp.dot(key_s[keys, :], query, preferred_element_type=full)
            if diagonal:
                scores = causal(scores, 0, 0)
            new_peak = jnp.maximum(peak, jnp.max(scores, axis=0, keepdims=True) * power)
            weights = jnp.exp2(scores * power - new_peak)
            sums = sums * jnp.exp2(peak - new_peak) + jnp.dot(
                value_s[:, keys], weights.astype(low), preferred_element_type=full
            )
            return new_peak, sums

        start = (jnp.full((1, block), masked, full), jnp.zeros((value_s.shape[0], block), full))
        current = lax.fori_loop(0, i, lambda j, now: step(j, now, False), start)
        peak, sums = step(i, current, True)
        mass = sums[HEAD_DIM : HEAD_DIM + 1]
        label = lane_labels(ends_ref, utterances, i * block, 1, block)
        out = (sums[0:HEAD_DIM] * jnp.where(label < utterances, 1.0 / mass, 0.0)).astype(low)
        mass_ref[:, span] = peak + jnp.log2(mass)
        for part in range(block // frames):
            out_ref[i * (block // frames) + part] = out[:, part * frames : (part + 1) * frames]
        return 0

    lax.fori_loop(0, total // block // copies, query_block, 0)


def block_of(total, copies):
    return min(1024, total // copies)


def attn_fwd(ends, rows, copies):
    sources, _, frames = rows.shape
    total = sources * frames
    return pl.pallas_call(
        functools.partial(forward_kernel, block=block_of(total, copies), copies=copies),
        out_shape=(
            jax.ShapeDtypeStruct((sources, HEAD_DIM, frames), low),
            jax.ShapeDtypeStruct((1, total), full),
        ),
        in_specs=[pl.BlockSpec(memory_space=pltpu.SMEM), pl.BlockSpec(memory_space=pltpu.VMEM)],
        out_specs=[pl.BlockSpec(memory_space=pltpu.VMEM)] * 2,
        scratch_shapes=[
            pltpu.VMEM((2 * HEAD_DIM, total), low),
            pltpu.VMEM((total, 2 * HEAD_DIM), low),
            pltpu.VMEM((HEAD_DIM + 16, total), low),
        ],
        compiler_params=pltpu.CompilerParams(vmem_limit_bytes=vmem_bytes),
        cost_estimate=pl.CostEstimate(
            flops=4 * total * total * HEAD_DIM, bytes_accessed=4 * rows.size, transcendentals=total * total // 2
        ),
        name="attention_forward",
    )(ends, rows)


def backward_kernel(
    ends_ref, rows_ref, grad_ref, out_ref, mass_ref, result_ref,
    query_s, key_s, keyt_s, value_s, grad_s, grad_query_s, *, block, copies
):
    sources, _, frames = rows_ref.shape
    utterances = ends_ref.shape[0] - 1
    share = ends_ref[utterances]
    scale = HEAD_DIM**-0.5
    power = scale * log2e
    total = sources * frames
    blocks = total // block
    row = lax.broadcasted_iota(jnp.int32, (HEAD_DIM, frames), 0)
    for source in range(sources):
        span = pl.ds(source * frames, frames)
        stage_scores(ends_ref, rows_ref, source, utterances, query_s, key_s)
        keyt_s[:, span] = rows_ref[source, HEAD_DIM : 2 * HEAD_DIM, :]
        grad = grad_ref[source]
        delta = jnp.sum(grad.astype(full) * out_ref[source].astype(full), axis=0, keepdims=True)
        first = delta.astype(low).astype(full)
        second = (delta - first).astype(low).astype(full)
        third = delta - first - second
        more = jnp.where(row == 0, -first, jnp.where(row == 1, -second, jnp.where(row == 2, -third, 0.0)))
        grad_s[0:HEAD_DIM, span] = grad
        grad_s[HEAD_DIM:, span] = more.astype(low)
        ones = jnp.where(row < 3, 1.0, 0.0).astype(low)
        value_s[span, :] = jnp.concatenate([rows_ref[source, 2 * HEAD_DIM :, :], ones], axis=0).T
    grad_query_s[...] = jnp.zeros_like(grad_query_s)
    across = (((1,), (1,)), ((), ()))

    def key_block(j, _):
        keys = pl.ds(pl.multiple_of(j * block, block), block)

        def step(i, current, diagonal):
            grad_key, grad_value = current
            span = pl.ds(pl.multiple_of(i * block, block), block)
            scores = jnp.dot(key_s[keys, :], query_s[:, span], preferred_element_type=full)
            if diagonal:
                scores = causal(scores, j * block, i * block)
            probs = jnp.exp2(scores * power - mass_ref[:, span])
            shifted = jnp.dot(value_s[keys, :], grad_s[:, span], preferred_element_type=full)
            grad_scores = (probs * shifted).astype(low)
            grad_query_s[:, span] += jnp.dot(keyt_s[:, keys], grad_scores, preferred_element_type=full)
            grad_value = grad_value + lax.dot_general(
                grad_s[0:HEAD_DIM, span], probs.astype(low), across, preferred_element_type=full
            )
            grad_key = grad_key + lax.dot_general(
                query_s[0:HEAD_DIM, span], grad_scores, across, preferred_element_type=full
            )
            return grad_key, grad_value

        zero = jnp.zeros((HEAD_DIM, block), full)
        if copies > 1:
            first = (j - share + copies - 1) // copies
            current = lax.fori_loop(
                first, blocks // copies, lambda turn, now: step(turn * copies + share, now, True), (zero, zero)
            )
        else:
            current = step(j, (zero, zero), True)
            current = lax.fori_loop(j + 1, blocks, lambda i, now: step(i, now, False), current)
        grad_key = (current[0] * scale).astype(low)
        grad_value = current[1].astype(low)
        for part in range(block // frames):
            lanes = slice(part * frames, (part + 1) * frames)
            place = j * (block // frames) + part
            result_ref[place, HEAD_DIM : 2 * HEAD_DIM, :] = grad_key[:, lanes]
            result_ref[place, 2 * HEAD_DIM :, :] = grad_value[:, lanes]
        return 0

    lax.fori_loop(0, blocks, key_block, 0)
    for source in range(sources):
        lanes = slice(source * frames, (source + 1) * frames)
        result_ref[source, 0:HEAD_DIM, :] = (grad_query_s[:, lanes] * scale).astype(low)


def attn_bwd(ends, rows, grads, outs, mass, copies):
    sources, _, frames = rows.shape
    total = sources * frames
    return pl.pallas_call(
        functools.partial(backward_kernel, block=block_of(total, copies), copies=copies),
        out_shape=jax.ShapeDtypeStruct(rows.shape, low),
        in_specs=[pl.BlockSpec(memory_space=pltpu.SMEM)] + [pl.BlockSpec(memory_space=pltpu.VMEM)] * 4,
        out_specs=pl.BlockSpec(memory_space=pltpu.VMEM),
        scratch_shapes=[
            pltpu.VMEM((2 * HEAD_DIM, total), low),
            pltpu.VMEM((total, 2 * HEAD_DIM), low),
            pltpu.VMEM((HEAD_DIM, total), low),
            pltpu.VMEM((total, 2 * HEAD_DIM), low),
            pltpu.VMEM((2 * HEAD_DIM, total), low),
            pltpu.VMEM((HEAD_DIM, total), full),
        ],
        compiler_params=pltpu.CompilerParams(vmem_limit_bytes=vmem_bytes),
        cost_estimate=pl.CostEstimate(
            flops=10 * total * total * HEAD_DIM, bytes_accessed=8 * rows.size, transcendentals=total * total // 2
        ),
        name="attention_backward",
    )(ends, rows, grads, outs, mass)


def norm_parts(inputs):
    centred = inputs - jnp.mean(inputs, axis=-1, keepdims=True)
    spread = jnp.mean(centred * centred, axis=-1, keepdims=True)
    inverse = lax.rsqrt(spread + eps)
    return centred * inverse, inverse


def norm_back(grad, unit, inverse, gain):
    scaled = grad * gain
    along = jnp.mean(scaled, axis=-1, keepdims=True)
    across = jnp.mean(scaled * unit, axis=-1, keepdims=True)
    return inverse * (scaled - along - unit * across)


def other_core(array):
    count = lax.axis_size("items")
    return lax.ppermute(array, "items", [(i, i ^ 1) for i in range(count)])


def to_heads(array):
    size = lax.axis_size("seq")
    copies = size // HEADS
    if copies > 1:
        array = jnp.repeat(array, copies, axis=0)
    return lax.all_to_all(array, "seq", 0, 0, tiled=True)


def to_frames(array):
    size = lax.axis_size("seq")
    copies = size // HEADS
    moved = lax.all_to_all(array, "seq", 0, 0, tiled=True)
    if copies > 1:
        moved = jnp.sum(moved.reshape((HEADS, copies) + moved.shape[1:]).astype(full), axis=1).astype(low)
    return moved


def half_columns(array, which):
    width = array.shape[-1] // 2
    return lax.dynamic_slice_in_dim(array, which * width, width, axis=-1)


def pick(array, index, axis):
    return lax.dynamic_index_in_dim(array, index, axis, keepdims=False)


def flipped(array, bit):
    size = lax.axis_size("seq")
    return lax.ppermute(array, "seq", [(i, i ^ bit) for i in range(size)])


def line_sum(parts):
    size = lax.axis_size("seq")
    lines = size // 4
    mine = lax.axis_index("seq") // 4
    up = down = None
    for step in range(1, lines):
        up_send = pick(parts, jnp.minimum(mine + lines - step, lines - 1), 0)
        down_send = pick(parts, jnp.maximum(mine - (lines - step), 0), 0)
        if up is not None:
            up_send = (up_send.astype(full) + up.astype(full)).astype(low)
            down_send = (down_send.astype(full) + down.astype(full)).astype(low)
        up = lax.ppermute(up_send, "seq", [(i, i + 4) for i in range(4 * step)])
        down = lax.ppermute(down_send, "seq", [(i, i - 4) for i in range(size - 4 * step, size)])
    total = pick(parts, mine, 0).astype(full)
    return total + up.astype(full) + down.astype(full)


def scatter_sum(make, first):
    me = lax.axis_index("seq")
    bits = (me % 2, (me // 2) % 2)
    second = 1 - first
    away = make(first, 1 - bits[first])
    arrived = flipped(away, 1 << first)
    kept = make(first, bits[first])
    mine, theirs = bits[second], 1 - bits[second]
    send = (pick(kept, theirs, 1).astype(full) + pick(arrived, theirs, 1).astype(full)).astype(low)
    came = flipped(send, 1 << second)
    total = (
        pick(kept, mine, 1).astype(full) + pick(arrived, mine, 1).astype(full) + came.astype(full)
    ).astype(low)
    return line_sum(total)


def term_maker(left, right, extra=None):
    lines = lax.axis_size("seq") // 4
    count, wide = left.shape
    rows = wide // (4 * lines)
    grid = left.reshape(count, lines, 2, 2, rows)

    def make(bit, value):
        chosen = pick(grid, value, 3 - bit)
        terms = jnp.einsum("tzbr,tn->zbrn", chosen, right, preferred_element_type=full).astype(low)
        if extra is not None:
            terms = jnp.concatenate([terms, pick(extra, value, 2 - bit)], axis=2)
        return terms

    return make


def gain_block(gain, columns):
    lines = lax.axis_size("seq") // 4
    rows = gain.shape[0] // (4 * lines)
    block = gain.astype(low).reshape(lines, 2, 2, 1, rows)
    return jnp.pad(block, ((0, 0), (0, 0), (0, 0), (0, GAIN_ROWS - 1), (0, columns - rows)))


def over_items(piece):
    count = lax.axis_size("items")
    pieces = lax.all_gather(piece.astype(low), "items", axis=0)
    pieces = pieces.reshape((count // 2, 2) + piece.shape)
    if count > 2:
        return jnp.sum(pieces.astype(full), axis=0)
    return pieces[0].astype(full)


def side_by_side(halves):
    return jnp.concatenate([halves[0], halves[1]], axis=-1)


def on_device(frames, lengths, w_qkv, w_out, w_up, w_down, gain_one, gain_two, cotangent):
    row_count, feature_count = frames.shape[1:]
    me = lax.axis_index("seq")
    core = lax.axis_index("items") % 2
    ends = jnp.cumsum(lengths[0]).astype(jnp.int32)
    places = me * row_count + jnp.arange(row_count, dtype=jnp.int32)
    present = (places < ends[-1]).astype(full)[:, None]

    inputs = frames[0].astype(full)
    unit_one, inverse_one = norm_parts(inputs)
    low_one = (unit_one * gain_one).astype(low)
    packed = jnp.dot(low_one, w_qkv, preferred_element_type=full).astype(low)
    by_head = packed.T.reshape(3, HEADS, HEAD_DIM, row_count).transpose(1, 0, 2, 3).reshape(HEADS, 3 * HEAD_DIM, row_count)
    head_rows = to_heads(by_head)
    copies = lax.axis_size("seq") // HEADS
    control = jnp.concatenate([ends, (me % copies)[None]])
    head_out, log_mass = attn_fwd(control, head_rows, copies)
    attended = to_frames(head_out).reshape(feature_count, row_count).T

    middle = inputs + jnp.dot(attended, w_out, preferred_element_type=full)
    unit_two, inverse_two = norm_parts(middle)
    low_two = (unit_two * gain_two).astype(low)
    hidden = jnp.dot(low_two, w_up, preferred_element_type=full)
    activated, pull_gelu = jax.vjp(jax.nn.gelu, hidden)
    act_low = activated.astype(low)
    mixed = jnp.dot(act_low, w_down, preferred_element_type=full)
    result = (present * (middle + mixed)).astype(low)
    grad_mixed = cotangent[0].astype(full) * present
    grad_mixed_low = grad_mixed.astype(low)
    grad_act = jnp.einsum("td,fd->tf", grad_mixed_low, w_down, preferred_element_type=full)
    grad_hidden = pull_gelu(grad_act)[0].astype(low)
    grad_normed_two = jnp.einsum("tf,df->td", grad_hidden, w_up, preferred_element_type=full)
    grad_gain_two = jnp.sum(grad_normed_two * unit_two, axis=0)
    grad_middle = grad_mixed + norm_back(grad_normed_two, unit_two, inverse_two, gain_two)
    grad_branch = grad_middle.astype(low)
    grad_attended = jnp.einsum("te,de->dt", grad_branch, w_out, preferred_element_type=full).astype(low)
    grad_attended = grad_attended * present[:, 0].astype(low)[None]
    grad_heads = to_heads(grad_attended.reshape(HEADS, HEAD_DIM, row_count))

    def both(left, right):
        lefts = jnp.concatenate([left, other_core(left)], axis=0)
        rights = jnp.concatenate(
            [half_columns(right, core), other_core(half_columns(right, 1 - core))], axis=0
        )
        return lefts, rights

    sum_down = scatter_sum(term_maker(*both(act_low, grad_mixed_low)), 1)
    sum_up = scatter_sum(term_maker(*both(low_two, grad_hidden)), 0)
    extra = gain_block(grad_gain_two, feature_count // 2)
    sum_out = scatter_sum(term_maker(*both(attended, grad_branch), extra), 0)

    grad_rows = attn_bwd(control, head_rows, grad_heads, head_out, log_mass, copies)
    grad_packed = to_frames(grad_rows)
    grad_packed = (
        grad_packed.reshape(HEADS, 3, HEAD_DIM, row_count).transpose(3, 1, 0, 2).reshape(row_count, 3 * feature_count)
    )
    lefts, rights = both(low_one, grad_packed)
    split = rights.shape[1] // 2
    grad_normed_one = jnp.einsum("te,de->td", grad_packed, w_qkv, preferred_element_type=full)
    grad_gain_one = jnp.sum(grad_normed_one * unit_one, axis=0)
    sum_qkv_a = scatter_sum(term_maker(lefts, rights[:, :split]), 0)
    extra = gain_block(grad_gain_one, rights.shape[1] - split)
    sum_qkv_b = scatter_sum(term_maker(lefts, rights[:, split:], extra), 1)
    grad_inputs = grad_middle + norm_back(grad_normed_one, unit_one, inverse_one, gain_one)

    rows_out = sum_up.shape[0]
    out_halves = over_items(sum_out)
    up = side_by_side(over_items(sum_up))
    down = side_by_side(over_items(sum_down))
    out = side_by_side(out_halves[:, :rows_out])
    b_halves = over_items(sum_qkv_b)
    a_halves = over_items(sum_qkv_a)
    qkv = side_by_side(jnp.concatenate([a_halves, b_halves[:, :rows_out]], axis=-1))
    sum_gain_two = jnp.sum(out_halves[:, rows_out, :rows_out], axis=0)
    sum_gain_one = jnp.sum(b_halves[:, rows_out, :rows_out], axis=0)
    return (result[None], grad_inputs[None], qkv, out, up, down, sum_gain_one, sum_gain_two)


def solution(mesh):
    return jax.shard_map(
        on_device,
        mesh=mesh,
        in_specs=(
            P("items", "seq", None),
            P("items", None),
            P(),
            P(),
            P(),
            P(),
            P(),
            P(),
            P("items", "seq", None),
        ),
        out_specs=(
            P("items", "seq", None),
            P("items", "seq", None),
            P("seq", None),
            P("seq", None),
            P("seq", None),
            P("seq", None),
            P("seq"),
            P("seq"),
        ),
        check_vma=False,
    )
```

```python
import functools

import jax
import jax.numpy as jnp
from jax import lax
from jax.experimental import pallas as pl
from jax.experimental.pallas import tpu as pltpu
from jax.sharding import PartitionSpec as P

HEADS = 16
HEAD_DIM = 64
eps = 1e-05
masked = -1e30
log2e = 1.4426950408889634
vmem_bytes = 56 * 2**20
low = jnp.bfloat16
full = jnp.float32


def lane_labels(ends_ref, utterances, start, rows, count):
    place = start + lax.broadcasted_iota(jnp.int32, (rows, count), 1)
    label = jnp.zeros((rows, count), jnp.int32)
    for u in range(utterances):
        label = label + (place >= ends_ref[u]).astype(jnp.int32)
    return label


def stage_scores(ends_ref, rows_ref, source, utterances, query_s, key_s):
    frames = rows_ref.shape[2]
    label = lane_labels(ends_ref, utterances, source * frames, HEAD_DIM, frames)
    row = lax.broadcasted_iota(jnp.int32, (HEAD_DIM, frames), 0)
    own = jnp.where(row == label, 1.0, 0.0).astype(low)
    barred = jnp.where((row != label) & (row <= utterances), masked, 0.0).astype(low)
    span = pl.ds(source * frames, frames)
    query_s[0:HEAD_DIM, span] = rows_ref[source, 0:HEAD_DIM, :]
    query_s[HEAD_DIM:, span] = own
    key_s[span, :] = jnp.concatenate([rows_ref[source, HEAD_DIM : 2 * HEAD_DIM, :], barred], axis=0).T


def causal(scores, key_start, query_start):
    key_place = key_start + lax.broadcasted_iota(jnp.int32, scores.shape, 0)
    query_place = query_start + lax.broadcasted_iota(jnp.int32, scores.shape, 1)
    return jnp.where(key_place <= query_place, scores, masked)


def forward_kernel(ends_ref, rows_ref, out_ref, mass_ref, query_s, key_s, value_s, *, block, copies):
    sources, _, frames = rows_ref.shape
    utterances = ends_ref.shape[0] - 1
    share = ends_ref[utterances]
    power = HEAD_DIM**-0.5 * log2e
    total = sources * frames
    for source in range(sources):
        stage_scores(ends_ref, rows_ref, source, utterances, query_s, key_s)
        span = pl.ds(source * frames, frames)
        value_s[0:HEAD_DIM, span] = rows_ref[source, 2 * HEAD_DIM :, :]
        row = lax.broadcasted_iota(jnp.int32, (value_s.shape[0] - HEAD_DIM, frames), 0)
        value_s[HEAD_DIM:, span] = jnp.where(row == 0, 1.0, 0.0).astype(low)
    if copies > 1:
        out_ref[...] = jnp.zeros_like(out_ref)
        mass_ref[...] = jnp.zeros_like(mass_ref)

    def query_block(turn, _):
        i = turn * copies + share if copies > 1 else turn
        span = pl.ds(pl.multiple_of(i * block, block), block)
        query = query_s[:, span]

        def step(j, current, diagonal):
            peak, sums = current
            keys = pl.ds(pl.multiple_of(j * block, block), block)
            scores = jnp.dot(key_s[keys, :], query, preferred_element_type=full)
            if diagonal:
                scores = causal(scores, 0, 0)
            new_peak = jnp.maximum(peak, jnp.max(scores, axis=0, keepdims=True) * power)
            weights = jnp.exp2(scores * power - new_peak)
            sums = sums * jnp.exp2(peak - new_peak) + jnp.dot(
                value_s[:, keys], weights.astype(low), preferred_element_type=full
            )
            return new_peak, sums

        start = (jnp.full((1, block), masked, full), jnp.zeros((value_s.shape[0], block), full))
        current = lax.fori_loop(0, i, lambda j, now: step(j, now, False), start)
        peak, sums = step(i, current, True)
        mass = sums[HEAD_DIM : HEAD_DIM + 1]
        label = lane_labels(ends_ref, utterances, i * block, 1, block)
        out = (sums[0:HEAD_DIM] * jnp.where(label < utterances, 1.0 / mass, 0.0)).astype(low)
        mass_ref[:, span] = peak + jnp.log2(mass)
        for part in range(block // frames):
            out_ref[i * (block // frames) + part] = out[:, part * frames : (part + 1) * frames]
        return 0

    lax.fori_loop(0, total // block // copies, query_block, 0)


def block_of(total, copies):
    return min(1024, total // copies)


def attn_fwd(ends, rows, copies):
    sources, _, frames = rows.shape
    total = sources * frames
    return pl.pallas_call(
        functools.partial(forward_kernel, block=block_of(total, copies), copies=copies),
        out_shape=(
            jax.ShapeDtypeStruct((sources, HEAD_DIM, frames), low),
            jax.ShapeDtypeStruct((1, total), full),
        ),
        in_specs=[pl.BlockSpec(memory_space=pltpu.SMEM), pl.BlockSpec(memory_space=pltpu.VMEM)],
        out_specs=[pl.BlockSpec(memory_space=pltpu.VMEM)] * 2,
        scratch_shapes=[
            pltpu.VMEM((2 * HEAD_DIM, total), low),
            pltpu.VMEM((total, 2 * HEAD_DIM), low),
            pltpu.VMEM((HEAD_DIM + 16, total), low),
        ],
        compiler_params=pltpu.CompilerParams(vmem_limit_bytes=vmem_bytes),
        cost_estimate=pl.CostEstimate(
            flops=20 * total * total * HEAD_DIM, bytes_accessed=4 * rows.size, transcendentals=total * total // 2
        ),
        name="attention_forward",
    )(ends, rows)


def backward_kernel(
    ends_ref, rows_ref, grad_ref, out_ref, mass_ref, result_ref,
    query_s, key_s, keyt_s, value_s, grad_s, grad_query_s, *, block, copies
):
    sources, _, frames = rows_ref.shape
    utterances = ends_ref.shape[0] - 1
    share = ends_ref[utterances]
    scale = HEAD_DIM**-0.5
    power = scale * log2e
    total = sources * frames
    blocks = total // block
    row = lax.broadcasted_iota(jnp.int32, (HEAD_DIM, frames), 0)
    for source in range(sources):
        span = pl.ds(source * frames, frames)
        stage_scores(ends_ref, rows_ref, source, utterances, query_s, key_s)
        keyt_s[:, span] = rows_ref[source, HEAD_DIM : 2 * HEAD_DIM, :]
        grad = grad_ref[source]
        delta = jnp.sum(grad.astype(full) * out_ref[source].astype(full), axis=0, keepdims=True)
        first = delta.astype(low).astype(full)
        second = (delta - first).astype(low).astype(full)
        third = delta - first - second
        more = jnp.where(row == 0, -first, jnp.where(row == 1, -second, jnp.where(row == 2, -third, 0.0)))
        grad_s[0:HEAD_DIM, span] = grad
        grad_s[HEAD_DIM:, span] = more.astype(low)
        ones = jnp.where(row < 3, 1.0, 0.0).astype(low)
        value_s[span, :] = jnp.concatenate([rows_ref[source, 2 * HEAD_DIM :, :], ones], axis=0).T
    grad_query_s[...] = jnp.zeros_like(grad_query_s)
    across = (((1,), (1,)), ((), ()))

    def key_block(j, _):
        keys = pl.ds(pl.multiple_of(j * block, block), block)

        def step(i, current, diagonal):
            grad_key, grad_value = current
            span = pl.ds(pl.multiple_of(i * block, block), block)
            scores = jnp.dot(key_s[keys, :], query_s[:, span], preferred_element_type=full)
            if diagonal:
                scores = causal(scores, j * block, i * block)
            probs = jnp.exp2(scores * power - mass_ref[:, span])
            shifted = jnp.dot(value_s[keys, :], grad_s[:, span], preferred_element_type=full)
            grad_scores = (probs * shifted).astype(low)
            grad_query_s[:, span] += jnp.dot(keyt_s[:, keys], grad_scores, preferred_element_type=full)
            grad_value = grad_value + lax.dot_general(
                grad_s[0:HEAD_DIM, span], probs.astype(low), across, preferred_element_type=full
            )
            grad_key = grad_key + lax.dot_general(
                query_s[0:HEAD_DIM, span], grad_scores, across, preferred_element_type=full
            )
            return grad_key, grad_value

        zero = jnp.zeros((HEAD_DIM, block), full)
        if copies > 1:
            first = (j - share + copies - 1) // copies
            current = lax.fori_loop(
                first, blocks // copies, lambda turn, now: step(turn * copies + share, now, True), (zero, zero)
            )
        else:
            current = step(j, (zero, zero), True)
            current = lax.fori_loop(j + 1, blocks, lambda i, now: step(i, now, False), current)
        grad_key = (current[0] * scale).astype(low)
        grad_value = current[1].astype(low)
        for part in range(block // frames):
            lanes = slice(part * frames, (part + 1) * frames)
            place = j * (block // frames) + part
            result_ref[place, HEAD_DIM : 2 * HEAD_DIM, :] = grad_key[:, lanes]
            result_ref[place, 2 * HEAD_DIM :, :] = grad_value[:, lanes]
        return 0

    lax.fori_loop(0, blocks, key_block, 0)
    for source in range(sources):
        lanes = slice(source * frames, (source + 1) * frames)
        result_ref[source, 0:HEAD_DIM, :] = (grad_query_s[:, lanes] * scale).astype(low)


def attn_bwd(ends, rows, grads, outs, mass, copies):
    sources, _, frames = rows.shape
    total = sources * frames
    return pl.pallas_call(
        functools.partial(backward_kernel, block=block_of(total, copies), copies=copies),
        out_shape=jax.ShapeDtypeStruct(rows.shape, low),
        in_specs=[pl.BlockSpec(memory_space=pltpu.SMEM)] + [pl.BlockSpec(memory_space=pltpu.VMEM)] * 4,
        out_specs=pl.BlockSpec(memory_space=pltpu.VMEM),
        scratch_shapes=[
            pltpu.VMEM((2 * HEAD_DIM, total), low),
            pltpu.VMEM((total, 2 * HEAD_DIM), low),
            pltpu.VMEM((HEAD_DIM, total), low),
            pltpu.VMEM((total, 2 * HEAD_DIM), low),
            pltpu.VMEM((2 * HEAD_DIM, total), low),
            pltpu.VMEM((HEAD_DIM, total), full),
        ],
        compiler_params=pltpu.CompilerParams(vmem_limit_bytes=vmem_bytes),
        cost_estimate=pl.CostEstimate(
            flops=35 * total * total * HEAD_DIM, bytes_accessed=8 * rows.size, transcendentals=total * total // 2
        ),
        name="attention_backward",
    )(ends, rows, grads, outs, mass)


def norm_parts(inputs):
    centred = inputs - jnp.mean(inputs, axis=-1, keepdims=True)
    spread = jnp.mean(centred * centred, axis=-1, keepdims=True)
    inverse = lax.rsqrt(spread + eps)
    return centred * inverse, inverse


def norm_back(grad, unit, inverse, gain):
    scaled = grad * gain
    along = jnp.mean(scaled, axis=-1, keepdims=True)
    across = jnp.mean(scaled * unit, axis=-1, keepdims=True)
    return inverse * (scaled - along - unit * across)


def project_kernel(frames_ref, gain_ref, query_ref, key_ref, value_ref, rows_ref, low_ref):
    @pl.when(pl.program_id(0) == 0)
    def _():
        unit, _ = norm_parts(frames_ref[...].astype(full))
        low_ref[...] = (unit * gain_ref[...]).astype(low)

    heads = rows_ref.shape[0]
    for part, weight_ref in enumerate((query_ref, key_ref, value_ref)):
        packed = jnp.dot(low_ref[...], weight_ref[...], preferred_element_type=full).astype(low).T
        for head in range(heads):
            rows_ref[head, part * HEAD_DIM : (part + 1) * HEAD_DIM, :] = packed[
                head * HEAD_DIM : (head + 1) * HEAD_DIM
            ]


def thirds(features, wide):
    count = features // wide
    return [pl.BlockSpec((features, wide), lambda i, part=part: (0, part * count + i)) for part in range(3)]


def project(frames, gain, w_qkv):
    rows, features = frames.shape
    wide = 4 * HEAD_DIM
    return pl.pallas_call(
        project_kernel,
        grid=(features // wide,),
        out_shape=(
            jax.ShapeDtypeStruct((HEADS, 3 * HEAD_DIM, rows), low),
            jax.ShapeDtypeStruct((rows, features), low),
        ),
        in_specs=[
            pl.BlockSpec((rows, features), lambda i: (0, 0)),
            pl.BlockSpec((1, features), lambda i: (0, 0)),
        ]
        + thirds(features, wide),
        out_specs=[
            pl.BlockSpec((4, 3 * HEAD_DIM, rows), lambda i: (i, 0, 0)),
            pl.BlockSpec((rows, features), lambda i: (0, 0)),
        ],
        compiler_params=pltpu.CompilerParams(vmem_limit_bytes=vmem_bytes),
        cost_estimate=pl.CostEstimate(
            flops=6 * rows * features * features, bytes_accessed=8 * features * features, transcendentals=0
        ),
        name="norm_and_project",
    )(frames, gain[None], w_qkv, w_qkv, w_qkv)


def middle_kernel(
    control_ref, frames_ref, att_ref, cot_ref, gain_ref, out_weight_ref, up_ref, down_ref,
    result_ref, grad_middle_ref, branch_ref, branch_away_ref, grad_att_ref, low_two_ref, act_ref,
    grad_hidden_ref, grad_hidden_away_ref, mixed_ref, mixed_away_ref,
    unit_s, inverse_s, sum_s, back_s, low_two_s, mixed_s,
):
    step = pl.program_id(0)
    steps = pl.num_programs(0)
    core = control_ref[0]
    valid = control_ref[1]
    rows, features = frames_ref.shape
    root = 0.7978845608028654
    cubic = 0.044715
    across = (((1,), (1,)), ((), ()))
    present = (lax.broadcasted_iota(jnp.int32, (rows, 1), 0) < valid).astype(full)

    def by_core(array, own_ref, away_ref):
        halves = (array[:, : features // 2], array[:, features // 2 :])
        for value in range(2):

            @pl.when(core == value)
            def _():
                own_ref[...] = halves[value]
                away_ref[...] = halves[1 - value]

    @pl.when(step == 0)
    def _():
        middle = frames_ref[...].astype(full) + jnp.dot(
            att_ref[...].T, out_weight_ref[...], preferred_element_type=full
        )
        unit, inverse = norm_parts(middle)
        unit_s[...] = unit
        inverse_s[...] = inverse
        low_two_s[...] = (unit * gain_ref[...]).astype(low)
        low_two_ref[...] = low_two_s[...].T
        mixed_s[...] = (cot_ref[...].astype(full) * present).astype(low)
        by_core(mixed_s[...], mixed_ref, mixed_away_ref)
        sum_s[...] = middle
        back_s[...] = jnp.zeros_like(back_s)

    hidden = jnp.dot(low_two_s[...], up_ref[...], preferred_element_type=full)
    grad_act = lax.dot_general(mixed_s[...], down_ref[...], across, preferred_element_type=full)
    square = hidden * hidden
    bent = jnp.tanh(root * hidden * (1.0 + cubic * square))
    half = 0.5 * (1.0 + bent)
    act = (hidden * half).astype(low)
    slope = half + (0.5 * root) * hidden * (1.0 - bent * bent) * (1.0 + (3.0 * cubic) * square)
    grad_hidden = (slope * grad_act).astype(low)
    act_ref[...] = act.T

    @pl.when(step < steps // 2)
    def _():
        grad_hidden_ref[...] = grad_hidden

    @pl.when(step >= steps // 2)
    def _():
        grad_hidden_away_ref[...] = grad_hidden

    sum_s[...] += jnp.dot(act, down_ref[...], preferred_element_type=full)
    back_s[...] += lax.dot_general(grad_hidden, up_ref[...], across, preferred_element_type=full)

    @pl.when(step == steps - 1)
    def _():
        result_ref[...] = (present * sum_s[...]).astype(low)
        grad_middle = mixed_s[...].astype(full) + norm_back(
            back_s[...], unit_s[...], inverse_s[...], gain_ref[...]
        )
        grad_middle_ref[...] = grad_middle
        branch = grad_middle.astype(low)
        by_core(branch, branch_ref, branch_away_ref)
        grad_att = lax.dot_general(out_weight_ref[...], branch, across, preferred_element_type=full)
        lane = (lax.broadcasted_iota(jnp.int32, (1, rows), 1) < valid).astype(full)
        grad_att_ref[...] = (grad_att * lane).astype(low)


def middle_part(core, valid, frames, att, cot, gain, w_out, w_up, w_down):
    rows, features = frames.shape
    hidden = w_up.shape[1]
    wide = 512
    steps = hidden // wide
    here = lambda i, s: (i + s[0] * (steps // 2)) % steps
    whole = lambda *shape: pl.BlockSpec(shape, lambda i, s: (0,) * len(shape))
    square = (rows, features)
    turned = (features, rows)
    halved = (rows, features // 2)
    outs = [
        (square, low, None),
        (square, full, None),
        (halved, low, None),
        (halved, low, None),
        (turned, low, None),
        (turned, low, None),
        ((hidden, rows), low, pl.BlockSpec((wide, rows), lambda i, s: (here(i, s), 0))),
        ((rows, hidden // 2), low, pl.BlockSpec((rows, wide), lambda i, s: (0, jnp.minimum(i, steps // 2 - 1)))),
        ((rows, hidden // 2), low, pl.BlockSpec((rows, wide), lambda i, s: (0, jnp.maximum(i - steps // 2, 0)))),
        (halved, low, None),
        (halved, low, None),
    ]
    return pl.pallas_call(
        middle_kernel,
        grid_spec=pltpu.PrefetchScalarGridSpec(
            num_scalar_prefetch=1,
            grid=(steps,),
            in_specs=[
                whole(*square),
                whole(*turned),
                whole(*square),
                whole(1, features),
                whole(features, features),
                pl.BlockSpec((features, wide), lambda i, s: (0, here(i, s))),
                pl.BlockSpec((wide, features), lambda i, s: (here(i, s), 0)),
            ],
            out_specs=[spec or whole(*shape) for shape, _, spec in outs],
            scratch_shapes=[
                pltpu.VMEM(square, full),
                pltpu.VMEM((rows, 1), full),
                pltpu.VMEM(square, full),
                pltpu.VMEM(square, full),
                pltpu.VMEM(square, low),
                pltpu.VMEM(square, low),
            ],
        ),
        out_shape=[jax.ShapeDtypeStruct(shape, kind) for shape, kind, _ in outs],
        compiler_params=pltpu.CompilerParams(vmem_limit_bytes=vmem_bytes),
        cost_estimate=pl.CostEstimate(
            flops=8 * rows * features * hidden + 4 * rows * features * features,
            bytes_accessed=4 * features * hidden + 2 * features * features,
            transcendentals=rows * hidden,
        ),
        name="middle",
    )(jnp.stack([core, valid]), frames, att, cot, gain[None], w_out, w_up, w_down)


def finish_kernel(frames_ref, middle_ref, gain_ref, rows_ref, query_ref, key_ref, value_ref, result_ref, back_s):
    step = pl.program_id(0)
    heads, _, rows = rows_ref.shape

    @pl.when(step == 0)
    def _():
        back_s[...] = jnp.zeros_like(back_s)

    total = back_s[...]
    for part, weight_ref in enumerate((query_ref, key_ref, value_ref)):
        grads = rows_ref[:, part * HEAD_DIM : (part + 1) * HEAD_DIM, :].reshape(heads * HEAD_DIM, rows)
        total = total + jnp.dot(weight_ref[...], grads, preferred_element_type=full)
    back_s[...] = total

    @pl.when(step == pl.num_programs(0) - 1)
    def _():
        unit, inverse = norm_parts(frames_ref[...].astype(full))
        result_ref[...] = middle_ref[...] + norm_back(back_s[...].T, unit, inverse, gain_ref[...])


def finish(frames, grad_middle, gain, grad_rows, w_qkv):
    rows, features = frames.shape
    wide = 4 * HEAD_DIM
    whole = lambda *shape: pl.BlockSpec(shape, lambda i: (0,) * len(shape))
    return pl.pallas_call(
        finish_kernel,
        grid=(features // wide,),
        out_shape=jax.ShapeDtypeStruct((rows, features), full),
        in_specs=[
            whole(rows, features),
            whole(rows, features),
            whole(1, features),
            pl.BlockSpec((4, 3 * HEAD_DIM, rows), lambda i: (i, 0, 0)),
        ]
        + thirds(features, wide),
        out_specs=whole(rows, features),
        scratch_shapes=[pltpu.VMEM((features, rows), full)],
        compiler_params=pltpu.CompilerParams(vmem_limit_bytes=vmem_bytes),
        cost_estimate=pl.CostEstimate(
            flops=6 * rows * features * features, bytes_accessed=8 * features * features, transcendentals=0
        ),
        name="input_gradient",
    )(frames, grad_middle, gain[None], grad_rows, w_qkv, w_qkv, w_qkv)


def terms_kernel(pick_ref, *refs, spans, needs, added):
    step = pl.program_id(0)
    refs = list(refs)
    take = lambda count: [refs.pop(0) for _ in range(count)]
    lefts = [{kind: take(2) for kind in kinds} for kinds in needs]
    rights = [take(2) for _ in range(3)]
    came = take(3) if added else [None] * 3
    outs = [take(2) if added else take(1) for _ in range(3)]
    for group, parts in enumerate(spans):
        at = 0
        for kind, start, stop in parts:
            own_ref, other_ref = lefts[group][kind]
            right_own_ref, right_other_ref = rights[kind]
            rows, frames = own_ref.shape[-2:]
            for block in range(start, stop) if kind == 2 else (None,):
                if block is None:
                    own, other = own_ref[...], other_ref[...]
                    right_own, right_other = right_own_ref[:, start:stop], right_other_ref[:, start:stop]
                else:
                    own, other = own_ref[:, 0, :, 0, :, block], other_ref[:, 0, :, 0, :, block]
                    right_own, right_other = right_own_ref[...], right_other_ref[...]
                total = jnp.dot(own.reshape(-1, frames), right_own, preferred_element_type=full)
                total = total + jnp.dot(other.reshape(-1, frames), right_other, preferred_element_type=full)
                wide = total.shape[1]
                total = total.reshape(-1, rows, wide)
                if not added:
                    outs[group][0][:, :, at : at + wide] = total.astype(low)
                else:
                    total = (total + came[group][:, :, at : at + wide].astype(full)).astype(low)

                    @pl.when(step == 0)
                    def _():
                        outs[group][0][:, :, at : at + wide] = total

                    @pl.when(step == 1)
                    def _():
                        outs[group][1][:, :, at : at + wide] = total
                at += wide


def terms_by_piece(spans, kept, bits, two, att, act, hidden, branch, mixed, came=None):
    size = lax.axis_size("seq")
    features, frames = two[0].shape
    rows = features // size
    blocks = act[0].shape[0] // features
    wide = mixed[0].shape[1]
    quarter = size // 4
    widths = [sum((stop - start) * (wide if kind == 2 else 1) for kind, start, stop in parts) for parts in spans]
    needs = [sorted({kind for kind, _, _ in parts}) for parts in spans]
    lefts, specs = [], []
    for group in range(3):
        after = (group + 1) % 3
        upper, lower = max(group, after), min(group, after)
        cut = (size >> (upper + 1), 2, 1 << (upper - lower - 1), 2, 1 << lower)

        def place(i, s, group=group, after=after, upper=upper):
            value = s[group] if kept else 1 - s[group]
            beyond = s[after] ^ (1 - i)
            return (value, beyond) if upper == group else (beyond, value)

        for kind in needs[group]:
            extra = (blocks, rows, frames) if kind == 2 else (rows, frames)

            def index(i, s, place=place, extra=extra):
                first, second = place(i, s)
                return (0, first, 0, second, 0) + (0,) * len(extra)

            lefts += [a.reshape(cut + extra) for a in (two, att, act)[kind]]
            specs += [pl.BlockSpec((cut[0], 1, cut[2], 1, cut[4]) + extra, index)] * 2
    rights = (*hidden, *branch, *mixed)
    specs += [pl.BlockSpec(a.shape, lambda i, s: (0, 0)) for a in rights]
    half = lambda width: pl.BlockSpec((None, quarter, rows, width), lambda i, s: (i, 0, 0, 0))
    if came is None:
        outs = [half(width) for width in widths]
        shapes = [jax.ShapeDtypeStruct((2, quarter, rows, width), low) for width in widths]
    else:
        specs += [half(width) for width in widths]
        outs = [pl.BlockSpec((quarter, rows, width), lambda i, s: (0, 0, 0)) for width in widths for _ in range(2)]
        shapes = [jax.ShapeDtypeStruct((quarter, rows, width), low) for width in widths for _ in range(2)]
    return pl.pallas_call(
        functools.partial(terms_kernel, spans=spans, needs=needs, added=came is not None),
        grid_spec=pltpu.PrefetchScalarGridSpec(num_scalar_prefetch=1, grid=(2,), in_specs=specs, out_specs=outs),
        out_shape=shapes,
        compiler_params=pltpu.CompilerParams(vmem_limit_bytes=vmem_bytes),
        cost_estimate=pl.CostEstimate(
            flops=2 * frames * features * sum(widths), bytes_accessed=2 * features * sum(widths), transcendentals=0
        ),
        name="terms_by_piece",
    )(jnp.stack(bits), *lefts, *rights, *(came or ()))


def plane_terms_kernel(core_ref, rows_ref, low_ref, keep_ref, send_ref, sum_s, turn_s):
    step = pl.program_id(0)
    lines, columns, frames = rows_ref.shape

    @pl.when(step == 0)
    def _():
        sum_s[...] = jnp.zeros_like(sum_s)

    total = sum_s[...] + jnp.dot(
        rows_ref[...].reshape(lines * columns, frames), low_ref[...], preferred_element_type=full
    )
    sum_s[...] = total

    @pl.when(step == pl.num_programs(0) - 1)
    def _():
        turn_s[...] = total.T.reshape(turn_s.shape)
        core = core_ref[0]
        keep_ref[...] = turn_s[:, :, core].reshape(keep_ref.shape)
        send_ref[...] = turn_s[:, :, 1 - core].astype(low).reshape(send_ref.shape)


def plane_terms(core, line_rows, low_plane):
    lines, count, columns, frames = line_rows.shape
    features = low_plane.shape[-1]
    rows = features // lines // count // 2
    shape = (lines, count * rows, lines * columns)
    whole = pl.BlockSpec(shape, lambda i: (0, 0, 0))
    return pl.pallas_call(
        plane_terms_kernel,
        grid=(count,),
        in_specs=[
            pl.BlockSpec(memory_space=pltpu.SMEM),
            pl.BlockSpec((lines, None, columns, frames), lambda i: (0, i, 0, 0)),
            pl.BlockSpec((None, frames, features), lambda i: (i, 0, 0)),
        ],
        out_specs=[whole, whole],
        out_shape=(jax.ShapeDtypeStruct(shape, full), jax.ShapeDtypeStruct(shape, low)),
        scratch_shapes=[
            pltpu.VMEM((lines * columns, features), full),
            pltpu.VMEM((lines, count, 2, rows, lines * columns), full),
        ],
        compiler_params=pltpu.CompilerParams(vmem_limit_bytes=vmem_bytes),
        cost_estimate=pl.CostEstimate(
            flops=2 * lines * count * columns * frames * features, bytes_accessed=8 * line_rows.size, transcendentals=0
        ),
        name="plane_terms",
    )(core[None], line_rows, low_plane)


def other_core(array):
    count = lax.axis_size("items")
    return lax.ppermute(array, "items", [(i, i ^ 1) for i in range(count)])


def to_heads(array):
    copies = lax.axis_size("seq") // HEADS
    if copies > 1:
        array = jnp.repeat(array, copies, axis=0)
    return lax.all_to_all(array, "seq", 0, 0, tiled=True)


def by_head(array, axis):
    copies = array.shape[axis] // HEADS
    if copies == 1:
        return array
    shape = array.shape[:axis] + (HEADS, copies) + array.shape[axis + 1 :]
    return jnp.sum(array.reshape(shape).astype(full), axis=axis + 1).astype(low)


def pick(array, index, axis):
    return lax.dynamic_index_in_dim(array, index, axis, keepdims=False)


def flipped(array, bit):
    return lax.ppermute(array, "seq", [(i, i ^ (1 << bit)) for i in range(lax.axis_size("seq"))])


def split_terms(terms, bit, left):
    axis = left.index(bit)
    mine = (lax.axis_index("seq") >> bit) & 1
    terms = [a.reshape((2,) * len(left) + a.shape[-2:]) for a in terms]

    def part(value):
        chosen = [pick(a, value, axis) for a in terms]
        return chosen[0] if len(chosen) == 1 else (chosen[0].astype(full) + chosen[1].astype(full)).astype(low)

    left.remove(bit)
    return part(1 - mine), part(mine)


def together(first, second):
    return (first.astype(full) + second.astype(full)).astype(low)


def over_items(piece):
    count = lax.axis_size("items")
    if count == 2:
        other = other_core(piece)
        first = lax.axis_index("items") == 0
        return jnp.stack([jnp.where(first, piece, other), jnp.where(first, other, piece)]).astype(full)
    pieces = lax.all_gather(piece, "items", axis=0)
    return jnp.sum(pieces.reshape((count // 2, 2) + piece.shape).astype(full), axis=0)


def my_rows(array, rows):
    return lax.dynamic_slice_in_dim(array, lax.axis_index("seq") * rows, rows, axis=0)


def on_device(frames, lengths, w_qkv, w_out, w_up, w_down, gain_one, gain_two, cotangent):
    row_count, features = frames.shape[1:]
    hidden_count = w_up.shape[1]
    size = lax.axis_size("seq")
    depth = size.bit_length() - 1
    me = lax.axis_index("seq")
    core = lax.axis_index("items") % 2
    copies = size // HEADS
    ends = jnp.cumsum(lengths[0]).astype(jnp.int32)
    valid = jnp.clip(ends[-1] - me * row_count, 0, row_count)
    control = jnp.concatenate([ends, (me % copies)[None]])
    rows_out = features // size

    head_parts, low_one = project(frames[0], gain_one, w_qkv)
    head_rows = to_heads(head_parts)
    lines = size // 4
    fours = [list(range(at, at + 4)) for at in range(0, size, 4)]
    columns = [list(range(at, size, 4)) for at in range(4)]
    low_plane = lax.all_gather(low_one, "seq", axis=0, axis_index_groups=fours)
    head_out, log_mass = attn_fwd(control, head_rows, copies)
    head_out, low_plane = lax.optimization_barrier((head_out, low_plane))
    moved = lax.all_to_all(head_out, "seq", 0, 0, tiled=True)
    attended = by_head(moved, 0).reshape(features, row_count)
    att = (attended, other_core(attended))

    result, grad_middle, branch, branch_away, grad_attended, two, act, hidden, hidden_away, mixed, mixed_away = (
        middle_part(core, valid, frames[0], attended, cotangent[0], gain_two, w_out, w_up, w_down)
    )
    grad_heads = to_heads(grad_attended.reshape(HEADS, HEAD_DIM, row_count))

    pairs = (
        (two, other_core(two)),
        att,
        (act, other_core(act)),
        (hidden, other_core(hidden_away)),
        (branch, other_core(branch_away)),
        (mixed, other_core(mixed_away)),
    )
    half = features // 2
    split = hidden_count // 2
    third = (split + half) * 3 // 5
    spans = (
        ((0, 0, third),),
        ((0, third, split), (1, 0, half), (2, 0, 1)),
        ((2, 1, hidden_count // features),),
    )
    bits = [(me >> bit) & 1 for bit in range(3)]
    came = terms_by_piece(spans, False, bits, *pairs)
    came = [flipped(a, bit) for bit, a in enumerate(came)]

    grad_rows = attn_bwd(control, head_rows, grad_heads, head_out, log_mass, copies)
    grad_rows, *came = lax.optimization_barrier((grad_rows, *came))
    across = lambda array, groups: lax.all_to_all(array, "seq", 0, 0, tiled=True, axis_index_groups=groups)
    line_rows = across(grad_rows.reshape(lines, 4, 3 * HEAD_DIM, row_count), columns)

    parts = terms_by_piece(spans, True, bits, *pairs, came=came)
    came = [flipped(parts[2 * g], (g + 1) % 3) for g in range(3)]
    left = [[bit for bit in range(depth - 1, -1, -1) if bit not in (g, (g + 1) % 3)] for g in range(3)]
    line_rows, *came = lax.optimization_barrier((line_rows, *came))
    terms = [(parts[2 * g + 1], came[g]) for g in range(3)]

    def halve(terms, turn):
        sent = []
        for g in range(3):
            bit = (g + turn) % 3 if turn < 3 else turn
            send, keep = split_terms(terms[g], bit, left[g])
            sent.append((keep, flipped(send, bit)))
        return sent

    terms = halve(terms, 2)
    grad_packed = across(line_rows.transpose(1, 0, 2, 3), fours)
    keep, send = plane_terms(core, line_rows, low_plane)
    both = (keep + other_core(send).astype(full)).astype(low)
    both, *came = lax.optimization_barrier((both, *[came for _, came in terms]))
    terms = [(kept, came[g]) for g, (kept, _) in enumerate(terms)]
    for turn in range(3, depth):
        terms = halve(terms, turn)

    pieces = lax.all_to_all(both.reshape(size, rows_out // 2, lines * 3 * HEAD_DIM), "seq", 0, 0, tiled=True)
    grad_packed = by_head(grad_packed.transpose(1, 0, 2, 3).reshape(size, 3 * HEAD_DIM, row_count), 0)
    grad_inputs = finish(frames[0], grad_middle, gain_one, grad_packed, w_qkv)
    grad_inputs, pieces, *came = lax.optimization_barrier((grad_inputs, pieces, *[came for _, came in terms]))
    terms = [(kept, came[g]) for g, (kept, _) in enumerate(terms)]
    sums = jnp.concatenate([together(*pair) for pair in terms], axis=-1)

    pieces = jnp.sum(pieces.reshape((lines, 4) + pieces.shape[1:]).astype(full), axis=0).astype(low)
    pieces = pieces.reshape(4, rows_out // 2, lines, 3, HEAD_DIM).transpose(1, 3, 2, 0, 4)
    pieces = by_head(pieces.reshape(rows_out // 2, 3, size, HEAD_DIM), 2)
    qkv = over_items(pieces.reshape(rows_out // 2, 3 * features)).reshape(rows_out, 3 * features)
    sums = over_items(sums)
    side = lambda start, stop: jnp.concatenate([sums[0, :, start:stop], sums[1, :, start:stop]], axis=-1)
    up = side(0, split)
    out = side(split, split + half)
    start = split + half
    down = jnp.concatenate([side(at, at + half) for at in range(start, start + split, half)], axis=0)
    sum_gain_one = jnp.sum(my_rows(w_qkv, rows_out).astype(full) * qkv, axis=1) / my_rows(gain_one, rows_out)
    sum_gain_two = jnp.sum(my_rows(w_up, rows_out).astype(full) * up, axis=1) / my_rows(gain_two, rows_out)
    return (result[None], grad_inputs[None], qkv, out, up, down, sum_gain_one, sum_gain_two)


def solution(mesh):
    return jax.shard_map(
        on_device,
        mesh=mesh,
        in_specs=(
            P("items", "seq", None),
            P("items", None),
            P(),
            P(),
            P(),
            P(),
            P(),
            P(),
            P("items", "seq", None),
        ),
        out_specs=(
            P("items", "seq", None),
            P("items", "seq", None),
            P("seq", None),
            P("seq", None),
            P("seq", None),
            P("seq", None),
            P("seq"),
            P("seq"),
        ),
        check_vma=False,
    )
```

```python
import functools

import jax
import jax.numpy as jnp
from jax import lax
from jax.experimental import pallas as pl
from jax.experimental.pallas import tpu as pltpu
from jax.sharding import PartitionSpec as P

HEADS = 16
HEAD_DIM = 64
eps = 1e-05
masked = -1e30
log2e = 1.4426950408889634
query_share = 1024
vmem_bytes = 56 * 2**20
low = jnp.bfloat16
full = jnp.float32


def lane_labels(ends_ref, utterances, start, rows, count):
    place = start + lax.broadcasted_iota(jnp.int32, (rows, count), 1)
    label = jnp.zeros((rows, count), jnp.int32)
    for u in range(utterances):
        label = label + (place >= ends_ref[u]).astype(jnp.int32)
    return label


def stage_scores(ends_ref, rows_ref, source, utterances, query_s, key_s):
    frames = rows_ref.shape[2]
    label = lane_labels(ends_ref, utterances, source * frames, HEAD_DIM, frames)
    row = lax.broadcasted_iota(jnp.int32, (HEAD_DIM, frames), 0)
    own = jnp.where(row == label, 1.0, 0.0).astype(low)
    barred = jnp.where((row != label) & (row <= utterances), masked, 0.0).astype(low)
    span = pl.ds(source * frames, frames)
    query_s[0:HEAD_DIM, span] = rows_ref[source, 0:HEAD_DIM, :]
    query_s[HEAD_DIM:, span] = own
    key_s[span, :] = jnp.concatenate([rows_ref[source, HEAD_DIM : 2 * HEAD_DIM, :], barred], axis=0).T


def causal(scores):
    key_place = lax.broadcasted_iota(jnp.int32, scores.shape, 0)
    query_place = lax.broadcasted_iota(jnp.int32, scores.shape, 1)
    return jnp.where(key_place <= query_place, scores, masked)


def forward_kernel(ends_ref, rows_ref, out_ref, mass_ref, query_s, key_s, value_s, *, block, part, copies):
    sources, _, frames = rows_ref.shape
    utterances = ends_ref.shape[0] - 1
    share = ends_ref[utterances]
    power = HEAD_DIM**-0.5 * log2e
    total = sources * frames
    for source in range(sources):
        stage_scores(ends_ref, rows_ref, source, utterances, query_s, key_s)
        span = pl.ds(source * frames, frames)
        value_s[0:HEAD_DIM, span] = rows_ref[source, 2 * HEAD_DIM :, :]
        row = lax.broadcasted_iota(jnp.int32, (value_s.shape[0] - HEAD_DIM, frames), 0)
        value_s[HEAD_DIM:, span] = jnp.where(row == 0, 1.0, 0.0).astype(low)
    if copies > 1:
        out_ref[...] = jnp.zeros_like(out_ref)
        mass_ref[...] = jnp.zeros_like(mass_ref)

    def add_keys(current, query, start, stop, diagonal):
        scores = jnp.dot(key_s[start:stop, :], query, preferred_element_type=full)
        if diagonal:
            scores = causal(scores)
        new_peak = jnp.max(scores, axis=0, keepdims=True) * power
        if current is not None:
            new_peak = jnp.maximum(current[0], new_peak)
        weights = jnp.exp2(scores * power - new_peak)
        sums = jnp.dot(value_s[:, start:stop], weights.astype(low), preferred_element_type=full)
        if current is not None:
            sums = sums + current[1] * jnp.exp2(current[0] - new_peak)
        return new_peak, sums

    def query_block(start):
        query = query_s[:, start : start + block]
        whole = add_keys(None, query, 0, start, False) if start else None
        for at in range(0, block, part):
            lanes = slice(at, at + part)
            current = None if whole is None else (whole[0][:, lanes], whole[1][:, lanes])
            if at:
                current = add_keys(current, query[:, lanes], start, start + at, False)
            peak, sums = add_keys(current, query[:, lanes], start + at, start + at + part, True)
            mass = sums[HEAD_DIM : HEAD_DIM + 1]
            label = lane_labels(ends_ref, utterances, start + at, 1, part)
            out = (sums[0:HEAD_DIM] * jnp.where(label < utterances, 1.0 / mass, 0.0)).astype(low)
            mass_ref[:, start + at : start + at + part] = peak + jnp.log2(mass)
            for piece in range(part // frames):
                out_ref[(start + at) // frames + piece] = out[:, piece * frames : (piece + 1) * frames]

    for start in range(0, total, block):
        shared(share, start // query_share, copies, functools.partial(query_block, start))


def shared(share, turn, copies, work):
    if copies == 1:
        work()
    else:
        pl.when(share == turn % copies)(work)


def attn_fwd(ends, rows, copies):
    sources, _, frames = rows.shape
    total = sources * frames
    return pl.pallas_call(
        functools.partial(forward_kernel, block=query_share, part=query_share, copies=copies),
        out_shape=(
            jax.ShapeDtypeStruct((sources, HEAD_DIM, frames), low),
            jax.ShapeDtypeStruct((1, total), full),
        ),
        in_specs=[pl.BlockSpec(memory_space=pltpu.SMEM), pl.BlockSpec(memory_space=pltpu.VMEM)],
        out_specs=[pl.BlockSpec(memory_space=pltpu.VMEM)] * 2,
        scratch_shapes=[
            pltpu.VMEM((2 * HEAD_DIM, total), low),
            pltpu.VMEM((total, 2 * HEAD_DIM), low),
            pltpu.VMEM((HEAD_DIM + 16, total), low),
        ],
        compiler_params=pltpu.CompilerParams(vmem_limit_bytes=vmem_bytes),
        cost_estimate=pl.CostEstimate(
            flops=20 * total * total * HEAD_DIM, bytes_accessed=4 * rows.size, transcendentals=total * total // 2
        ),
        name="attention_forward",
    )(ends, rows)


def backward_kernel(
    ends_ref, rows_ref, grad_ref, out_ref, mass_ref, result_ref,
    query_s, key_s, keyt_s, value_s, grad_s, grad_key_s, grad_value_s, *, block, copies
):
    sources, _, frames = rows_ref.shape
    utterances = ends_ref.shape[0] - 1
    share = ends_ref[utterances]
    scale = HEAD_DIM**-0.5
    power = scale * log2e
    total = sources * frames
    row = lax.broadcasted_iota(jnp.int32, (HEAD_DIM, frames), 0)
    for source in range(sources):
        span = pl.ds(source * frames, frames)
        stage_scores(ends_ref, rows_ref, source, utterances, query_s, key_s)
        keyt_s[:, span] = rows_ref[source, HEAD_DIM : 2 * HEAD_DIM, :]
        grad = grad_ref[source]
        delta = jnp.sum(grad.astype(full) * out_ref[source].astype(full), axis=0, keepdims=True)
        first = delta.astype(low).astype(full)
        second = (delta - first).astype(low).astype(full)
        third = delta - first - second
        more = jnp.where(row == 0, -first, jnp.where(row == 1, -second, jnp.where(row == 2, -third, 0.0)))
        grad_s[0:HEAD_DIM, span] = grad
        grad_s[HEAD_DIM:, span] = more.astype(low)
        ones = jnp.where(row < 3, 1.0, 0.0).astype(low)
        value_s[span, :] = jnp.concatenate([rows_ref[source, 2 * HEAD_DIM :, :], ones], axis=0).T
    across = (((1,), (1,)), ((), ()))
    if copies > 1:
        grad_key_s[...] = jnp.zeros_like(grad_key_s)
        grad_value_s[...] = jnp.zeros_like(grad_value_s)
        result_ref[:, 0:HEAD_DIM, :] = jnp.zeros((sources, HEAD_DIM, frames), low)

    def query_block(start):
        span = slice(start, start + block)

        def add_keys(first, last, diagonal):
            keys = slice(first, last)
            scores = jnp.dot(key_s[keys, :], query_s[:, span], preferred_element_type=full)
            if diagonal:
                scores = causal(scores)
            probs = jnp.exp2(scores * power - mass_ref[:, span])
            shifted = jnp.dot(value_s[keys, :], grad_s[:, span], preferred_element_type=full)
            grad_scores = (probs * shifted).astype(low)
            grad_value = lax.dot_general(
                grad_s[0:HEAD_DIM, span], probs.astype(low), across, preferred_element_type=full
            )
            grad_key = lax.dot_general(query_s[0:HEAD_DIM, span], grad_scores, across, preferred_element_type=full)
            if diagonal and copies == 1:
                grad_value_s[:, keys] = grad_value
                grad_key_s[:, keys] = grad_key
            else:
                grad_value_s[:, keys] += grad_value
                grad_key_s[:, keys] += grad_key
            return jnp.dot(keyt_s[:, keys], grad_scores, preferred_element_type=full)

        grad_query = add_keys(start, start + block, True)
        if start:
            grad_query = grad_query + add_keys(0, start, False)
        grad_query = (grad_query * scale).astype(low)
        for piece in range(block // frames):
            result_ref[start // frames + piece, 0:HEAD_DIM, :] = grad_query[:, piece * frames : (piece + 1) * frames]

    for start in range(0, total, block):
        shared(share, start // query_share, copies, functools.partial(query_block, start))
    for source in range(sources):
        lanes = slice(source * frames, (source + 1) * frames)
        result_ref[source, HEAD_DIM : 2 * HEAD_DIM, :] = (grad_key_s[:, lanes] * scale).astype(low)
        result_ref[source, 2 * HEAD_DIM :, :] = grad_value_s[:, lanes].astype(low)


def attn_bwd(ends, rows, grads, outs, mass, copies):
    sources, _, frames = rows.shape
    total = sources * frames
    return pl.pallas_call(
        functools.partial(backward_kernel, block=max(frames, total // 16), copies=copies),
        out_shape=jax.ShapeDtypeStruct(rows.shape, low),
        in_specs=[pl.BlockSpec(memory_space=pltpu.SMEM)] + [pl.BlockSpec(memory_space=pltpu.VMEM)] * 4,
        out_specs=pl.BlockSpec(memory_space=pltpu.VMEM),
        scratch_shapes=[
            pltpu.VMEM((2 * HEAD_DIM, total), low),
            pltpu.VMEM((total, 2 * HEAD_DIM), low),
            pltpu.VMEM((HEAD_DIM, total), low),
            pltpu.VMEM((total, 2 * HEAD_DIM), low),
            pltpu.VMEM((2 * HEAD_DIM, total), low),
            pltpu.VMEM((HEAD_DIM, total), full),
            pltpu.VMEM((HEAD_DIM, total), full),
        ],
        compiler_params=pltpu.CompilerParams(vmem_limit_bytes=vmem_bytes),
        cost_estimate=pl.CostEstimate(
            flops=35 * total * total * HEAD_DIM, bytes_accessed=8 * rows.size, transcendentals=total * total // 2
        ),
        name="attention_backward",
    )(ends, rows, grads, outs, mass)


def norm_parts(inputs):
    centred = inputs - jnp.mean(inputs, axis=-1, keepdims=True)
    spread = jnp.mean(centred * centred, axis=-1, keepdims=True)
    inverse = lax.rsqrt(spread + eps)
    return centred * inverse, inverse


def norm_back(grad, unit, inverse, gain):
    scaled = grad * gain
    along = jnp.mean(scaled, axis=-1, keepdims=True)
    across = jnp.mean(scaled * unit, axis=-1, keepdims=True)
    return inverse * (scaled - along - unit * across)


def project_kernel(frames_ref, gain_ref, query_ref, key_ref, value_ref, rows_ref, low_ref):
    @pl.when(pl.program_id(0) == 0)
    def _():
        unit, _ = norm_parts(frames_ref[...].astype(full))
        low_ref[...] = (unit * gain_ref[...]).astype(low)

    heads = rows_ref.shape[0]
    for part, weight_ref in enumerate((query_ref, key_ref, value_ref)):
        packed = jnp.dot(low_ref[...], weight_ref[...], preferred_element_type=full).astype(low).T
        for head in range(heads):
            rows_ref[head, part * HEAD_DIM : (part + 1) * HEAD_DIM, :] = packed[
                head * HEAD_DIM : (head + 1) * HEAD_DIM
            ]


def thirds(features, wide):
    count = features // wide
    return [pl.BlockSpec((features, wide), lambda i, part=part: (0, part * count + i)) for part in range(3)]


def project(frames, gain, w_qkv):
    rows, features = frames.shape
    wide = 4 * HEAD_DIM
    return pl.pallas_call(
        project_kernel,
        grid=(features // wide,),
        out_shape=(
            jax.ShapeDtypeStruct((HEADS, 3 * HEAD_DIM, rows), low),
            jax.ShapeDtypeStruct((rows, features), low),
        ),
        in_specs=[
            pl.BlockSpec((rows, features), lambda i: (0, 0)),
            pl.BlockSpec((1, features), lambda i: (0, 0)),
        ]
        + thirds(features, wide),
        out_specs=[
            pl.BlockSpec((4, 3 * HEAD_DIM, rows), lambda i: (i, 0, 0)),
            pl.BlockSpec((rows, features), lambda i: (0, 0)),
        ],
        compiler_params=pltpu.CompilerParams(vmem_limit_bytes=vmem_bytes),
        cost_estimate=pl.CostEstimate(
            flops=6 * rows * features * features, bytes_accessed=8 * features * features, transcendentals=0
        ),
        name="norm_and_project",
    )(frames, gain[None], w_qkv, w_qkv, w_qkv)


def middle_kernel(
    control_ref, frames_ref, att_ref, cot_ref, gain_ref, out_weight_ref, up_ref, down_ref,
    result_ref, grad_middle_ref, branch_ref, branch_away_ref, grad_att_ref, low_two_ref, act_ref,
    grad_hidden_ref, grad_hidden_away_ref,
    unit_s, inverse_s, sum_s, back_s, low_two_s, mixed_s,
):
    step = pl.program_id(0)
    steps = pl.num_programs(0)
    core = control_ref[0]
    valid = control_ref[1]
    rows, features = frames_ref.shape
    root = 0.7978845608028654
    cubic = 0.044715
    across = (((1,), (1,)), ((), ()))
    present = (lax.broadcasted_iota(jnp.int32, (rows, 1), 0) < valid).astype(full)

    def by_core(array, own_ref, away_ref):
        halves = (array[:, : features // 2], array[:, features // 2 :])
        for value in range(2):

            @pl.when(core == value)
            def _():
                own_ref[...] = halves[value]
                away_ref[...] = halves[1 - value]

    @pl.when(step == 0)
    def _():
        middle = frames_ref[...].astype(full) + jnp.dot(
            att_ref[...].T, out_weight_ref[...], preferred_element_type=full
        )
        unit, inverse = norm_parts(middle)
        unit_s[...] = unit
        inverse_s[...] = inverse
        low_two_s[...] = (unit * gain_ref[...]).astype(low)
        low_two_ref[...] = low_two_s[...].T
        mixed_s[...] = (cot_ref[...].astype(full) * present).astype(low)
        sum_s[...] = middle
        back_s[...] = jnp.zeros_like(back_s)

    hidden = jnp.dot(low_two_s[...], up_ref[...], preferred_element_type=full)
    grad_act = lax.dot_general(mixed_s[...], down_ref[...], across, preferred_element_type=full)
    square = hidden * hidden
    bent = jnp.tanh(root * hidden * (1.0 + cubic * square))
    half = 0.5 * (1.0 + bent)
    act = (hidden * half).astype(low)
    slope = half + (0.5 * root) * hidden * (1.0 - bent * bent) * (1.0 + (3.0 * cubic) * square)
    grad_hidden = (slope * grad_act).astype(low)
    turned = act.T
    places, cores, high, piece, _ = act_ref.shape
    for at in range(high * places * cores):
        outer, place, half = at // (places * cores), at // cores % places, at % cores
        act_ref[place, half, outer] = turned[at * piece : (at + 1) * piece]

    @pl.when(step < steps // 2)
    def _():
        grad_hidden_ref[...] = grad_hidden

    @pl.when(step >= steps // 2)
    def _():
        grad_hidden_away_ref[...] = grad_hidden

    sum_s[...] += jnp.dot(act, down_ref[...], preferred_element_type=full)
    back_s[...] += lax.dot_general(grad_hidden, up_ref[...], across, preferred_element_type=full)

    @pl.when(step == steps - 1)
    def _():
        result_ref[...] = (present * sum_s[...]).astype(low)
        grad_middle = mixed_s[...].astype(full) + norm_back(
            back_s[...], unit_s[...], inverse_s[...], gain_ref[...]
        )
        grad_middle_ref[...] = grad_middle
        branch = grad_middle.astype(low)
        by_core(branch, branch_ref, branch_away_ref)
        grad_att = lax.dot_general(out_weight_ref[...], branch, across, preferred_element_type=full)
        lane = (lax.broadcasted_iota(jnp.int32, (1, rows), 1) < valid).astype(full)
        grad_att_ref[...] = (grad_att * lane).astype(low)


def middle_part(core, valid, frames, att, cot, gain, w_out, w_up, w_down):
    rows, features = frames.shape
    hidden = w_up.shape[1]
    wide = 1024
    steps = hidden // wide
    size = lax.axis_size("seq")
    piece = hidden // size
    here = lambda i, s: (i + s[0] * (steps // 2)) % steps
    whole = lambda *shape: pl.BlockSpec(shape, lambda i, s: (0,) * len(shape))
    square = (rows, features)
    turned = (features, rows)
    halved = (rows, features // 2)
    outs = [
        (square, low, None),
        (square, full, None),
        (halved, low, None),
        (halved, low, None),
        (turned, low, None),
        (turned, low, None),
        (
            (4, 2, size // 4, piece // 2, rows),
            low,
            pl.BlockSpec((4, 2, wide // piece // 4, piece // 2, rows), lambda i, s: (0, 0, here(i, s), 0, 0)),
        ),
        ((rows, hidden // 2), low, pl.BlockSpec((rows, wide), lambda i, s: (0, jnp.minimum(i, steps // 2 - 1)))),
        ((rows, hidden // 2), low, pl.BlockSpec((rows, wide), lambda i, s: (0, jnp.maximum(i - steps // 2, 0)))),
    ]
    return pl.pallas_call(
        middle_kernel,
        grid_spec=pltpu.PrefetchScalarGridSpec(
            num_scalar_prefetch=1,
            grid=(steps,),
            in_specs=[
                whole(*square),
                whole(*turned),
                whole(*square),
                whole(1, features),
                whole(features, features),
                pl.BlockSpec((features, wide), lambda i, s: (0, here(i, s))),
                pl.BlockSpec((wide, features), lambda i, s: (here(i, s), 0)),
            ],
            out_specs=[spec or whole(*shape) for shape, _, spec in outs],
            scratch_shapes=[
                pltpu.VMEM(square, full),
                pltpu.VMEM((rows, 1), full),
                pltpu.VMEM(square, full),
                pltpu.VMEM(square, full),
                pltpu.VMEM(square, low),
                pltpu.VMEM(square, low),
            ],
        ),
        out_shape=[jax.ShapeDtypeStruct(shape, kind) for shape, kind, _ in outs],
        compiler_params=pltpu.CompilerParams(vmem_limit_bytes=vmem_bytes),
        cost_estimate=pl.CostEstimate(
            flops=8 * rows * features * hidden + 4 * rows * features * features,
            bytes_accessed=4 * features * hidden + 2 * features * features,
            transcendentals=rows * hidden,
        ),
        name="middle",
    )(jnp.stack([core, valid]), frames, att, cot, gain[None], w_out, w_up, w_down)


def finish_kernel(frames_ref, middle_ref, gain_ref, rows_ref, query_ref, key_ref, value_ref, result_ref, back_s):
    step = pl.program_id(0)
    heads, _, rows = rows_ref.shape

    @pl.when(step == 0)
    def _():
        back_s[...] = jnp.zeros_like(back_s)

    total = back_s[...]
    for part, weight_ref in enumerate((query_ref, key_ref, value_ref)):
        grads = rows_ref[:, part * HEAD_DIM : (part + 1) * HEAD_DIM, :].reshape(heads * HEAD_DIM, rows)
        total = total + jnp.dot(weight_ref[...], grads, preferred_element_type=full)
    back_s[...] = total

    @pl.when(step == pl.num_programs(0) - 1)
    def _():
        unit, inverse = norm_parts(frames_ref[...].astype(full))
        result_ref[...] = middle_ref[...] + norm_back(back_s[...].T, unit, inverse, gain_ref[...])


def finish(frames, grad_middle, gain, grad_rows, w_qkv):
    rows, features = frames.shape
    wide = 4 * HEAD_DIM
    whole = lambda *shape: pl.BlockSpec(shape, lambda i: (0,) * len(shape))
    return pl.pallas_call(
        finish_kernel,
        grid=(features // wide,),
        out_shape=jax.ShapeDtypeStruct((rows, features), full),
        in_specs=[
            whole(rows, features),
            whole(rows, features),
            whole(1, features),
            pl.BlockSpec((4, 3 * HEAD_DIM, rows), lambda i: (i, 0, 0)),
        ]
        + thirds(features, wide),
        out_specs=whole(rows, features),
        scratch_shapes=[pltpu.VMEM((features, rows), full)],
        compiler_params=pltpu.CompilerParams(vmem_limit_bytes=vmem_bytes),
        cost_estimate=pl.CostEstimate(
            flops=6 * rows * features * features, bytes_accessed=8 * features * features, transcendentals=0
        ),
        name="input_gradient",
    )(frames, grad_middle, gain[None], grad_rows, w_qkv, w_qkv, w_qkv)


def terms_kernel(pick_ref, *refs, groups, needs, sets):
    step = pl.program_id(0)
    refs = list(refs)
    take = lambda count: [refs.pop(0) for _ in range(count)]
    lefts = [{kind: take(2) for kind in kinds} for kinds in needs]
    rights = [take(2) for _ in range(2)]
    aways, kepts = take(len(sets)), take(len(sets))

    def write(outs):
        for out_ref, members in zip(outs, sets):
            at = 0
            for group in members:
                for kind, start, stop in groups[group][3]:
                    own_ref, other_ref = lefts[group][kind]
                    rows, frames = own_ref.shape[-2:]
                    left = jnp.concatenate([ref[...].reshape(-1, frames) for ref in (own_ref, other_ref)], axis=1)
                    right = jnp.concatenate([ref[:, start:stop] for ref in rights[kind]], axis=0)
                    terms = jnp.dot(left, right, preferred_element_type=full)
                    out_ref[:, :, at : at + stop - start] = terms.astype(low).reshape(-1, rows, stop - start)
                    at += stop - start

    @pl.when(step < 2)
    def _():
        write(aways)

    @pl.when(step >= 2)
    def _():
        write(kepts)


def terms_by_piece(groups, sets, bits, two, att, hidden, branch):
    size = lax.axis_size("seq")
    features, frames = two[0].shape
    rows = features // size
    quarter = size // 4
    widths = [sum(stop - start for group in members for _, start, stop in groups[group][3]) for members in sets]
    needs = [sorted({kind for kind, _, _ in parts}) for *_, parts in groups]
    lefts, specs = [], []
    for (first, after, _, _), kinds in zip(groups, needs):
        upper, lower = max(first, after), min(first, after)
        cut = (size >> (upper + 1), 2, 1 << (upper - lower - 1), 2, 1 << lower)

        def index(i, s, first=first, after=after, upper=upper):
            value = s[first] ^ (1 - i // 2)
            beyond = s[after] ^ (1 - i % 2)
            outer, inner = (value, beyond) if upper == first else (beyond, value)
            return (0, outer, 0, inner, 0, 0, 0)

        for kind in kinds:
            lefts += [a.reshape(cut + (rows, frames)) for a in (two, att)[kind]]
            specs += [pl.BlockSpec((cut[0], 1, cut[2], 1, cut[4], rows, frames), index)] * 2
    rights = (*hidden, *branch)
    specs += [pl.BlockSpec(a.shape, lambda i, s: (0, 0)) for a in rights]
    outs = [pl.BlockSpec((None, quarter, rows, w), lambda i, s: (jnp.minimum(i, 1), 0, 0, 0)) for w in widths]
    outs += [pl.BlockSpec((None, quarter, rows, w), lambda i, s: (jnp.maximum(i - 2, 0), 0, 0, 0)) for w in widths]
    terms = pl.pallas_call(
        functools.partial(terms_kernel, groups=groups, needs=needs, sets=sets),
        grid_spec=pltpu.PrefetchScalarGridSpec(num_scalar_prefetch=1, grid=(4,), in_specs=specs, out_specs=outs),
        out_shape=[jax.ShapeDtypeStruct((2, quarter, rows, w), low) for w in widths * 2],
        compiler_params=pltpu.CompilerParams(vmem_limit_bytes=vmem_bytes),
        cost_estimate=pl.CostEstimate(
            flops=4 * frames * features * sum(widths), bytes_accessed=4 * features * sum(widths), transcendentals=0
        ),
        name="terms_by_piece",
    )(jnp.stack(bits), *lefts, *rights)
    return terms[: len(sets)], terms[len(sets) :]


def tall_terms_kernel(pick_ref, *refs):
    step = pl.program_id(0)
    acts, mixed, outs = refs[:8], refs[8:16], refs[16:]
    high, rows, frames = acts[0].shape

    def write(out_ref):
        total = None
        for act_ref, mixed_ref in zip(acts, mixed):
            terms = jnp.dot(act_ref[...].reshape(high * rows, frames), mixed_ref[...], preferred_element_type=full)
            total = terms if total is None else total + terms
        out_ref[...] = total.astype(low).reshape(out_ref.shape)

    for value in range(2):
        pl.when(step == value)(functools.partial(write, outs[value]))


def tall_terms(core, place, bit, act_own, act_other, mixed_own, mixed_other):
    count, _, high, rows, frames = act_own.shape
    features = mixed_own[0].shape[-1]
    half = high // 2
    cut = lambda a: a.reshape(a.shape[:-3] + (half, 2, rows, frames))
    own = lambda other: pl.BlockSpec(
        (None, None, half, None, rows, frames), lambda i, s: (s[1] ^ other, s[0], 0, s[2] ^ (1 - i), 0, 0)
    )
    away = lambda other: pl.BlockSpec(
        (None, half, None, rows, frames), lambda i, s: (s[1] ^ other, 0, s[2] ^ (1 - i), 0, 0)
    )
    whole = lambda *shape: pl.BlockSpec(shape, lambda i, s: (0,) * len(shape))
    return pl.pallas_call(
        tall_terms_kernel,
        grid_spec=pltpu.PrefetchScalarGridSpec(
            num_scalar_prefetch=1,
            grid=(2,),
            in_specs=[own(other) for other in range(4)]
            + [away(other) for other in range(4)]
            + [whole(frames, features)] * 8,
            out_specs=[whole(half, rows, features)] * 2,
        ),
        out_shape=[jax.ShapeDtypeStruct((half, rows, features), low)] * 2,
        compiler_params=pltpu.CompilerParams(vmem_limit_bytes=vmem_bytes),
        cost_estimate=pl.CostEstimate(
            flops=4 * count * frames * high * rows * features, bytes_accessed=16 * frames * features, transcendentals=0
        ),
        name="tall_terms",
    )(jnp.stack([core, place, bit]), *[cut(act_own)] * 4, *[cut(act_other)] * 4, *mixed_own, *mixed_other)


def add_split_kernel(pick_ref, *refs, sets, spans):
    step = pl.program_id(0)
    terms, outs = refs[: 2 * len(spans)], refs[2 * len(spans) :]

    def write(outs):
        for out_ref, members in zip(outs, sets):
            at = 0
            for group in members:
                first, second = [ref[:, :, :, spans[group]] for ref in terms[2 * group : 2 * group + 2]]
                width = first.shape[-1]
                out_ref[:, :, :, at : at + width] = (first.astype(full) + second.astype(full)).astype(low)
                at += width

    pl.when(step == 0)(functools.partial(write, outs[: len(sets)]))
    pl.when(step == 1)(functools.partial(write, outs[len(sets) :]))


def add_split(pairs, old_sets, sets, widths, outer, inner, mine):
    rows = pairs[0][0].shape[-2]
    arrays, specs, spans = [], [], []
    for group in range(len(widths)):
        ((which, members),) = [(which, members) for which, members in enumerate(old_sets) if group in members]
        at = sum(widths[other] for other in members[: members.index(group)])
        spans.append(slice(at, at + widths[group]))
        index = lambda i, s, group=group: (0, s[group] ^ (1 - i), 0, 0, 0)
        columns = pairs[which][0].shape[-1]
        arrays += [a.reshape(outer, 2, inner, rows, columns) for a in pairs[which]]
        specs += [pl.BlockSpec((outer, None, inner, rows, columns), index)] * 2
    shapes = [(outer, inner, rows, sum(widths[group] for group in members)) for members in sets]
    sums = pl.pallas_call(
        functools.partial(add_split_kernel, sets=sets, spans=spans),
        grid_spec=pltpu.PrefetchScalarGridSpec(
            num_scalar_prefetch=1,
            grid=(2,),
            in_specs=specs,
            out_specs=[pl.BlockSpec(shape, lambda i, s: (0, 0, 0, 0)) for shape in shapes * 2],
        ),
        out_shape=[jax.ShapeDtypeStruct(shape, low) for shape in shapes * 2],
        compiler_params=pltpu.CompilerParams(vmem_limit_bytes=vmem_bytes),
        name="add_split",
    )(jnp.stack(mine), *arrays)
    sums = [a.reshape((outer * inner,) + a.shape[2:]) for a in sums]
    return sums[: len(sets)], sums[len(sets) :]


def plane_terms_kernel(pick_ref, *refs):
    rows, lows, (keep_ref, send_ref, turn_s) = refs[:4], refs[4:8], refs[8:]
    core = pick_ref[0]
    lines, columns, frames = rows[0].shape
    total = None
    for rows_ref, low_ref in zip(rows, lows):
        terms = jnp.dot(rows_ref[...].reshape(lines * columns, frames), low_ref[...], preferred_element_type=full)
        total = terms if total is None else total + terms
    turn_s[...] = total.T.reshape(turn_s.shape)
    keep_ref[...] = turn_s[:, :, core].reshape(keep_ref.shape)
    send_ref[...] = turn_s[:, :, 1 - core].astype(low).reshape(send_ref.shape)


def plane_terms(core, place, line_rows, lows):
    lines, count, columns, frames = line_rows.shape
    features = lows[0].shape[-1]
    rows = features // lines // count // 2
    shape = (lines, count * rows, lines * columns)
    whole = pl.BlockSpec(shape, lambda i, s: (0, 0, 0))
    source = lambda other: pl.BlockSpec((lines, None, columns, frames), lambda i, s: (0, s[1] ^ other, 0, 0))
    return pl.pallas_call(
        plane_terms_kernel,
        grid_spec=pltpu.PrefetchScalarGridSpec(
            num_scalar_prefetch=1,
            grid=(1,),
            in_specs=[source(other) for other in range(4)]
            + [pl.BlockSpec((frames, features), lambda i, s: (0, 0))] * 4,
            out_specs=[whole, whole],
            scratch_shapes=[pltpu.VMEM((lines, count, 2, rows, lines * columns), full)],
        ),
        out_shape=(jax.ShapeDtypeStruct(shape, full), jax.ShapeDtypeStruct(shape, low)),
        compiler_params=pltpu.CompilerParams(vmem_limit_bytes=vmem_bytes),
        cost_estimate=pl.CostEstimate(
            flops=2 * lines * count * columns * frames * features, bytes_accessed=8 * line_rows.size, transcendentals=0
        ),
        name="plane_terms",
    )(jnp.stack([core, place]), *[line_rows] * 4, *lows)


def gain_sum(weights, grads, gain):
    total = jnp.sum(weights.astype(full) * grads, axis=1, keepdims=True)
    return jnp.broadcast_to(total, (total.shape[0], 128)).T[0:1] / gain


def wide_output_kernel(pick_ref, halves_ref, weight_ref, gain_ref, up_ref, out_ref, sum_ref):
    split, half = up_ref.shape[1] // 2, out_ref.shape[1] // 2
    for side in range(2):
        up_ref[:, side * split : (side + 1) * split] = halves_ref[side, :, 0:split].astype(full)
        out_ref[:, side * half : (side + 1) * half] = halves_ref[side, :, split : split + half].astype(full)
    sum_ref[...] = gain_sum(weight_ref[...], up_ref[...], gain_ref[...])


def tall_output_kernel(pick_ref, halves_ref, weight_ref, gain_ref, qkv_ref, sum_ref):
    rows = qkv_ref.shape[0] // 2
    for side in range(2):
        qkv_ref[side * rows : (side + 1) * rows, :] = halves_ref[side].astype(full)
    sum_ref[...] = gain_sum(weight_ref[...], qkv_ref[...], gain_ref[...])


def write_outputs(kernel, halves, weight, gain, shapes, name):
    size = lax.axis_size("seq")
    rows = weight.shape[0] // size
    whole = lambda *shape: pl.BlockSpec(shape, lambda i, s: (0,) * len(shape))
    shapes = [*shapes, (1, rows)]
    return pl.pallas_call(
        kernel,
        grid_spec=pltpu.PrefetchScalarGridSpec(
            num_scalar_prefetch=1,
            grid=(1,),
            in_specs=[
                whole(*halves.shape),
                pl.BlockSpec((rows, weight.shape[1]), lambda i, s: (s[0], 0)),
                pl.BlockSpec((None, 1, rows), lambda i, s: (s[0], 0, 0)),
            ],
            out_specs=[whole(*shape) for shape in shapes],
        ),
        out_shape=[jax.ShapeDtypeStruct(shape, full) for shape in shapes],
        compiler_params=pltpu.CompilerParams(vmem_limit_bytes=vmem_bytes),
        name=name,
    )(lax.axis_index("seq")[None], halves, weight, gain.reshape(size, 1, rows))


def other_core(array):
    count = lax.axis_size("items")
    return lax.ppermute(array, "items", [(i, i ^ 1) for i in range(count)])


def to_heads(array):
    copies = lax.axis_size("seq") // HEADS
    if copies > 1:
        array = jnp.repeat(array, copies, axis=0)
    return lax.all_to_all(array, "seq", 0, 0, tiled=True)


def by_head(array, axis):
    copies = array.shape[axis] // HEADS
    if copies == 1:
        return array
    shape = array.shape[:axis] + (HEADS, copies) + array.shape[axis + 1 :]
    return jnp.sum(array.reshape(shape).astype(full), axis=axis + 1).astype(low)


def pick(array, index, axis):
    return lax.dynamic_index_in_dim(array, index, axis, keepdims=False)


def flipped(array, bit):
    return lax.ppermute(array, "seq", [(i, i ^ (1 << bit)) for i in range(lax.axis_size("seq"))])


def split_terms(terms, bit, left):
    axis = left.index(bit)
    mine = (lax.axis_index("seq") >> bit) & 1
    terms = [a.reshape((2,) * len(left) + a.shape[-2:]) for a in terms]

    def part(value):
        chosen = [pick(a, value, axis) for a in terms]
        return chosen[0] if len(chosen) == 1 else (chosen[0].astype(full) + chosen[1].astype(full)).astype(low)

    left.remove(bit)
    return part(1 - mine), part(mine)


def together(first, second):
    return (first.astype(full) + second.astype(full)).astype(low)


def over_items(piece):
    count = lax.axis_size("items")
    if count == 2:
        other = other_core(piece)
        first = lax.axis_index("items") == 0
        return jnp.stack([jnp.where(first, piece, other), jnp.where(first, other, piece)])
    pieces = lax.all_gather(piece, "items", axis=0)
    return jnp.sum(pieces.reshape((count // 2, 2) + piece.shape).astype(full), axis=0)


def on_device(frames, lengths, w_qkv, w_out, w_up, w_down, gain_one, gain_two, cotangent):
    row_count, features = frames.shape[1:]
    hidden_count = w_up.shape[1]
    size = lax.axis_size("seq")
    depth = size.bit_length() - 1
    me = lax.axis_index("seq")
    core = lax.axis_index("items") % 2
    copies = size // HEADS
    ends = jnp.cumsum(lengths[0]).astype(jnp.int32)
    valid = jnp.clip(ends[-1] - me * row_count, 0, row_count)
    control = jnp.concatenate([ends, (me % copies)[None]])
    rows_out = features // size

    lines = size // 4
    fours = [list(range(at, at + 4)) for at in range(0, size, 4)]
    columns = [list(range(at, size, 4)) for at in range(4)]
    across = lambda array, groups: lax.all_to_all(array, "seq", 0, 0, tiled=True, axis_index_groups=groups)
    bits = [(me >> bit) & 1 for bit in range(depth)]

    head_parts, low_one = project(frames[0], gain_one, w_qkv)
    head_rows = to_heads(head_parts)
    mixed = cotangent[0] * (jnp.arange(row_count) < valid).astype(low)[:, None]
    mixed_x, mixed_y = flipped(mixed, 0), flipped(mixed, 1)
    head_rows, low_one, mixed_x, mixed_y = lax.optimization_barrier((head_rows, low_one, mixed_x, mixed_y))
    low_x, mixed_xy = flipped(low_one, 0), flipped(mixed_x, 1)
    head_out, log_mass = attn_fwd(control, head_rows, copies)
    head_out, low_x, mixed_xy = lax.optimization_barrier((head_out, low_x, mixed_xy))
    mixed_own = (mixed, mixed_x, mixed_y, mixed_xy)
    moved = lax.all_to_all(head_out, "seq", 0, 0, tiled=True)
    attended = by_head(moved, 0).reshape(features, row_count)
    attended, low_one, low_x = lax.optimization_barrier((attended, low_one, low_x))
    lows = (low_one, low_x, flipped(low_one, 1), flipped(low_x, 1))
    att = (attended, other_core(attended))

    result, grad_middle, branch, branch_away, grad_attended, two, act, hidden, hidden_away = middle_part(
        core, valid, frames[0], attended, cotangent[0], gain_two, w_out, w_up, w_down
    )
    grad_attended, lows = lax.optimization_barrier((grad_attended, lows))
    grad_heads = to_heads(grad_attended.reshape(HEADS, HEAD_DIM, row_count))
    acts = across(act, fours)

    pairs = (
        (two, other_core(two)),
        att,
        (hidden, other_core(hidden_away)),
        (branch, other_core(branch_away)),
    )
    half = features // 2
    split = hidden_count // 2
    groups = (
        (0, 1, 2, ((0, 0, half),)),
        (1, 0, 2, ((0, half, 2 * half),)),
        (2, 0, 1, ((0, 2 * half, 7 * half // 2),)),
        (2, 1, 0, ((0, 7 * half // 2, split), (1, 0, half))),
    )
    widths = [sum(stop - start for _, start, stop in parts) for *_, parts in groups]
    sets = [((0,), (1,), (2, 3)), ((0, 3), (1, 2)), ((0, 1), (2,), (3,)), ((0, 1, 2, 3),)]
    travel = lambda arrays, turn: [flipped(a, groups[members[0]][turn]) for a, members in zip(arrays, sets[turn])]
    away, kept = terms_by_piece(groups, sets[0], bits[:3], *pairs)
    came = travel(away, 0)
    mixed_other = [other_core(a) for a in mixed_own]
    grad_heads, mixed_other, *kept = lax.optimization_barrier((grad_heads, mixed_other, *kept))

    grad_rows = attn_bwd(control, head_rows, grad_heads, head_out, log_mass, copies)
    grad_rows, acts, *came = lax.optimization_barrier((grad_rows, acts, *came))
    line_rows = across(grad_rows.reshape(lines, 4, 3 * HEAD_DIM, row_count), columns)

    sends, keeps = add_split(list(zip(kept, came)), sets[0], sets[1], widths, 1, lines, [1 + 0 * me] * 4)
    acts, *sends = lax.optimization_barrier((acts, *sends))
    came = travel(sends, 1)
    acts_other = other_core(pick(acts, 1 - core, 1))
    tall_send, tall_keep = tall_terms(core, me % 4, bits[2], acts, acts_other, mixed_own, mixed_other)
    tall_came = flipped(tall_send, 2)
    tall_keep, *came = lax.optimization_barrier((tall_keep, *came))

    sends, keeps = add_split(list(zip(keeps, came)), sets[1], sets[2], widths, lines // 2, 1, [bits[group[2]] for group in groups])
    line_rows, *sends = lax.optimization_barrier((line_rows, *sends))
    came = travel(sends, 2)
    keep, send = plane_terms(core, me % 4, line_rows, lows)
    turned = line_rows.transpose(1, 0, 2, 3)
    keep, send, turned, tall_came, *came = lax.optimization_barrier((keep, send, turned, tall_came, *came))
    (wide_send,), (wide_keep,) = add_split(list(zip(keeps, came)), sets[2], sets[3], widths, lines // 4, 1, [bits[3]] * 4)
    tall_left = list(range(depth - 1, 2, -1))
    tall_send, tall_keep = split_terms((tall_keep, tall_came), 3, tall_left)
    keep, wide_send, tall_send = lax.optimization_barrier((keep, wide_send, tall_send))
    wide_terms, wide_left = (wide_keep, flipped(wide_send, 3)), list(range(depth - 1, 3, -1))
    tall_rest = (tall_keep, flipped(tall_send, 3))
    for bit in range(4, depth):
        more, rest = split_terms(wide_terms, bit, wide_left)
        wide_terms = (rest, flipped(more, bit))
        more, rest = split_terms(tall_rest, bit, tall_left)
        tall_rest = (rest, flipped(more, bit))

    both = (keep + other_core(send).astype(full)).astype(low)
    grad_packed = across(turned, fours)
    line_left = list(range(depth - 1, 1, -1))
    send, line_keep = split_terms((both,), 2, line_left)
    line_came, wide_came, tall_came = lax.optimization_barrier((flipped(send, 2), wide_terms[1], tall_rest[1]))
    line_terms, wide_terms, tall_rest = (line_keep, line_came), (wide_terms[0], wide_came), (tall_rest[0], tall_came)
    for bit in range(3, depth):
        send, keep = split_terms(line_terms, bit, line_left)
        line_terms = (keep, flipped(send, bit))
    pieces = across(together(*line_terms).reshape(4, rows_out // 2, lines * 3 * HEAD_DIM), fours)

    grad_packed = by_head(grad_packed.transpose(1, 0, 2, 3).reshape(size, 3 * HEAD_DIM, row_count), 0)
    grad_inputs = finish(frames[0], grad_middle, gain_one, grad_packed, w_qkv)
    grad_inputs, pieces, wide_came, tall_came = lax.optimization_barrier(
        (grad_inputs, pieces, wide_terms[1], tall_rest[1])
    )
    sums = over_items(together(wide_terms[0], wide_came).reshape(rows_out, split + half))
    up, out, sum_gain_two = write_outputs(
        wide_output_kernel, sums, w_up, gain_two, [(rows_out, hidden_count), (rows_out, features)], "wide_outputs"
    )
    down = over_items(together(tall_rest[0], tall_came).reshape(-1, features)).astype(full)
    down = down.reshape(hidden_count // size, features)
    pieces = pieces.reshape(4, rows_out // 2, lines, 3, HEAD_DIM).transpose(1, 3, 2, 0, 4)
    pieces = by_head(pieces.reshape(rows_out // 2, 3, size, HEAD_DIM), 2)
    pieces = over_items(pieces.reshape(rows_out // 2, 3 * features))
    qkv, sum_gain_one = write_outputs(
        tall_output_kernel, pieces, w_qkv, gain_one, [(rows_out, 3 * features)], "tall_outputs"
    )
    return (result[None], grad_inputs[None], qkv, out, up, down, sum_gain_one[0], sum_gain_two[0])


def solution(mesh):
    return jax.shard_map(
        on_device,
        mesh=mesh,
        in_specs=(
            P("items", "seq", None),
            P("items", None),
            P(),
            P(),
            P(),
            P(),
            P(),
            P(),
            P("items", "seq", None),
        ),
        out_specs=(
            P("items", "seq", None),
            P("items", "seq", None),
            P("seq", None),
            P("seq", None),
            P("seq", None),
            P("seq", None),
            P("seq"),
            P("seq"),
        ),
        check_vma=False,
    )
```

```python
import functools

import jax
import jax.numpy as jnp
from jax import lax
from jax.experimental import pallas as pl
from jax.experimental.pallas import tpu as pltpu
from jax.sharding import PartitionSpec as P

HEADS = 16
HEAD_DIM = 64
eps = 1e-05
masked = -1e30
log2e = 1.4426950408889634
query_share = 1024
vmem_bytes = 56 * 2**20
low = jnp.bfloat16
full = jnp.float32


def lane_labels(ends_ref, utterances, start, rows, count):
    place = start + lax.broadcasted_iota(jnp.int32, (rows, count), 1)
    label = jnp.zeros((rows, count), jnp.int32)
    for u in range(utterances):
        label = label + (place >= ends_ref[u]).astype(jnp.int32)
    return label


def stage_scores(ends_ref, rows_ref, source, utterances, query_s, key_s):
    frames = rows_ref.shape[2]
    label = lane_labels(ends_ref, utterances, source * frames, HEAD_DIM, frames)
    row = lax.broadcasted_iota(jnp.int32, (HEAD_DIM, frames), 0)
    own = jnp.where(row == label, 1.0, 0.0).astype(low)
    barred = jnp.where((row != label) & (row <= utterances), masked, 0.0).astype(low)
    span = pl.ds(source * frames, frames)
    query_s[0:HEAD_DIM, span] = rows_ref[source, 0:HEAD_DIM, :]
    query_s[HEAD_DIM:, span] = own
    key_s[span, :] = jnp.concatenate([rows_ref[source, HEAD_DIM : 2 * HEAD_DIM, :], barred], axis=0).T


def causal(scores):
    key_place = lax.broadcasted_iota(jnp.int32, scores.shape, 0)
    query_place = lax.broadcasted_iota(jnp.int32, scores.shape, 1)
    return jnp.where(key_place <= query_place, scores, masked)


def forward_kernel(ends_ref, rows_ref, out_ref, mass_ref, query_s, key_s, value_s, *, block, part, copies):
    sources, _, frames = rows_ref.shape
    utterances = ends_ref.shape[0] - 1
    share = ends_ref[utterances]
    power = HEAD_DIM**-0.5 * log2e
    total = sources * frames
    for source in range(sources):
        stage_scores(ends_ref, rows_ref, source, utterances, query_s, key_s)
        span = pl.ds(source * frames, frames)
        value_s[0:HEAD_DIM, span] = rows_ref[source, 2 * HEAD_DIM :, :]
        row = lax.broadcasted_iota(jnp.int32, (value_s.shape[0] - HEAD_DIM, frames), 0)
        value_s[HEAD_DIM:, span] = jnp.where(row == 0, 1.0, 0.0).astype(low)
    if copies > 1:
        out_ref[...] = jnp.zeros_like(out_ref)
        mass_ref[...] = jnp.zeros_like(mass_ref)

    def add_keys(current, query, start, stop, diagonal):
        scores = jnp.dot(key_s[start:stop, :], query, preferred_element_type=full)
        if diagonal:
            scores = causal(scores)
        new_peak = jnp.max(scores, axis=0, keepdims=True) * power
        if current is not None:
            new_peak = jnp.maximum(current[0], new_peak)
        weights = jnp.exp2(scores * power - new_peak)
        sums = jnp.dot(value_s[:, start:stop], weights.astype(low), preferred_element_type=full)
        if current is not None:
            sums = sums + current[1] * jnp.exp2(current[0] - new_peak)
        return new_peak, sums

    def query_block(start):
        query = query_s[:, start : start + block]
        whole = add_keys(None, query, 0, start, False) if start else None
        for at in range(0, block, part):
            lanes = slice(at, at + part)
            current = None if whole is None else (whole[0][:, lanes], whole[1][:, lanes])
            if at:
                current = add_keys(current, query[:, lanes], start, start + at, False)
            peak, sums = add_keys(current, query[:, lanes], start + at, start + at + part, True)
            mass = sums[HEAD_DIM : HEAD_DIM + 1]
            label = lane_labels(ends_ref, utterances, start + at, 1, part)
            out = (sums[0:HEAD_DIM] * jnp.where(label < utterances, 1.0 / mass, 0.0)).astype(low)
            mass_ref[:, start + at : start + at + part] = peak + jnp.log2(mass)
            for piece in range(part // frames):
                out_ref[(start + at) // frames + piece] = out[:, piece * frames : (piece + 1) * frames]

    for start in range(0, total, block):
        shared(share, start // query_share, copies, functools.partial(query_block, start))


def shared(share, turn, copies, work):
    if copies == 1:
        work()
    else:
        pl.when(share == turn % copies)(work)


def attn_fwd(ends, rows, copies):
    sources, _, frames = rows.shape
    total = sources * frames
    return pl.pallas_call(
        functools.partial(forward_kernel, block=query_share, part=query_share, copies=copies),
        out_shape=(
            jax.ShapeDtypeStruct((sources, HEAD_DIM, frames), low),
            jax.ShapeDtypeStruct((1, total), full),
        ),
        in_specs=[pl.BlockSpec(memory_space=pltpu.SMEM), pl.BlockSpec(memory_space=pltpu.VMEM)],
        out_specs=[pl.BlockSpec(memory_space=pltpu.VMEM)] * 2,
        scratch_shapes=[
            pltpu.VMEM((2 * HEAD_DIM, total), low),
            pltpu.VMEM((total, 2 * HEAD_DIM), low),
            pltpu.VMEM((HEAD_DIM + 16, total), low),
        ],
        compiler_params=pltpu.CompilerParams(vmem_limit_bytes=vmem_bytes),
        cost_estimate=pl.CostEstimate(
            flops=20 * total * total * HEAD_DIM, bytes_accessed=4 * rows.size, transcendentals=total * total // 2
        ),
        name="attention_forward",
    )(ends, rows)


def backward_kernel(
    ends_ref, rows_ref, grad_ref, out_ref, mass_ref, result_ref,
    query_s, key_s, keyt_s, value_s, grad_s, grad_key_s, grad_value_s, *, block, copies
):
    sources, _, frames = rows_ref.shape
    utterances = ends_ref.shape[0] - 1
    share = ends_ref[utterances]
    scale = HEAD_DIM**-0.5
    power = scale * log2e
    total = sources * frames
    row = lax.broadcasted_iota(jnp.int32, (HEAD_DIM, frames), 0)
    for source in range(sources):
        span = pl.ds(source * frames, frames)
        stage_scores(ends_ref, rows_ref, source, utterances, query_s, key_s)
        keyt_s[:, span] = rows_ref[source, HEAD_DIM : 2 * HEAD_DIM, :]
        grad = grad_ref[source]
        delta = jnp.sum(grad.astype(full) * out_ref[source].astype(full), axis=0, keepdims=True)
        first = delta.astype(low).astype(full)
        second = (delta - first).astype(low).astype(full)
        third = delta - first - second
        more = jnp.where(row == 0, -first, jnp.where(row == 1, -second, jnp.where(row == 2, -third, 0.0)))
        grad_s[0:HEAD_DIM, span] = grad
        grad_s[HEAD_DIM:, span] = more.astype(low)
        ones = jnp.where(row < 3, 1.0, 0.0).astype(low)
        value_s[span, :] = jnp.concatenate([rows_ref[source, 2 * HEAD_DIM :, :], ones], axis=0).T
    across = (((1,), (1,)), ((), ()))
    if copies > 1:
        grad_key_s[...] = jnp.zeros_like(grad_key_s)
        grad_value_s[...] = jnp.zeros_like(grad_value_s)
        result_ref[:, 0:HEAD_DIM, :] = jnp.zeros((sources, HEAD_DIM, frames), low)

    def query_block(start):
        span = slice(start, start + block)

        def add_keys(first, last, diagonal):
            keys = slice(first, last)
            scores = jnp.dot(key_s[keys, :], query_s[:, span], preferred_element_type=full)
            if diagonal:
                scores = causal(scores)
            probs = jnp.exp2(scores * power - mass_ref[:, span])
            shifted = jnp.dot(value_s[keys, :], grad_s[:, span], preferred_element_type=full)
            grad_scores = (probs * shifted).astype(low)
            grad_value = lax.dot_general(
                grad_s[0:HEAD_DIM, span], probs.astype(low), across, preferred_element_type=full
            )
            grad_key = lax.dot_general(query_s[0:HEAD_DIM, span], grad_scores, across, preferred_element_type=full)
            if diagonal and copies == 1:
                grad_value_s[:, keys] = grad_value
                grad_key_s[:, keys] = grad_key
            else:
                grad_value_s[:, keys] += grad_value
                grad_key_s[:, keys] += grad_key
            return jnp.dot(keyt_s[:, keys], grad_scores, preferred_element_type=full)

        grad_query = add_keys(start, start + block, True)
        if start:
            grad_query = grad_query + add_keys(0, start, False)
        grad_query = (grad_query * scale).astype(low)
        for piece in range(block // frames):
            result_ref[start // frames + piece, 0:HEAD_DIM, :] = grad_query[:, piece * frames : (piece + 1) * frames]

    for start in range(0, total, block):
        shared(share, start // query_share, copies, functools.partial(query_block, start))
    for source in range(sources):
        lanes = slice(source * frames, (source + 1) * frames)
        result_ref[source, HEAD_DIM : 2 * HEAD_DIM, :] = (grad_key_s[:, lanes] * scale).astype(low)
        result_ref[source, 2 * HEAD_DIM :, :] = grad_value_s[:, lanes].astype(low)


def attn_bwd(ends, rows, grads, outs, mass, copies):
    sources, _, frames = rows.shape
    total = sources * frames
    return pl.pallas_call(
        functools.partial(backward_kernel, block=max(frames, total // 16), copies=copies),
        out_shape=jax.ShapeDtypeStruct(rows.shape, low),
        in_specs=[pl.BlockSpec(memory_space=pltpu.SMEM)] + [pl.BlockSpec(memory_space=pltpu.VMEM)] * 4,
        out_specs=pl.BlockSpec(memory_space=pltpu.VMEM),
        scratch_shapes=[
            pltpu.VMEM((2 * HEAD_DIM, total), low),
            pltpu.VMEM((total, 2 * HEAD_DIM), low),
            pltpu.VMEM((HEAD_DIM, total), low),
            pltpu.VMEM((total, 2 * HEAD_DIM), low),
            pltpu.VMEM((2 * HEAD_DIM, total), low),
            pltpu.VMEM((HEAD_DIM, total), full),
            pltpu.VMEM((HEAD_DIM, total), full),
        ],
        compiler_params=pltpu.CompilerParams(vmem_limit_bytes=vmem_bytes),
        cost_estimate=pl.CostEstimate(
            flops=35 * total * total * HEAD_DIM, bytes_accessed=8 * rows.size, transcendentals=total * total // 2
        ),
        name="attention_backward",
    )(ends, rows, grads, outs, mass)


def norm_parts(inputs):
    centred = inputs - jnp.mean(inputs, axis=-1, keepdims=True)
    spread = jnp.mean(centred * centred, axis=-1, keepdims=True)
    inverse = lax.rsqrt(spread + eps)
    return centred * inverse, inverse


def norm_back(grad, unit, inverse, gain):
    scaled = grad * gain
    along = jnp.mean(scaled, axis=-1, keepdims=True)
    across = jnp.mean(scaled * unit, axis=-1, keepdims=True)
    return inverse * (scaled - along - unit * across)


def project_kernel(frames_ref, gain_ref, query_ref, key_ref, value_ref, rows_ref, low_ref):
    @pl.when(pl.program_id(0) == 0)
    def _():
        unit, _ = norm_parts(frames_ref[...].astype(full))
        low_ref[...] = (unit * gain_ref[...]).astype(low)

    heads = rows_ref.shape[0]
    for part, weight_ref in enumerate((query_ref, key_ref, value_ref)):
        packed = jnp.dot(low_ref[...], weight_ref[...], preferred_element_type=full).astype(low).T
        for head in range(heads):
            rows_ref[head, part * HEAD_DIM : (part + 1) * HEAD_DIM, :] = packed[
                head * HEAD_DIM : (head + 1) * HEAD_DIM
            ]


def thirds(features, wide):
    count = features // wide
    return [pl.BlockSpec((features, wide), lambda i, part=part: (0, part * count + i)) for part in range(3)]


def project(frames, gain, w_qkv):
    rows, features = frames.shape
    wide = 4 * HEAD_DIM
    return pl.pallas_call(
        project_kernel,
        grid=(features // wide,),
        out_shape=(
            jax.ShapeDtypeStruct((HEADS, 3 * HEAD_DIM, rows), low),
            jax.ShapeDtypeStruct((rows, features), low),
        ),
        in_specs=[
            pl.BlockSpec((rows, features), lambda i: (0, 0)),
            pl.BlockSpec((1, features), lambda i: (0, 0)),
        ]
        + thirds(features, wide),
        out_specs=[
            pl.BlockSpec((4, 3 * HEAD_DIM, rows), lambda i: (i, 0, 0)),
            pl.BlockSpec((rows, features), lambda i: (0, 0)),
        ],
        compiler_params=pltpu.CompilerParams(vmem_limit_bytes=vmem_bytes),
        cost_estimate=pl.CostEstimate(
            flops=6 * rows * features * features, bytes_accessed=8 * features * features, transcendentals=0
        ),
        name="norm_and_project",
    )(frames, gain[None], w_qkv, w_qkv, w_qkv)


def middle_kernel(
    control_ref, frames_ref, att_ref, cot_ref, gain_ref, out_weight_ref, up_ref, down_ref,
    result_ref, grad_middle_ref, branch_ref, branch_away_ref, grad_att_ref, low_two_ref, act_ref,
    grad_hidden_ref, grad_hidden_away_ref,
    unit_s, inverse_s, sum_s, back_s, low_two_s, mixed_s,
):
    step = pl.program_id(0)
    steps = pl.num_programs(0)
    core = control_ref[0]
    valid = control_ref[1]
    rows, features = frames_ref.shape
    root = 0.7978845608028654
    cubic = 0.044715
    across = (((1,), (1,)), ((), ()))
    present = (lax.broadcasted_iota(jnp.int32, (rows, 1), 0) < valid).astype(full)

    def by_core(array, own_ref, away_ref):
        halves = (array[:, : features // 2], array[:, features // 2 :])
        for value in range(2):

            @pl.when(core == value)
            def _():
                own_ref[...] = halves[value]
                away_ref[...] = halves[1 - value]

    @pl.when(step == 0)
    def _():
        middle = frames_ref[...].astype(full) + jnp.dot(
            att_ref[...].T, out_weight_ref[...], preferred_element_type=full
        )
        unit, inverse = norm_parts(middle)
        unit_s[...] = unit
        inverse_s[...] = inverse
        low_two_s[...] = (unit * gain_ref[...]).astype(low)
        low_two_ref[...] = low_two_s[...].T
        mixed_s[...] = (cot_ref[...].astype(full) * present).astype(low)
        sum_s[...] = middle
        back_s[...] = jnp.zeros_like(back_s)

    hidden = jnp.dot(low_two_s[...], up_ref[...], preferred_element_type=full)
    grad_act = lax.dot_general(mixed_s[...], down_ref[...], across, preferred_element_type=full)
    square = hidden * hidden
    bent = jnp.tanh(root * hidden * (1.0 + cubic * square))
    half = 0.5 * (1.0 + bent)
    act = (hidden * half).astype(low)
    slope = half + (0.5 * root) * hidden * (1.0 - bent * bent) * (1.0 + (3.0 * cubic) * square)
    grad_hidden = (slope * grad_act).astype(low)
    turned = act.T
    places, cores, high, piece, _ = act_ref.shape
    for at in range(high * places * cores):
        outer, place, half = at // (places * cores), at // cores % places, at % cores
        act_ref[place, half, outer] = turned[at * piece : (at + 1) * piece]

    @pl.when(step < steps // 2)
    def _():
        grad_hidden_ref[...] = grad_hidden

    @pl.when(step >= steps // 2)
    def _():
        grad_hidden_away_ref[...] = grad_hidden

    sum_s[...] += jnp.dot(act, down_ref[...], preferred_element_type=full)
    back_s[...] += lax.dot_general(grad_hidden, up_ref[...], across, preferred_element_type=full)

    @pl.when(step == steps - 1)
    def _():
        result_ref[...] = (present * sum_s[...]).astype(low)
        grad_middle = mixed_s[...].astype(full) + norm_back(
            back_s[...], unit_s[...], inverse_s[...], gain_ref[...]
        )
        grad_middle_ref[...] = grad_middle
        branch = grad_middle.astype(low)
        by_core(branch, branch_ref, branch_away_ref)
        grad_att = lax.dot_general(out_weight_ref[...], branch, across, preferred_element_type=full)
        lane = (lax.broadcasted_iota(jnp.int32, (1, rows), 1) < valid).astype(full)
        grad_att_ref[...] = (grad_att * lane).astype(low)


def middle_part(core, valid, frames, att, cot, gain, w_out, w_up, w_down):
    rows, features = frames.shape
    hidden = w_up.shape[1]
    wide = 1024
    steps = hidden // wide
    size = lax.axis_size("seq")
    piece = hidden // size
    here = lambda i, s: (i + s[0] * (steps // 2)) % steps
    whole = lambda *shape: pl.BlockSpec(shape, lambda i, s: (0,) * len(shape))
    square = (rows, features)
    turned = (features, rows)
    halved = (rows, features // 2)
    outs = [
        (square, low, None),
        (square, full, None),
        (halved, low, None),
        (halved, low, None),
        (turned, low, None),
        (turned, low, None),
        (
            (4, 2, size // 4, piece // 2, rows),
            low,
            pl.BlockSpec((4, 2, wide // piece // 4, piece // 2, rows), lambda i, s: (0, 0, here(i, s), 0, 0)),
        ),
        ((rows, hidden // 2), low, pl.BlockSpec((rows, wide), lambda i, s: (0, jnp.minimum(i, steps // 2 - 1)))),
        ((rows, hidden // 2), low, pl.BlockSpec((rows, wide), lambda i, s: (0, jnp.maximum(i - steps // 2, 0)))),
    ]
    return pl.pallas_call(
        middle_kernel,
        grid_spec=pltpu.PrefetchScalarGridSpec(
            num_scalar_prefetch=1,
            grid=(steps,),
            in_specs=[
                whole(*square),
                whole(*turned),
                whole(*square),
                whole(1, features),
                whole(features, features),
                pl.BlockSpec((features, wide), lambda i, s: (0, here(i, s))),
                pl.BlockSpec((wide, features), lambda i, s: (here(i, s), 0)),
            ],
            out_specs=[spec or whole(*shape) for shape, _, spec in outs],
            scratch_shapes=[
                pltpu.VMEM(square, full),
                pltpu.VMEM((rows, 1), full),
                pltpu.VMEM(square, full),
                pltpu.VMEM(square, full),
                pltpu.VMEM(square, low),
                pltpu.VMEM(square, low),
            ],
        ),
        out_shape=[jax.ShapeDtypeStruct(shape, kind) for shape, kind, _ in outs],
        compiler_params=pltpu.CompilerParams(vmem_limit_bytes=vmem_bytes),
        cost_estimate=pl.CostEstimate(
            flops=8 * rows * features * hidden + 4 * rows * features * features,
            bytes_accessed=4 * features * hidden + 2 * features * features,
            transcendentals=rows * hidden,
        ),
        name="middle",
    )(jnp.stack([core, valid]), frames, att, cot, gain[None], w_out, w_up, w_down)


def finish_kernel(frames_ref, middle_ref, gain_ref, rows_ref, query_ref, key_ref, value_ref, result_ref, back_s):
    step = pl.program_id(0)
    heads, _, rows = rows_ref.shape

    @pl.when(step == 0)
    def _():
        back_s[...] = jnp.zeros_like(back_s)

    total = back_s[...]
    for part, weight_ref in enumerate((query_ref, key_ref, value_ref)):
        grads = rows_ref[:, part * HEAD_DIM : (part + 1) * HEAD_DIM, :].reshape(heads * HEAD_DIM, rows)
        total = total + jnp.dot(weight_ref[...], grads, preferred_element_type=full)
    back_s[...] = total

    @pl.when(step == pl.num_programs(0) - 1)
    def _():
        unit, inverse = norm_parts(frames_ref[...].astype(full))
        result_ref[...] = middle_ref[...] + norm_back(back_s[...].T, unit, inverse, gain_ref[...])


def finish(frames, grad_middle, gain, grad_rows, w_qkv):
    rows, features = frames.shape
    wide = 4 * HEAD_DIM
    whole = lambda *shape: pl.BlockSpec(shape, lambda i: (0,) * len(shape))
    return pl.pallas_call(
        finish_kernel,
        grid=(features // wide,),
        out_shape=jax.ShapeDtypeStruct((rows, features), full),
        in_specs=[
            whole(rows, features),
            whole(rows, features),
            whole(1, features),
            pl.BlockSpec((4, 3 * HEAD_DIM, rows), lambda i: (i, 0, 0)),
        ]
        + thirds(features, wide),
        out_specs=whole(rows, features),
        scratch_shapes=[pltpu.VMEM((features, rows), full)],
        compiler_params=pltpu.CompilerParams(vmem_limit_bytes=vmem_bytes),
        cost_estimate=pl.CostEstimate(
            flops=6 * rows * features * features, bytes_accessed=8 * features * features, transcendentals=0
        ),
        name="input_gradient",
    )(frames, grad_middle, gain[None], grad_rows, w_qkv, w_qkv, w_qkv)


def terms_kernel(pick_ref, *refs, groups, needs, sets, came_sets):
    step = pl.program_id(0)
    refs = list(refs)
    take = lambda count: [refs.pop(0) for _ in range(count)]
    lefts = [{kind: take(2) for kind in kinds} for kinds in needs]
    rights = [take(2) for _ in range(2)]
    came = take(len(came_sets))
    places = {}
    for came_ref, members in zip(came, came_sets):
        at = 0
        for group in members:
            places[group] = (came_ref, at)
            at += sum(stop - start for _, start, stop in groups[group][3])

    def write(outs):
        for out_ref, members in zip(outs, sets):
            at = 0
            for group in members:
                inner = 0
                for kind, start, stop in groups[group][3]:
                    own_ref, other_ref = lefts[group][kind]
                    rows, frames = own_ref.shape[-2:]
                    left = jnp.concatenate([ref[...].reshape(-1, frames) for ref in (own_ref, other_ref)], axis=1)
                    right = jnp.concatenate([ref[:, start:stop] for ref in rights[kind]], axis=0)
                    terms = jnp.dot(left, right, preferred_element_type=full).reshape(-1, rows, stop - start)
                    if came:
                        came_ref, first = places[group]
                        first += inner
                        terms = terms + came_ref[:, :, first : first + stop - start].astype(full)
                    out_ref[:, :, at : at + stop - start] = terms.astype(low)
                    at += stop - start
                    inner += stop - start

    if not came:
        write(refs)
    else:
        pl.when(step == 0)(functools.partial(write, refs[: len(sets)]))
        pl.when(step == 1)(functools.partial(write, refs[len(sets) :]))


def terms_by_piece(groups, sets, bits, two, att, hidden, branch, came=(), came_sets=()):
    size = lax.axis_size("seq")
    features, frames = two[0].shape
    rows = features // size
    quarter = size // 4
    width_of = lambda members: sum(stop - start for group in members for _, start, stop in groups[group][3])
    needs = [sorted({kind for kind, _, _ in parts}) for *_, parts in groups]
    lefts, specs = [], []
    for (first, after, _, _), kinds in zip(groups, needs):
        upper, lower = max(first, after), min(first, after)
        cut = (size >> (upper + 1), 2, 1 << (upper - lower - 1), 2, 1 << lower)

        def index(i, s, first=first, after=after, upper=upper):
            value = s[first] if came else 1 - s[first]
            beyond = s[after] ^ (1 - i)
            outer, inner = (value, beyond) if upper == first else (beyond, value)
            return (0, outer, 0, inner, 0, 0, 0)

        for kind in kinds:
            lefts += [a.reshape(cut + (rows, frames)) for a in (two, att)[kind]]
            specs += [pl.BlockSpec((cut[0], 1, cut[2], 1, cut[4], rows, frames), index)] * 2
    rights = (*hidden, *branch)
    specs += [pl.BlockSpec(a.shape, lambda i, s: (0, 0)) for a in rights]
    half = lambda members: pl.BlockSpec((None, quarter, rows, width_of(members)), lambda i, s: (i, 0, 0, 0))
    specs += [half(members) for members in came_sets]
    shapes = [(quarter, rows, width_of(members)) for members in sets]
    if came:
        shapes = shapes * 2
        outs = [pl.BlockSpec(shape, lambda i, s: (0, 0, 0)) for shape in shapes]
    else:
        outs = [half(members) for members in sets]
        shapes = [(2,) + shape for shape in shapes]
    return pl.pallas_call(
        functools.partial(terms_kernel, groups=groups, needs=needs, sets=sets, came_sets=came_sets),
        grid_spec=pltpu.PrefetchScalarGridSpec(num_scalar_prefetch=1, grid=(2,), in_specs=specs, out_specs=outs),
        out_shape=[jax.ShapeDtypeStruct(shape, low) for shape in shapes],
        compiler_params=pltpu.CompilerParams(vmem_limit_bytes=vmem_bytes),
        cost_estimate=pl.CostEstimate(
            flops=2 * frames * features * 5 * features // 2, bytes_accessed=5 * features * features, transcendentals=0
        ),
        name="terms_by_piece",
    )(jnp.stack(bits), *lefts, *rights, *came)


def tall_terms_kernel(pick_ref, *refs):
    step = pl.program_id(0)
    acts, mixed, outs = refs[:8], refs[8:16], refs[16:]
    high, rows, frames = acts[0].shape

    def write(out_ref):
        total = None
        for act_ref, mixed_ref in zip(acts, mixed):
            terms = jnp.dot(act_ref[...].reshape(high * rows, frames), mixed_ref[...], preferred_element_type=full)
            total = terms if total is None else total + terms
        out_ref[...] = total.astype(low).reshape(out_ref.shape)

    for value in range(2):
        pl.when(step == value)(functools.partial(write, outs[value]))


def tall_terms(core, place, bit, act_own, act_other, mixed_own, mixed_other):
    count, _, high, rows, frames = act_own.shape
    features = mixed_own[0].shape[-1]
    half = high // 2
    cut = lambda a: a.reshape(a.shape[:-3] + (half, 2, rows, frames))
    own = lambda other: pl.BlockSpec(
        (None, None, half, None, rows, frames), lambda i, s: (s[1] ^ other, s[0], 0, s[2] ^ (1 - i), 0, 0)
    )
    away = lambda other: pl.BlockSpec(
        (None, half, None, rows, frames), lambda i, s: (s[1] ^ other, 0, s[2] ^ (1 - i), 0, 0)
    )
    whole = lambda *shape: pl.BlockSpec(shape, lambda i, s: (0,) * len(shape))
    return pl.pallas_call(
        tall_terms_kernel,
        grid_spec=pltpu.PrefetchScalarGridSpec(
            num_scalar_prefetch=1,
            grid=(2,),
            in_specs=[own(other) for other in range(4)]
            + [away(other) for other in range(4)]
            + [whole(frames, features)] * 8,
            out_specs=[whole(half, rows, features)] * 2,
        ),
        out_shape=[jax.ShapeDtypeStruct((half, rows, features), low)] * 2,
        compiler_params=pltpu.CompilerParams(vmem_limit_bytes=vmem_bytes),
        cost_estimate=pl.CostEstimate(
            flops=4 * count * frames * high * rows * features, bytes_accessed=16 * frames * features, transcendentals=0
        ),
        name="tall_terms",
    )(jnp.stack([core, place, bit]), *[cut(act_own)] * 4, *[cut(act_other)] * 4, *mixed_own, *mixed_other)


def add_split_kernel(pick_ref, *refs, sets, spans):
    step = pl.program_id(0)
    terms, outs = refs[: 2 * len(spans)], refs[2 * len(spans) :]

    def write(outs):
        for out_ref, members in zip(outs, sets):
            at = 0
            for group in members:
                first, second = [ref[:, :, :, spans[group]] for ref in terms[2 * group : 2 * group + 2]]
                width = first.shape[-1]
                out_ref[:, :, :, at : at + width] = (first.astype(full) + second.astype(full)).astype(low)
                at += width

    pl.when(step == 0)(functools.partial(write, outs[: len(sets)]))
    pl.when(step == 1)(functools.partial(write, outs[len(sets) :]))


def add_split(pairs, old_sets, sets, widths, outer, inner, mine):
    rows = pairs[0][0].shape[-2]
    arrays, specs, spans = [], [], []
    for group in range(len(widths)):
        ((which, members),) = [(which, members) for which, members in enumerate(old_sets) if group in members]
        at = sum(widths[other] for other in members[: members.index(group)])
        spans.append(slice(at, at + widths[group]))
        index = lambda i, s, group=group: (0, s[group] ^ (1 - i), 0, 0, 0)
        columns = pairs[which][0].shape[-1]
        arrays += [a.reshape(outer, 2, inner, rows, columns) for a in pairs[which]]
        specs += [pl.BlockSpec((outer, None, inner, rows, columns), index)] * 2
    shapes = [(outer, inner, rows, sum(widths[group] for group in members)) for members in sets]
    sums = pl.pallas_call(
        functools.partial(add_split_kernel, sets=sets, spans=spans),
        grid_spec=pltpu.PrefetchScalarGridSpec(
            num_scalar_prefetch=1,
            grid=(2,),
            in_specs=specs,
            out_specs=[pl.BlockSpec(shape, lambda i, s: (0, 0, 0, 0)) for shape in shapes * 2],
        ),
        out_shape=[jax.ShapeDtypeStruct(shape, low) for shape in shapes * 2],
        compiler_params=pltpu.CompilerParams(vmem_limit_bytes=vmem_bytes),
        name="add_split",
    )(jnp.stack(mine), *arrays)
    sums = [a.reshape((outer * inner,) + a.shape[2:]) for a in sums]
    return sums[: len(sets)], sums[len(sets) :]


def plane_terms_kernel(pick_ref, *refs):
    rows, lows, (keep_ref, send_ref, turn_s) = refs[:4], refs[4:8], refs[8:]
    core = pick_ref[0]
    lines, columns, frames = rows[0].shape
    total = None
    for rows_ref, low_ref in zip(rows, lows):
        terms = jnp.dot(rows_ref[...].reshape(lines * columns, frames), low_ref[...], preferred_element_type=full)
        total = terms if total is None else total + terms
    turn_s[...] = total.T.reshape(turn_s.shape)
    keep_ref[...] = turn_s[:, :, core].reshape(keep_ref.shape)
    send_ref[...] = turn_s[:, :, 1 - core].astype(low).reshape(send_ref.shape)


def plane_terms(core, place, line_rows, lows):
    lines, count, columns, frames = line_rows.shape
    features = lows[0].shape[-1]
    rows = features // lines // count // 2
    shape = (lines, count * rows, lines * columns)
    whole = pl.BlockSpec(shape, lambda i, s: (0, 0, 0))
    source = lambda other: pl.BlockSpec((lines, None, columns, frames), lambda i, s: (0, s[1] ^ other, 0, 0))
    return pl.pallas_call(
        plane_terms_kernel,
        grid_spec=pltpu.PrefetchScalarGridSpec(
            num_scalar_prefetch=1,
            grid=(1,),
            in_specs=[source(other) for other in range(4)]
            + [pl.BlockSpec((frames, features), lambda i, s: (0, 0))] * 4,
            out_specs=[whole, whole],
            scratch_shapes=[pltpu.VMEM((lines, count, 2, rows, lines * columns), full)],
        ),
        out_shape=(jax.ShapeDtypeStruct(shape, full), jax.ShapeDtypeStruct(shape, low)),
        compiler_params=pltpu.CompilerParams(vmem_limit_bytes=vmem_bytes),
        cost_estimate=pl.CostEstimate(
            flops=2 * lines * count * columns * frames * features, bytes_accessed=8 * line_rows.size, transcendentals=0
        ),
        name="plane_terms",
    )(jnp.stack([core, place]), *[line_rows] * 4, *lows)


def gain_sum(weights, grads, gain):
    total = jnp.sum(weights.astype(full) * grads, axis=1, keepdims=True)
    return jnp.broadcast_to(total, (total.shape[0], 128)).T[0:1] / gain


def wide_output_kernel(pick_ref, halves_ref, weight_ref, gain_ref, up_ref, out_ref, sum_ref):
    split, half = up_ref.shape[1] // 2, out_ref.shape[1] // 2
    for side in range(2):
        up_ref[:, side * split : (side + 1) * split] = halves_ref[side, :, 0:split].astype(full)
        out_ref[:, side * half : (side + 1) * half] = halves_ref[side, :, split : split + half].astype(full)
    sum_ref[...] = gain_sum(weight_ref[...], up_ref[...], gain_ref[...])


def tall_output_kernel(pick_ref, halves_ref, weight_ref, gain_ref, qkv_ref, sum_ref):
    rows = qkv_ref.shape[0] // 2
    for side in range(2):
        qkv_ref[side * rows : (side + 1) * rows, :] = halves_ref[side].astype(full)
    sum_ref[...] = gain_sum(weight_ref[...], qkv_ref[...], gain_ref[...])


def write_outputs(kernel, halves, weight, gain, shapes, name):
    size = lax.axis_size("seq")
    rows = weight.shape[0] // size
    whole = lambda *shape: pl.BlockSpec(shape, lambda i, s: (0,) * len(shape))
    shapes = [*shapes, (1, rows)]
    return pl.pallas_call(
        kernel,
        grid_spec=pltpu.PrefetchScalarGridSpec(
            num_scalar_prefetch=1,
            grid=(1,),
            in_specs=[
                whole(*halves.shape),
                pl.BlockSpec((rows, weight.shape[1]), lambda i, s: (s[0], 0)),
                pl.BlockSpec((None, 1, rows), lambda i, s: (s[0], 0, 0)),
            ],
            out_specs=[whole(*shape) for shape in shapes],
        ),
        out_shape=[jax.ShapeDtypeStruct(shape, full) for shape in shapes],
        compiler_params=pltpu.CompilerParams(vmem_limit_bytes=vmem_bytes),
        name=name,
    )(lax.axis_index("seq")[None], halves, weight, gain.reshape(size, 1, rows))


def other_core(array):
    count = lax.axis_size("items")
    return lax.ppermute(array, "items", [(i, i ^ 1) for i in range(count)])


def to_heads(array):
    copies = lax.axis_size("seq") // HEADS
    if copies > 1:
        array = jnp.repeat(array, copies, axis=0)
    return lax.all_to_all(array, "seq", 0, 0, tiled=True)


def by_head(array, axis):
    copies = array.shape[axis] // HEADS
    if copies == 1:
        return array
    shape = array.shape[:axis] + (HEADS, copies) + array.shape[axis + 1 :]
    return jnp.sum(array.reshape(shape).astype(full), axis=axis + 1).astype(low)


def pick(array, index, axis):
    return lax.dynamic_index_in_dim(array, index, axis, keepdims=False)


def swapped(array, bits):
    return lax.ppermute(array, "seq", [(i, i ^ bits) for i in range(lax.axis_size("seq"))])


def flipped(array, bit):
    return swapped(array, 1 << bit)


def split_terms(terms, bit, left):
    axis = left.index(bit)
    mine = (lax.axis_index("seq") >> bit) & 1
    terms = [a.reshape((2,) * len(left) + a.shape[-2:]) for a in terms]

    def part(value):
        chosen = [pick(a, value, axis) for a in terms]
        return chosen[0] if len(chosen) == 1 else (chosen[0].astype(full) + chosen[1].astype(full)).astype(low)

    left.remove(bit)
    return part(1 - mine), part(mine)


def together(first, second):
    return (first.astype(full) + second.astype(full)).astype(low)


def over_items(piece):
    count = lax.axis_size("items")
    if count == 2:
        other = other_core(piece)
        first = lax.axis_index("items") == 0
        return jnp.stack([jnp.where(first, piece, other), jnp.where(first, other, piece)])
    pieces = lax.all_gather(piece, "items", axis=0)
    return jnp.sum(pieces.reshape((count // 2, 2) + piece.shape).astype(full), axis=0)


def on_device(frames, lengths, w_qkv, w_out, w_up, w_down, gain_one, gain_two, cotangent):
    row_count, features = frames.shape[1:]
    hidden_count = w_up.shape[1]
    size = lax.axis_size("seq")
    depth = size.bit_length() - 1
    me = lax.axis_index("seq")
    core = lax.axis_index("items") % 2
    copies = size // HEADS
    ends = jnp.cumsum(lengths[0]).astype(jnp.int32)
    valid = jnp.clip(ends[-1] - me * row_count, 0, row_count)
    control = jnp.concatenate([ends, (me % copies)[None]])
    rows_out = features // size

    lines = size // 4
    fours = [list(range(at, at + 4)) for at in range(0, size, 4)]
    columns = [list(range(at, size, 4)) for at in range(4)]
    across = lambda array, groups: lax.all_to_all(array, "seq", 0, 0, tiled=True, axis_index_groups=groups)
    bits = [(me >> bit) & 1 for bit in range(depth)]

    head_parts, low_one = project(frames[0], gain_one, w_qkv)
    head_rows = to_heads(head_parts)
    mixed = cotangent[0] * (jnp.arange(row_count) < valid).astype(low)[:, None]
    mixed_x, mixed_y = flipped(mixed, 0), flipped(mixed, 1)
    head_rows, low_one, mixed_x, mixed_y = lax.optimization_barrier((head_rows, low_one, mixed_x, mixed_y))
    low_x, mixed_xy = flipped(low_one, 0), flipped(mixed_x, 1)
    head_out, log_mass = attn_fwd(control, head_rows, copies)
    head_out, low_x, mixed_xy = lax.optimization_barrier((head_out, low_x, mixed_xy))
    mixed_own = (mixed, mixed_x, mixed_y, mixed_xy)
    moved = lax.all_to_all(head_out, "seq", 0, 0, tiled=True)
    attended = by_head(moved, 0).reshape(features, row_count)
    attended, low_one, low_x = lax.optimization_barrier((attended, low_one, low_x))
    lows = (low_one, low_x, flipped(low_one, 1), flipped(low_x, 1))
    att = (attended, other_core(attended))

    result, grad_middle, branch, branch_away, grad_attended, two, act, hidden, hidden_away = middle_part(
        core, valid, frames[0], attended, cotangent[0], gain_two, w_out, w_up, w_down
    )
    grad_attended, two, act, hidden, hidden_away, branch, branch_away, lows = lax.optimization_barrier(
        (grad_attended, two, act, hidden, hidden_away, branch, branch_away, lows)
    )
    grad_heads = to_heads(grad_attended.reshape(HEADS, HEAD_DIM, row_count))
    acts = across(act, fours)

    pairs = (
        (two, other_core(two)),
        att,
        (hidden, other_core(hidden_away)),
        (branch, other_core(branch_away)),
    )
    half = features // 2
    split = hidden_count // 2
    groups = (
        (0, 1, 2, ((0, 0, half),)),
        (1, 0, 2, ((0, half, 2 * half),)),
        (2, 0, 1, ((0, 2 * half, 7 * half // 2),)),
        (2, 1, 0, ((0, 7 * half // 2, split), (1, 0, half))),
    )
    widths = [sum(stop - start for _, start, stop in parts) for *_, parts in groups]
    sets = [((0,), (1,), (2, 3)), ((0, 3), (1, 2)), ((0, 1), (2,), (3,)), ((0, 1, 2, 3),)]
    travel = lambda arrays, turn: [flipped(a, groups[members[0]][turn]) for a, members in zip(arrays, sets[turn])]
    away = list(terms_by_piece(groups, sets[0], bits[:3], *pairs))
    grad_heads, away[0] = lax.optimization_barrier((grad_heads, away[0]))
    came = travel(away, 0)
    mixed_other = [other_core(a) for a in mixed_own]
    grad_heads, mixed_other = lax.optimization_barrier((grad_heads, mixed_other))

    grad_rows = attn_bwd(control, head_rows, grad_heads, head_out, log_mass, copies)
    grad_rows, acts, *came = lax.optimization_barrier((grad_rows, acts, *came))
    line_rows = across(grad_rows.reshape(lines, 4, 3 * HEAD_DIM, row_count), columns)

    halves = terms_by_piece(groups, sets[1], bits[:3], *pairs, came, sets[0])
    sends, keeps = halves[:2], halves[2:]
    acts, *sends = lax.optimization_barrier((acts, *sends))
    came = travel(sends, 1)
    acts_other = other_core(pick(acts, 1 - core, 1))
    tall_send, tall_keep = tall_terms(core, me % 4, bits[2], acts, acts_other, mixed_own, mixed_other)
    tall_came = flipped(tall_send, 2)
    tall_keep, *came = lax.optimization_barrier((tall_keep, *came))

    sends, keeps = add_split(list(zip(keeps, came)), sets[1], sets[2], widths, lines // 2, 1, [bits[group[2]] for group in groups])
    line_rows, *sends = lax.optimization_barrier((line_rows, *sends))
    came = travel(sends, 2)
    turned = line_rows.transpose(1, 0, 2, 3)
    line_rows, turned = lax.optimization_barrier((line_rows, turned))
    grad_packed = across(turned, fours)
    keep, send = plane_terms(core, me % 4, line_rows, lows)
    keep, send, tall_came, *came = lax.optimization_barrier((keep, send, tall_came, *came))
    both = (keep + other_core(send).astype(full)).astype(low)
    line_left = list(range(depth - 1, 1, -1))
    send, line_keep = split_terms((both,), 2, line_left)
    line_came = flipped(send, 2)
    line_keep, tall_came, *came = lax.optimization_barrier((line_keep, tall_came, *came))
    (wide_send,), (wide_keep,) = add_split(list(zip(keeps, came)), sets[2], sets[3], widths, lines // 4, 1, [bits[3]] * 4)
    tall_left = list(range(depth - 1, 2, -1))
    tall_send, tall_keep = split_terms((tall_keep, tall_came), 3, tall_left)
    wide_terms, wide_left = (wide_keep, flipped(wide_send, 3)), list(range(depth - 1, 3, -1))
    tall_rest = (tall_keep, flipped(tall_send, 3))
    for bit in range(4, depth):
        more, rest = split_terms(wide_terms, bit, wide_left)
        wide_terms = (rest, flipped(more, bit))
        more, rest = split_terms(tall_rest, bit, tall_left)
        tall_rest = (rest, flipped(more, bit))
    line_came, tall_came = lax.optimization_barrier((line_came, tall_rest[1]))
    tall_rest = (tall_rest[0], tall_came)
    line_terms = (line_keep, line_came)
    for bit in range(3, depth):
        send, keep = split_terms(line_terms, bit, line_left)
        grad_packed, send = lax.optimization_barrier((grad_packed, send))
        line_terms = (keep, flipped(send, bit))
    grad_packed = by_head(grad_packed.transpose(1, 0, 2, 3).reshape(size, 3 * HEAD_DIM, row_count), 0)
    grad_inputs = finish(frames[0], grad_middle, gain_one, grad_packed, w_qkv)
    line_came, wide_came, grad_inputs = lax.optimization_barrier((line_terms[1], wide_terms[1], grad_inputs))
    pieces = together(line_terms[0], line_came).reshape(4, rows_out // 2, lines * 3 * HEAD_DIM)
    pieces = across(pieces, fours)

    sums = over_items(together(wide_terms[0], wide_came).reshape(rows_out, split + half))
    up, out, sum_gain_two = write_outputs(
        wide_output_kernel, sums, w_up, gain_two, [(rows_out, hidden_count), (rows_out, features)], "wide_outputs"
    )
    down = over_items(together(tall_rest[0], tall_came).reshape(-1, features)).astype(full)
    down = down.reshape(hidden_count // size, features)
    pieces, up, out, down, sum_gain_two = lax.optimization_barrier((pieces, up, out, down, sum_gain_two))
    pieces = pieces.reshape(4, rows_out // 2, lines, 3, HEAD_DIM).transpose(1, 3, 2, 0, 4)
    pieces = by_head(pieces.reshape(rows_out // 2, 3, size, HEAD_DIM), 2)
    pieces = over_items(pieces.reshape(rows_out // 2, 3 * features))
    qkv, sum_gain_one = write_outputs(
        tall_output_kernel, pieces, w_qkv, gain_one, [(rows_out, 3 * features)], "tall_outputs"
    )
    return (result[None], grad_inputs[None], qkv, out, up, down, sum_gain_one[0], sum_gain_two[0])


def solution(mesh):
    return jax.shard_map(
        on_device,
        mesh=mesh,
        in_specs=(
            P("items", "seq", None),
            P("items", None),
            P(),
            P(),
            P(),
            P(),
            P(),
            P(),
            P("items", "seq", None),
        ),
        out_specs=(
            P("items", "seq", None),
            P("items", "seq", None),
            P("seq", None),
            P("seq", None),
            P("seq", None),
            P("seq", None),
            P("seq"),
            P("seq"),
        ),
        check_vma=False,
    )
```

```python
import functools

import jax
import jax.numpy as jnp
from jax import lax
from jax.experimental import pallas as pl
from jax.experimental.pallas import tpu as pltpu
from jax.sharding import PartitionSpec as P

HEADS = 16
HEAD_DIM = 64
eps = 1e-05
masked = -1e30
log2e = 1.4426950408889634
query_share = 1024
vmem_bytes = 56 * 2**20
low = jnp.bfloat16
full = jnp.float32


def lane_labels(ends_ref, utterances, start, rows, count):
    place = start + lax.broadcasted_iota(jnp.int32, (rows, count), 1)
    label = jnp.zeros((rows, count), jnp.int32)
    for u in range(utterances):
        label = label + (place >= ends_ref[u]).astype(jnp.int32)
    return label


def stage_scores(ends_ref, rows_ref, source, utterances, query_s, key_s, mass=None):
    frames = rows_ref.shape[2]
    label = lane_labels(ends_ref, utterances, source * frames, HEAD_DIM, frames)
    row = lax.broadcasted_iota(jnp.int32, (HEAD_DIM, frames), 0)
    own = jnp.where(row == label, 1.0, 0.0)
    barred = jnp.where((row != label) & (row <= utterances), masked, 0.0)
    if mass is not None:
        first = mass.astype(low).astype(full)
        second = (mass - first).astype(low).astype(full)
        for at, term in enumerate((first, second, mass - first - second)):
            own = jnp.where(row == utterances + 1 + at, -term, own)
        barred = jnp.where((row > utterances) & (row <= utterances + 3), 1.0, barred)
    span = pl.ds(source * frames, frames)
    query = rows_ref[source, 0:HEAD_DIM, :]
    query_s[0:HEAD_DIM, span] = query
    query_s[HEAD_DIM : 2 * HEAD_DIM, span] = query
    query_s[2 * HEAD_DIM : 3 * HEAD_DIM, span] = own.astype(low)
    query_s[3 * HEAD_DIM :, span] = jnp.zeros((HEAD_DIM, frames), low)
    key = rows_ref[source, HEAD_DIM : 2 * HEAD_DIM, :].astype(full) * (HEAD_DIM**-0.5 * log2e)
    main = key.astype(low)
    rest = (key - main.astype(full)).astype(low)
    key_s[span, 0 : 2 * HEAD_DIM] = jnp.concatenate([main, rest], axis=0).T
    key_s[span, 2 * HEAD_DIM :] = jnp.concatenate([barred.astype(low), jnp.zeros((HEAD_DIM, frames), low)], axis=0).T


def causal(scores):
    key_place = lax.broadcasted_iota(jnp.int32, scores.shape, 0)
    query_place = lax.broadcasted_iota(jnp.int32, scores.shape, 1)
    return jnp.where(key_place <= query_place, scores, masked)


def forward_kernel(ends_ref, rows_ref, out_ref, mass_ref, query_s, key_s, value_s, *, block, part, copies):
    sources, _, frames = rows_ref.shape
    utterances = ends_ref.shape[0] - 1
    share = ends_ref[utterances]
    total = sources * frames
    for source in range(sources):
        stage_scores(ends_ref, rows_ref, source, utterances, query_s, key_s)
        span = pl.ds(source * frames, frames)
        value_s[0:HEAD_DIM, span] = rows_ref[source, 2 * HEAD_DIM :, :]
        row = lax.broadcasted_iota(jnp.int32, (value_s.shape[0] - HEAD_DIM, frames), 0)
        value_s[HEAD_DIM:, span] = jnp.where(row == 0, 1.0, 0.0).astype(low)
    if copies > 1:
        out_ref[...] = jnp.zeros_like(out_ref)
        mass_ref[...] = jnp.zeros_like(mass_ref)

    def add_keys(current, query, start, stop, diagonal):
        scores = jnp.dot(key_s[start:stop, :], query, preferred_element_type=full)
        if diagonal:
            scores = causal(scores)
        new_peak = jnp.max(scores, axis=0, keepdims=True)
        if current is not None:
            new_peak = jnp.maximum(current[0], new_peak)
        weights = jnp.exp2(scores - new_peak)
        sums = jnp.dot(value_s[:, start:stop], weights.astype(low), preferred_element_type=full)
        if current is not None:
            sums = sums + current[1] * jnp.exp2(current[0] - new_peak)
        return new_peak, sums

    def query_block(start):
        query = query_s[:, start : start + block]
        whole = add_keys(None, query, 0, start, False) if start else None
        for at in range(0, block, part):
            lanes = slice(at, at + part)
            current = None if whole is None else (whole[0][:, lanes], whole[1][:, lanes])
            if at:
                current = add_keys(current, query[:, lanes], start, start + at, False)
            peak, sums = add_keys(current, query[:, lanes], start + at, start + at + part, True)
            mass = sums[HEAD_DIM : HEAD_DIM + 1]
            label = lane_labels(ends_ref, utterances, start + at, 1, part)
            out = (sums[0:HEAD_DIM] * jnp.where(label < utterances, 1.0 / mass, 0.0)).astype(low)
            mass_ref[:, start + at : start + at + part] = peak + jnp.log2(mass)
            for piece in range(part // frames):
                out_ref[(start + at) // frames + piece] = out[:, piece * frames : (piece + 1) * frames]

    for start in range(0, total, block):
        shared(share, start // query_share, copies, functools.partial(query_block, start))


def shared(share, turn, copies, work):
    if copies == 1:
        work()
    else:
        pl.when(share == turn % copies)(work)


def attn_fwd(ends, rows, copies):
    sources, _, frames = rows.shape
    total = sources * frames
    return pl.pallas_call(
        functools.partial(forward_kernel, block=query_share, part=query_share, copies=copies),
        out_shape=(
            jax.ShapeDtypeStruct((sources, HEAD_DIM, frames), low),
            jax.ShapeDtypeStruct((1, total), full),
        ),
        in_specs=[pl.BlockSpec(memory_space=pltpu.SMEM), pl.BlockSpec(memory_space=pltpu.VMEM)],
        out_specs=[pl.BlockSpec(memory_space=pltpu.VMEM)] * 2,
        scratch_shapes=[
            pltpu.VMEM((4 * HEAD_DIM, total), low),
            pltpu.VMEM((total, 4 * HEAD_DIM), low),
            pltpu.VMEM((HEAD_DIM + 16, total), low),
        ],
        compiler_params=pltpu.CompilerParams(vmem_limit_bytes=vmem_bytes),
        cost_estimate=pl.CostEstimate(
            flops=20 * total * total * HEAD_DIM, bytes_accessed=4 * rows.size, transcendentals=total * total // 2
        ),
        name="attention_forward",
    )(ends, rows)


def backward_kernel(
    ends_ref, rows_ref, grad_ref, out_ref, mass_ref, result_ref,
    query_s, key_s, keyt_s, value_s, grad_s, grad_key_s, grad_value_s, *, block, copies
):
    sources, _, frames = rows_ref.shape
    utterances = ends_ref.shape[0] - 1
    share = ends_ref[utterances]
    scale = HEAD_DIM**-0.5
    total = sources * frames
    row = lax.broadcasted_iota(jnp.int32, (HEAD_DIM, frames), 0)
    for source in range(sources):
        span = pl.ds(source * frames, frames)
        stage_scores(ends_ref, rows_ref, source, utterances, query_s, key_s, mass_ref[:, span])
        keyt_s[:, span] = rows_ref[source, HEAD_DIM : 2 * HEAD_DIM, :]
        grad = grad_ref[source]
        delta = jnp.sum(grad.astype(full) * out_ref[source].astype(full), axis=0, keepdims=True)
        first = delta.astype(low).astype(full)
        second = (delta - first).astype(low).astype(full)
        third = delta - first - second
        more = jnp.where(row == 0, -first, jnp.where(row == 1, -second, jnp.where(row == 2, -third, 0.0)))
        grad_s[0:HEAD_DIM, span] = grad
        grad_s[HEAD_DIM:, span] = more.astype(low)
        ones = jnp.where(row < 3, 1.0, 0.0).astype(low)
        value_s[span, :] = jnp.concatenate([rows_ref[source, 2 * HEAD_DIM :, :], ones], axis=0).T
    across = (((1,), (1,)), ((), ()))
    if copies > 1:
        grad_key_s[...] = jnp.zeros_like(grad_key_s)
        grad_value_s[...] = jnp.zeros_like(grad_value_s)
        result_ref[:, 0:HEAD_DIM, :] = jnp.zeros((sources, HEAD_DIM, frames), low)

    def query_block(start):
        span = slice(start, start + block)

        def add_keys(first, last, diagonal):
            keys = slice(first, last)
            scores = jnp.dot(key_s[keys, :], query_s[:, span], preferred_element_type=full)
            if diagonal:
                scores = causal(scores)
            probs = jnp.exp2(scores)
            shifted = jnp.dot(value_s[keys, :], grad_s[:, span], preferred_element_type=full)
            grad_scores = (probs * shifted).astype(low)
            grad_value = lax.dot_general(
                grad_s[0:HEAD_DIM, span], probs.astype(low), across, preferred_element_type=full
            )
            grad_key = lax.dot_general(query_s[0:HEAD_DIM, span], grad_scores, across, preferred_element_type=full)
            if diagonal and copies == 1:
                grad_value_s[:, keys] = grad_value
                grad_key_s[:, keys] = grad_key
            else:
                grad_value_s[:, keys] += grad_value
                grad_key_s[:, keys] += grad_key
            return jnp.dot(keyt_s[:, keys], grad_scores, preferred_element_type=full)

        grad_query = add_keys(start, start + block, True)
        if start:
            grad_query = grad_query + add_keys(0, start, False)
        grad_query = (grad_query * scale).astype(low)
        for piece in range(block // frames):
            result_ref[start // frames + piece, 0:HEAD_DIM, :] = grad_query[:, piece * frames : (piece + 1) * frames]

    for start in range(0, total, block):
        shared(share, start // query_share, copies, functools.partial(query_block, start))
    for source in range(sources):
        lanes = slice(source * frames, (source + 1) * frames)
        result_ref[source, HEAD_DIM : 2 * HEAD_DIM, :] = (grad_key_s[:, lanes] * scale).astype(low)
        result_ref[source, 2 * HEAD_DIM :, :] = grad_value_s[:, lanes].astype(low)


def attn_bwd(ends, rows, grads, outs, mass, copies):
    sources, _, frames = rows.shape
    total = sources * frames
    return pl.pallas_call(
        functools.partial(backward_kernel, block=max(frames, total // 16), copies=copies),
        out_shape=jax.ShapeDtypeStruct(rows.shape, low),
        in_specs=[pl.BlockSpec(memory_space=pltpu.SMEM)] + [pl.BlockSpec(memory_space=pltpu.VMEM)] * 4,
        out_specs=pl.BlockSpec(memory_space=pltpu.VMEM),
        scratch_shapes=[
            pltpu.VMEM((4 * HEAD_DIM, total), low),
            pltpu.VMEM((total, 4 * HEAD_DIM), low),
            pltpu.VMEM((HEAD_DIM, total), low),
            pltpu.VMEM((total, 2 * HEAD_DIM), low),
            pltpu.VMEM((2 * HEAD_DIM, total), low),
            pltpu.VMEM((HEAD_DIM, total), full),
            pltpu.VMEM((HEAD_DIM, total), full),
        ],
        compiler_params=pltpu.CompilerParams(vmem_limit_bytes=vmem_bytes),
        cost_estimate=pl.CostEstimate(
            flops=35 * total * total * HEAD_DIM, bytes_accessed=8 * rows.size, transcendentals=total * total // 2
        ),
        name="attention_backward",
    )(ends, rows, grads, outs, mass)


def norm_parts(inputs):
    centred = inputs - jnp.mean(inputs, axis=-1, keepdims=True)
    spread = jnp.mean(centred * centred, axis=-1, keepdims=True)
    inverse = lax.rsqrt(spread + eps)
    return centred * inverse, inverse


def norm_back(grad, unit, inverse, gain):
    scaled = grad * gain
    along = jnp.mean(scaled, axis=-1, keepdims=True)
    across = jnp.mean(scaled * unit, axis=-1, keepdims=True)
    return inverse * (scaled - along - unit * across)


def project_kernel(frames_ref, gain_ref, query_ref, key_ref, value_ref, rows_ref, low_ref):
    @pl.when(pl.program_id(0) == 0)
    def _():
        unit, _ = norm_parts(frames_ref[...].astype(full))
        low_ref[...] = (unit * gain_ref[...]).astype(low)

    heads = rows_ref.shape[0]
    for part, weight_ref in enumerate((query_ref, key_ref, value_ref)):
        packed = jnp.dot(low_ref[...], weight_ref[...], preferred_element_type=full).astype(low).T
        for head in range(heads):
            rows_ref[head, part * HEAD_DIM : (part + 1) * HEAD_DIM, :] = packed[
                head * HEAD_DIM : (head + 1) * HEAD_DIM
            ]


def thirds(features, wide):
    count = features // wide
    return [pl.BlockSpec((features, wide), lambda i, part=part: (0, part * count + i)) for part in range(3)]


def project(frames, gain, w_qkv):
    rows, features = frames.shape
    wide = 4 * HEAD_DIM
    return pl.pallas_call(
        project_kernel,
        grid=(features // wide,),
        out_shape=(
            jax.ShapeDtypeStruct((HEADS, 3 * HEAD_DIM, rows), low),
            jax.ShapeDtypeStruct((rows, features), low),
        ),
        in_specs=[
            pl.BlockSpec((rows, features), lambda i: (0, 0)),
            pl.BlockSpec((1, features), lambda i: (0, 0)),
        ]
        + thirds(features, wide),
        out_specs=[
            pl.BlockSpec((4, 3 * HEAD_DIM, rows), lambda i: (i, 0, 0)),
            pl.BlockSpec((rows, features), lambda i: (0, 0)),
        ],
        compiler_params=pltpu.CompilerParams(vmem_limit_bytes=vmem_bytes),
        cost_estimate=pl.CostEstimate(
            flops=6 * rows * features * features, bytes_accessed=8 * features * features, transcendentals=0
        ),
        name="norm_and_project",
    )(frames, gain[None], w_qkv, w_qkv, w_qkv)


def middle_kernel(
    control_ref, frames_ref, att_ref, cot_ref, gain_ref, out_weight_ref, up_ref, down_ref,
    result_ref, grad_middle_ref, branch_ref, branch_away_ref, grad_att_ref, low_two_ref,
    act_0_ref, act_1_ref, act_2_ref, act_3_ref, grad_hidden_ref, grad_hidden_away_ref,
    unit_s, inverse_s, sum_s, back_s, low_two_s, mixed_s, act_s,
):
    step = pl.program_id(0)
    steps = pl.num_programs(0)
    core = control_ref[0]
    valid = control_ref[1]
    rows, features = frames_ref.shape
    root = 0.7978845608028654
    cubic = 0.044715
    across = (((1,), (1,)), ((), ()))
    present = (lax.broadcasted_iota(jnp.int32, (rows, 1), 0) < valid).astype(full)

    def by_core(array, own_ref, away_ref):
        halves = (array[:, : features // 2], array[:, features // 2 :])
        for value in range(2):

            @pl.when(core == value)
            def _():
                own_ref[...] = halves[value]
                away_ref[...] = halves[1 - value]

    @pl.when(step == 0)
    def _():
        middle = frames_ref[...].astype(full) + jnp.dot(
            att_ref[...].T, out_weight_ref[...], preferred_element_type=full
        )
        unit, inverse = norm_parts(middle)
        unit_s[...] = unit
        inverse_s[...] = inverse
        low_two_s[...] = (unit * gain_ref[...]).astype(low)
        low_two_ref[...] = low_two_s[...].T
        mixed_s[...] = (cot_ref[...].astype(full) * present).astype(low)
        sum_s[...] = middle
        back_s[...] = jnp.zeros_like(back_s)

    hidden = jnp.dot(low_two_s[...], up_ref[...], preferred_element_type=full)
    grad_act = lax.dot_general(mixed_s[...], down_ref[...], across, preferred_element_type=full)
    square = hidden * hidden
    bent = jnp.tanh(root * hidden * (1.0 + cubic * square))
    half = 0.5 * (1.0 + bent)
    act = (hidden * half).astype(low)
    slope = half + (0.5 * root) * hidden * (1.0 - bent * bent) * (1.0 + (3.0 * cubic) * square)
    grad_hidden = (slope * grad_act).astype(low)
    turned = act.T
    places, cores, high, piece, _ = act_s.shape
    for at in range(high * places * cores):
        outer, place, half_at = at // (places * cores), at // cores % places, at % cores
        act_s[place, half_at, outer] = turned[at * piece : (at + 1) * piece]
    for other, act_ref in enumerate((act_0_ref, act_1_ref, act_2_ref, act_3_ref)):
        act_ref[...] = act_s[control_ref[2] ^ other]

    @pl.when(step < steps // 2)
    def _():
        grad_hidden_ref[...] = grad_hidden

    @pl.when(step >= steps // 2)
    def _():
        grad_hidden_away_ref[...] = grad_hidden

    sum_s[...] += jnp.dot(act, down_ref[...], preferred_element_type=full)
    back_s[...] += lax.dot_general(grad_hidden, up_ref[...], across, preferred_element_type=full)

    @pl.when(step == steps - 1)
    def _():
        result_ref[...] = (present * sum_s[...]).astype(low)
        grad_middle = mixed_s[...].astype(full) + norm_back(
            back_s[...], unit_s[...], inverse_s[...], gain_ref[...]
        )
        grad_middle_ref[...] = grad_middle
        branch = grad_middle.astype(low)
        by_core(branch, branch_ref, branch_away_ref)
        grad_att = lax.dot_general(out_weight_ref[...], branch, across, preferred_element_type=full)
        lane = (lax.broadcasted_iota(jnp.int32, (1, rows), 1) < valid).astype(full)
        grad_att_ref[...] = (grad_att * lane).astype(low)


def middle_part(core, valid, place, frames, att, cot, gain, w_out, w_up, w_down):
    rows, features = frames.shape
    hidden = w_up.shape[1]
    wide = 1024
    steps = hidden // wide
    size = lax.axis_size("seq")
    piece = hidden // size
    here = lambda i, s: (i + s[0] * (steps // 2)) % steps
    whole = lambda *shape: pl.BlockSpec(shape, lambda i, s: (0,) * len(shape))
    square = (rows, features)
    turned = (features, rows)
    halved = (rows, features // 2)
    outs = [
        (square, low, None),
        (square, full, None),
        (halved, low, None),
        (halved, low, None),
        (turned, low, None),
        (turned, low, None),
        *[
            (
                (2, size // 4, piece // 2, rows),
                low,
                pl.BlockSpec((2, wide // piece // 4, piece // 2, rows), lambda i, s: (0, here(i, s), 0, 0)),
            )
        ]
        * 4,
        ((rows, hidden // 2), low, pl.BlockSpec((rows, wide), lambda i, s: (0, jnp.minimum(i, steps // 2 - 1)))),
        ((rows, hidden // 2), low, pl.BlockSpec((rows, wide), lambda i, s: (0, jnp.maximum(i - steps // 2, 0)))),
    ]
    return pl.pallas_call(
        middle_kernel,
        grid_spec=pltpu.PrefetchScalarGridSpec(
            num_scalar_prefetch=1,
            grid=(steps,),
            in_specs=[
                whole(*square),
                whole(*turned),
                whole(*square),
                whole(1, features),
                whole(features, features),
                pl.BlockSpec((features, wide), lambda i, s: (0, here(i, s))),
                pl.BlockSpec((wide, features), lambda i, s: (here(i, s), 0)),
            ],
            out_specs=[spec or whole(*shape) for shape, _, spec in outs],
            scratch_shapes=[
                pltpu.VMEM(square, full),
                pltpu.VMEM((rows, 1), full),
                pltpu.VMEM(square, full),
                pltpu.VMEM(square, full),
                pltpu.VMEM(square, low),
                pltpu.VMEM(square, low),
                pltpu.VMEM((4, 2, wide // piece // 4, piece // 2, rows), low),
            ],
        ),
        out_shape=[jax.ShapeDtypeStruct(shape, kind) for shape, kind, _ in outs],
        compiler_params=pltpu.CompilerParams(vmem_limit_bytes=vmem_bytes),
        cost_estimate=pl.CostEstimate(
            flops=8 * rows * features * hidden + 4 * rows * features * features,
            bytes_accessed=4 * features * hidden + 2 * features * features,
            transcendentals=rows * hidden,
        ),
        name="middle",
    )(jnp.stack([core, valid, place]), frames, att, cot, gain[None], w_out, w_up, w_down)


def finish_kernel(frames_ref, middle_ref, gain_ref, rows_ref, query_ref, key_ref, value_ref, result_ref, back_s):
    step = pl.program_id(0)
    heads, _, rows = rows_ref.shape

    @pl.when(step == 0)
    def _():
        back_s[...] = jnp.zeros_like(back_s)

    total = back_s[...]
    for part, weight_ref in enumerate((query_ref, key_ref, value_ref)):
        grads = rows_ref[:, part * HEAD_DIM : (part + 1) * HEAD_DIM, :].reshape(heads * HEAD_DIM, rows)
        total = total + jnp.dot(weight_ref[...], grads, preferred_element_type=full)
    back_s[...] = total

    @pl.when(step == pl.num_programs(0) - 1)
    def _():
        unit, inverse = norm_parts(frames_ref[...].astype(full))
        result_ref[...] = middle_ref[...] + norm_back(back_s[...].T, unit, inverse, gain_ref[...])


def finish(frames, grad_middle, gain, grad_rows, w_qkv):
    rows, features = frames.shape
    wide = 4 * HEAD_DIM
    whole = lambda *shape: pl.BlockSpec(shape, lambda i: (0,) * len(shape))
    return pl.pallas_call(
        finish_kernel,
        grid=(features // wide,),
        out_shape=jax.ShapeDtypeStruct((rows, features), full),
        in_specs=[
            whole(rows, features),
            whole(rows, features),
            whole(1, features),
            pl.BlockSpec((4, 3 * HEAD_DIM, rows), lambda i: (i, 0, 0)),
        ]
        + thirds(features, wide),
        out_specs=whole(rows, features),
        scratch_shapes=[pltpu.VMEM((features, rows), full)],
        compiler_params=pltpu.CompilerParams(vmem_limit_bytes=vmem_bytes),
        cost_estimate=pl.CostEstimate(
            flops=6 * rows * features * features, bytes_accessed=8 * features * features, transcendentals=0
        ),
        name="input_gradient",
    )(frames, grad_middle, gain[None], grad_rows, w_qkv, w_qkv, w_qkv)


def terms_kernel(pick_ref, *refs, groups, needs, sets, came_sets):
    step = pl.program_id(0)
    refs = list(refs)
    take = lambda count: [refs.pop(0) for _ in range(count)]
    lefts = [{kind: take(2) for kind in kinds} for kinds in needs]
    rights = [take(2) for _ in range(2)]
    came = take(len(came_sets))
    places = {}
    for came_ref, members in zip(came, came_sets):
        at = 0
        for group in members:
            places[group] = (came_ref, at)
            at += sum(stop - start for _, start, stop in groups[group][3])

    def write(outs):
        for out_ref, members in zip(outs, sets):
            at = 0
            for group in members:
                inner = 0
                for kind, start, stop in groups[group][3]:
                    own_ref, other_ref = lefts[group][kind]
                    rows, frames = own_ref.shape[-2:]
                    left = jnp.concatenate([ref[...].reshape(-1, frames) for ref in (own_ref, other_ref)], axis=1)
                    right = jnp.concatenate([ref[:, start:stop] for ref in rights[kind]], axis=0)
                    terms = jnp.dot(left, right, preferred_element_type=full).reshape(-1, rows, stop - start)
                    if came:
                        came_ref, first = places[group]
                        first += inner
                        terms = terms + came_ref[:, :, first : first + stop - start].astype(full)
                    out_ref[:, :, at : at + stop - start] = terms.astype(low)
                    at += stop - start
                    inner += stop - start

    if not came:
        write(refs)
    else:
        pl.when(step == 0)(functools.partial(write, refs[: len(sets)]))
        pl.when(step == 1)(functools.partial(write, refs[len(sets) :]))


def terms_by_piece(groups, sets, bits, two, att, hidden, branch, came=(), came_sets=()):
    size = lax.axis_size("seq")
    features, frames = two[0].shape
    rows = features // size
    quarter = size // 4
    width_of = lambda members: sum(stop - start for group in members for _, start, stop in groups[group][3])
    needs = [sorted({kind for kind, _, _ in parts}) for *_, parts in groups]
    lefts, specs = [], []
    for (first, after, _, _), kinds in zip(groups, needs):
        upper, lower = max(first, after), min(first, after)
        cut = (size >> (upper + 1), 2, 1 << (upper - lower - 1), 2, 1 << lower)

        def index(i, s, first=first, after=after, upper=upper):
            value = s[first] if came else 1 - s[first]
            beyond = s[after] ^ (1 - i)
            outer, inner = (value, beyond) if upper == first else (beyond, value)
            return (0, outer, 0, inner, 0, 0, 0)

        for kind in kinds:
            lefts += [a.reshape(cut + (rows, frames)) for a in (two, att)[kind]]
            specs += [pl.BlockSpec((cut[0], 1, cut[2], 1, cut[4], rows, frames), index)] * 2
    rights = (*hidden, *branch)
    specs += [pl.BlockSpec(a.shape, lambda i, s: (0, 0)) for a in rights]
    half = lambda members: pl.BlockSpec((None, quarter, rows, width_of(members)), lambda i, s: (i, 0, 0, 0))
    specs += [half(members) for members in came_sets]
    shapes = [(quarter, rows, width_of(members)) for members in sets]
    if came:
        shapes = shapes * 2
        outs = [pl.BlockSpec(shape, lambda i, s: (0, 0, 0)) for shape in shapes]
    else:
        outs = [half(members) for members in sets]
        shapes = [(2,) + shape for shape in shapes]
    return pl.pallas_call(
        functools.partial(terms_kernel, groups=groups, needs=needs, sets=sets, came_sets=came_sets),
        grid_spec=pltpu.PrefetchScalarGridSpec(num_scalar_prefetch=1, grid=(2,), in_specs=specs, out_specs=outs),
        out_shape=[jax.ShapeDtypeStruct(shape, low) for shape in shapes],
        compiler_params=pltpu.CompilerParams(vmem_limit_bytes=vmem_bytes),
        cost_estimate=pl.CostEstimate(
            flops=2 * frames * features * 5 * features // 2, bytes_accessed=5 * features * features, transcendentals=0
        ),
        name="terms_by_piece",
    )(jnp.stack(bits), *lefts, *rights, *came)


def tall_terms_kernel(pick_ref, *refs):
    step = pl.program_id(0)
    acts, mixed, outs = refs[:8], refs[8:16], refs[16:]
    high, rows, frames = acts[0].shape

    def write(out_ref):
        total = None
        for act_ref, mixed_ref in zip(acts, mixed):
            terms = jnp.dot(act_ref[...].reshape(high * rows, frames), mixed_ref[...], preferred_element_type=full)
            total = terms if total is None else total + terms
        out_ref[...] = total.astype(low).reshape(out_ref.shape)

    for value in range(2):
        pl.when(step == value)(functools.partial(write, outs[value]))


def tall_terms(core, bit, act_own, act_other, mixed_own, mixed_other):
    count, high, rows, frames = act_other.shape
    features = mixed_own[0].shape[-1]
    half = high // 2
    cut = lambda a: a.reshape(a.shape[:-3] + (half, 2, rows, frames))
    own = pl.BlockSpec((None, half, None, rows, frames), lambda i, s: (s[0], 0, s[1] ^ (1 - i), 0, 0))
    away = lambda other: pl.BlockSpec((None, half, None, rows, frames), lambda i, s: (other, 0, s[1] ^ (1 - i), 0, 0))
    whole = lambda *shape: pl.BlockSpec(shape, lambda i, s: (0,) * len(shape))
    return pl.pallas_call(
        tall_terms_kernel,
        grid_spec=pltpu.PrefetchScalarGridSpec(
            num_scalar_prefetch=1,
            grid=(2,),
            in_specs=[own] * 4
            + [away(other) for other in range(4)]
            + [whole(frames, features)] * 8,
            out_specs=[whole(half, rows, features)] * 2,
        ),
        out_shape=[jax.ShapeDtypeStruct((half, rows, features), low)] * 2,
        compiler_params=pltpu.CompilerParams(vmem_limit_bytes=vmem_bytes),
        cost_estimate=pl.CostEstimate(
            flops=4 * count * frames * high * rows * features, bytes_accessed=16 * frames * features, transcendentals=0
        ),
        name="tall_terms",
    )(jnp.stack([core, bit]), *[cut(a) for a in act_own], *[cut(act_other)] * 4, *mixed_own, *mixed_other)


def add_split_kernel(pick_ref, *refs, sets, spans):
    step = pl.program_id(0)
    terms, outs = refs[: 2 * len(spans)], refs[2 * len(spans) :]

    def write(outs):
        for out_ref, members in zip(outs, sets):
            at = 0
            for group in members:
                first, second = [ref[:, :, :, spans[group]] for ref in terms[2 * group : 2 * group + 2]]
                width = first.shape[-1]
                out_ref[:, :, :, at : at + width] = (first.astype(full) + second.astype(full)).astype(low)
                at += width

    pl.when(step == 0)(functools.partial(write, outs[: len(sets)]))
    pl.when(step == 1)(functools.partial(write, outs[len(sets) :]))


def add_split(pairs, old_sets, sets, widths, outer, inner, mine):
    rows = pairs[0][0].shape[-2]
    arrays, specs, spans = [], [], []
    for group in range(len(widths)):
        ((which, members),) = [(which, members) for which, members in enumerate(old_sets) if group in members]
        at = sum(widths[other] for other in members[: members.index(group)])
        spans.append(slice(at, at + widths[group]))
        index = lambda i, s, group=group: (0, s[group] ^ (1 - i), 0, 0, 0)
        columns = pairs[which][0].shape[-1]
        arrays += [a.reshape(outer, 2, inner, rows, columns) for a in pairs[which]]
        specs += [pl.BlockSpec((outer, None, inner, rows, columns), index)] * 2
    shapes = [(outer, inner, rows, sum(widths[group] for group in members)) for members in sets]
    sums = pl.pallas_call(
        functools.partial(add_split_kernel, sets=sets, spans=spans),
        grid_spec=pltpu.PrefetchScalarGridSpec(
            num_scalar_prefetch=1,
            grid=(2,),
            in_specs=specs,
            out_specs=[pl.BlockSpec(shape, lambda i, s: (0, 0, 0, 0)) for shape in shapes * 2],
        ),
        out_shape=[jax.ShapeDtypeStruct(shape, low) for shape in shapes * 2],
        compiler_params=pltpu.CompilerParams(vmem_limit_bytes=vmem_bytes),
        name="add_split",
    )(jnp.stack(mine), *arrays)
    sums = [a.reshape((outer * inner,) + a.shape[2:]) for a in sums]
    return sums[: len(sets)], sums[len(sets) :]


def plane_terms_kernel(pick_ref, *refs):
    rows, lows, (keep_ref, send_ref, turn_s) = refs[:4], refs[4:8], refs[8:]
    core = pick_ref[0]
    lines, columns, frames = rows[0].shape
    total = None
    for rows_ref, low_ref in zip(rows, lows):
        terms = jnp.dot(rows_ref[...].reshape(lines * columns, frames), low_ref[...], preferred_element_type=full)
        total = terms if total is None else total + terms
    turn_s[...] = total.T.reshape(turn_s.shape)
    keep_ref[...] = turn_s[:, :, core].reshape(keep_ref.shape)
    send_ref[...] = turn_s[:, :, 1 - core].astype(low).reshape(send_ref.shape)


def plane_terms(core, place, line_rows, lows):
    lines, count, columns, frames = line_rows.shape
    features = lows[0].shape[-1]
    rows = features // lines // count // 2
    shape = (lines, count * rows, lines * columns)
    whole = pl.BlockSpec(shape, lambda i, s: (0, 0, 0))
    source = lambda other: pl.BlockSpec((lines, None, columns, frames), lambda i, s: (0, s[1] ^ other, 0, 0))
    return pl.pallas_call(
        plane_terms_kernel,
        grid_spec=pltpu.PrefetchScalarGridSpec(
            num_scalar_prefetch=1,
            grid=(1,),
            in_specs=[source(other) for other in range(4)]
            + [pl.BlockSpec((frames, features), lambda i, s: (0, 0))] * 4,
            out_specs=[whole, whole],
            scratch_shapes=[pltpu.VMEM((lines, count, 2, rows, lines * columns), full)],
        ),
        out_shape=(jax.ShapeDtypeStruct(shape, full), jax.ShapeDtypeStruct(shape, low)),
        compiler_params=pltpu.CompilerParams(vmem_limit_bytes=vmem_bytes),
        cost_estimate=pl.CostEstimate(
            flops=2 * lines * count * columns * frames * features, bytes_accessed=8 * line_rows.size, transcendentals=0
        ),
        name="plane_terms",
    )(jnp.stack([core, place]), *[line_rows] * 4, *lows)


def gain_sum(weights, grads, gain):
    total = jnp.sum(weights.astype(full) * grads, axis=1, keepdims=True)
    return jnp.broadcast_to(total, (total.shape[0], 128)).T[0:1] / gain


def wide_output_kernel(pick_ref, halves_ref, weight_ref, gain_ref, up_ref, out_ref, sum_ref):
    split, half = up_ref.shape[1] // 2, out_ref.shape[1] // 2
    for side in range(2):
        up_ref[:, side * split : (side + 1) * split] = halves_ref[side, :, 0:split].astype(full)
        out_ref[:, side * half : (side + 1) * half] = halves_ref[side, :, split : split + half].astype(full)
    sum_ref[...] = gain_sum(weight_ref[...], up_ref[...], gain_ref[...])


def tall_output_kernel(pick_ref, halves_ref, weight_ref, gain_ref, qkv_ref, sum_ref):
    rows = qkv_ref.shape[0] // 2
    for side in range(2):
        qkv_ref[side * rows : (side + 1) * rows, :] = halves_ref[side].astype(full)
    sum_ref[...] = gain_sum(weight_ref[...], qkv_ref[...], gain_ref[...])


def write_outputs(kernel, halves, weight, gain, shapes, name):
    size = lax.axis_size("seq")
    rows = weight.shape[0] // size
    whole = lambda *shape: pl.BlockSpec(shape, lambda i, s: (0,) * len(shape))
    shapes = [*shapes, (1, rows)]
    return pl.pallas_call(
        kernel,
        grid_spec=pltpu.PrefetchScalarGridSpec(
            num_scalar_prefetch=1,
            grid=(1,),
            in_specs=[
                whole(*halves.shape),
                pl.BlockSpec((rows, weight.shape[1]), lambda i, s: (s[0], 0)),
                pl.BlockSpec((None, 1, rows), lambda i, s: (s[0], 0, 0)),
            ],
            out_specs=[whole(*shape) for shape in shapes],
        ),
        out_shape=[jax.ShapeDtypeStruct(shape, full) for shape in shapes],
        compiler_params=pltpu.CompilerParams(vmem_limit_bytes=vmem_bytes),
        name=name,
    )(lax.axis_index("seq")[None], halves, weight, gain.reshape(size, 1, rows))


def other_core(array):
    count = lax.axis_size("items")
    return lax.ppermute(array, "items", [(i, i ^ 1) for i in range(count)])


def to_heads(array):
    copies = lax.axis_size("seq") // HEADS
    if copies > 1:
        array = jnp.repeat(array, copies, axis=0)
    return lax.all_to_all(array, "seq", 0, 0, tiled=True)


def by_head(array, axis):
    copies = array.shape[axis] // HEADS
    if copies == 1:
        return array
    shape = array.shape[:axis] + (HEADS, copies) + array.shape[axis + 1 :]
    return jnp.sum(array.reshape(shape).astype(full), axis=axis + 1).astype(low)


def pick(array, index, axis):
    return lax.dynamic_index_in_dim(array, index, axis, keepdims=False)


def swapped(array, bits):
    return lax.ppermute(array, "seq", [(i, i ^ bits) for i in range(lax.axis_size("seq"))])


def flipped(array, bit):
    return swapped(array, 1 << bit)


def split_terms(terms, bit, left):
    axis = left.index(bit)
    mine = (lax.axis_index("seq") >> bit) & 1
    terms = [a.reshape((2,) * len(left) + a.shape[-2:]) for a in terms]

    def part(value):
        chosen = [pick(a, value, axis) for a in terms]
        return chosen[0] if len(chosen) == 1 else (chosen[0].astype(full) + chosen[1].astype(full)).astype(low)

    left.remove(bit)
    return part(1 - mine), part(mine)


def together(first, second):
    return (first.astype(full) + second.astype(full)).astype(low)


def over_items(piece):
    count = lax.axis_size("items")
    if count == 2:
        other = other_core(piece)
        first = lax.axis_index("items") == 0
        return jnp.stack([jnp.where(first, piece, other), jnp.where(first, other, piece)])
    pieces = lax.all_gather(piece, "items", axis=0)
    return jnp.sum(pieces.reshape((count // 2, 2) + piece.shape).astype(full), axis=0)


def on_device(frames, lengths, w_qkv, w_out, w_up, w_down, gain_one, gain_two, cotangent):
    row_count, features = frames.shape[1:]
    hidden_count = w_up.shape[1]
    size = lax.axis_size("seq")
    depth = size.bit_length() - 1
    me = lax.axis_index("seq")
    core = lax.axis_index("items") % 2
    copies = size // HEADS
    ends = jnp.cumsum(lengths[0]).astype(jnp.int32)
    valid = jnp.clip(ends[-1] - me * row_count, 0, row_count)
    control = jnp.concatenate([ends, (me % copies)[None]])
    rows_out = features // size

    lines = size // 4
    fours = [list(range(at, at + 4)) for at in range(0, size, 4)]
    columns = [list(range(at, size, 4)) for at in range(4)]
    across = lambda array, groups: lax.all_to_all(array, "seq", 0, 0, tiled=True, axis_index_groups=groups)
    bits = [(me >> bit) & 1 for bit in range(depth)]

    head_parts, low_one = project(frames[0], gain_one, w_qkv)
    head_rows = to_heads(head_parts)
    mixed = cotangent[0] * (jnp.arange(row_count) < valid).astype(low)[:, None]
    mixed_x, mixed_y = flipped(mixed, 0), flipped(mixed, 1)
    head_rows, low_one, mixed_x, mixed_y = lax.optimization_barrier((head_rows, low_one, mixed_x, mixed_y))
    low_x, mixed_xy = flipped(low_one, 0), flipped(mixed_x, 1)
    head_out, log_mass = attn_fwd(control, head_rows, copies)
    head_out, low_x, mixed_xy = lax.optimization_barrier((head_out, low_x, mixed_xy))
    mixed_own = (mixed, mixed_x, mixed_y, mixed_xy)
    moved = lax.all_to_all(head_out, "seq", 0, 0, tiled=True)
    attended = by_head(moved, 0).reshape(features, row_count)
    attended, low_one, low_x = lax.optimization_barrier((attended, low_one, low_x))
    lows = (low_one, low_x, flipped(low_one, 1), flipped(low_x, 1))
    att = (attended, other_core(attended))

    result, grad_middle, branch, branch_away, grad_attended, two, *acts, hidden, hidden_away = middle_part(
        core, valid, me % 4, frames[0], attended, cotangent[0], gain_two, w_out, w_up, w_down
    )
    grad_attended, two, acts, hidden, hidden_away, branch, branch_away, lows = lax.optimization_barrier(
        (grad_attended, two, acts, hidden, hidden_away, branch, branch_away, lows)
    )
    grad_heads = to_heads(grad_attended.reshape(HEADS, HEAD_DIM, row_count))
    acts = [acts[0]] + [swapped(acts[other], other) for other in range(1, 4)]

    pairs = (
        (two, other_core(two)),
        att,
        (hidden, other_core(hidden_away)),
        (branch, other_core(branch_away)),
    )
    half = features // 2
    split = hidden_count // 2
    groups = (
        (0, 1, 2, ((0, 0, half),)),
        (1, 0, 2, ((0, half, 2 * half),)),
        (2, 0, 1, ((0, 2 * half, 7 * half // 2),)),
        (2, 1, 0, ((0, 7 * half // 2, split), (1, 0, half))),
    )
    widths = [sum(stop - start for _, start, stop in parts) for *_, parts in groups]
    sets = [((0,), (1,), (2, 3)), ((0, 3), (1, 2)), ((0, 1), (2,), (3,)), ((0, 1, 2, 3),)]
    travel = lambda arrays, turn: [flipped(a, groups[members[0]][turn]) for a, members in zip(arrays, sets[turn])]
    away = list(terms_by_piece(groups, sets[0], bits[:3], *pairs))
    grad_heads, away[0] = lax.optimization_barrier((grad_heads, away[0]))
    came = travel(away, 0)
    mixed_other = [other_core(a) for a in mixed_own]
    grad_heads, mixed_other = lax.optimization_barrier((grad_heads, mixed_other))

    grad_rows = attn_bwd(control, head_rows, grad_heads, head_out, log_mass, copies)
    grad_rows, acts, *came = lax.optimization_barrier((grad_rows, acts, *came))
    line_rows = across(grad_rows.reshape(lines, 4, 3 * HEAD_DIM, row_count), columns)

    halves = terms_by_piece(groups, sets[1], bits[:3], *pairs, came, sets[0])
    sends, keeps = halves[:2], halves[2:]
    acts, *sends = lax.optimization_barrier((acts, *sends))
    came = travel(sends, 1)
    acts_other = other_core(jnp.stack([pick(a, 1 - core, 0) for a in acts]))
    tall_send, tall_keep = tall_terms(core, bits[2], acts, acts_other, mixed_own, mixed_other)
    tall_came = flipped(tall_send, 2)
    tall_keep, *came = lax.optimization_barrier((tall_keep, *came))

    sends, keeps = add_split(list(zip(keeps, came)), sets[1], sets[2], widths, lines // 2, 1, [bits[group[2]] for group in groups])
    line_rows, *sends = lax.optimization_barrier((line_rows, *sends))
    came = travel(sends, 2)
    turned = line_rows.transpose(1, 0, 2, 3)
    line_rows, turned = lax.optimization_barrier((line_rows, turned))
    grad_packed = across(turned, fours)
    keep, send = plane_terms(core, me % 4, line_rows, lows)
    keep, send, tall_came, *came = lax.optimization_barrier((keep, send, tall_came, *came))
    both = (keep + other_core(send).astype(full)).astype(low)
    line_left = list(range(depth - 1, 1, -1))
    send, line_keep = split_terms((both,), 2, line_left)
    line_came = flipped(send, 2)
    line_keep, tall_came, *came = lax.optimization_barrier((line_keep, tall_came, *came))
    (wide_send,), (wide_keep,) = add_split(list(zip(keeps, came)), sets[2], sets[3], widths, lines // 4, 1, [bits[3]] * 4)
    tall_left = list(range(depth - 1, 2, -1))
    tall_send, tall_keep = split_terms((tall_keep, tall_came), 3, tall_left)
    wide_terms, wide_left = (wide_keep, flipped(wide_send, 3)), list(range(depth - 1, 3, -1))
    tall_rest = (tall_keep, flipped(tall_send, 3))
    for bit in range(4, depth):
        more, rest = split_terms(wide_terms, bit, wide_left)
        wide_terms = (rest, flipped(more, bit))
        more, rest = split_terms(tall_rest, bit, tall_left)
        tall_rest = (rest, flipped(more, bit))
    line_came, tall_came = lax.optimization_barrier((line_came, tall_rest[1]))
    tall_rest = (tall_rest[0], tall_came)
    line_terms = (line_keep, line_came)
    for bit in range(3, depth):
        send, keep = split_terms(line_terms, bit, line_left)
        grad_packed, send = lax.optimization_barrier((grad_packed, send))
        line_terms = (keep, flipped(send, bit))
    grad_packed = by_head(grad_packed.transpose(1, 0, 2, 3).reshape(size, 3 * HEAD_DIM, row_count), 0)
    grad_inputs = finish(frames[0], grad_middle, gain_one, grad_packed, w_qkv)
    line_came, wide_came, grad_inputs = lax.optimization_barrier((line_terms[1], wide_terms[1], grad_inputs))
    pieces = together(line_terms[0], line_came).reshape(4, rows_out // 2, lines * 3 * HEAD_DIM)
    pieces = across(pieces, fours)

    sums = over_items(together(wide_terms[0], wide_came).reshape(rows_out, split + half))
    up, out, sum_gain_two = write_outputs(
        wide_output_kernel, sums, w_up, gain_two, [(rows_out, hidden_count), (rows_out, features)], "wide_outputs"
    )
    down = over_items(together(tall_rest[0], tall_came).reshape(-1, features)).astype(full)
    down = down.reshape(hidden_count // size, features)
    pieces, up, out, down, sum_gain_two = lax.optimization_barrier((pieces, up, out, down, sum_gain_two))
    pieces = pieces.reshape(4, rows_out // 2, lines, 3, HEAD_DIM).transpose(1, 3, 2, 0, 4)
    pieces = by_head(pieces.reshape(rows_out // 2, 3, size, HEAD_DIM), 2)
    pieces = over_items(pieces.reshape(rows_out // 2, 3 * features))
    qkv, sum_gain_one = write_outputs(
        tall_output_kernel, pieces, w_qkv, gain_one, [(rows_out, 3 * features)], "tall_outputs"
    )
    return (result[None], grad_inputs[None], qkv, out, up, down, sum_gain_one[0], sum_gain_two[0])


def solution(mesh):
    return jax.shard_map(
        on_device,
        mesh=mesh,
        in_specs=(
            P("items", "seq", None),
            P("items", None),
            P(),
            P(),
            P(),
            P(),
            P(),
            P(),
            P("items", "seq", None),
        ),
        out_specs=(
            P("items", "seq", None),
            P("items", "seq", None),
            P("seq", None),
            P("seq", None),
            P("seq", None),
            P("seq", None),
            P("seq"),
            P("seq"),
        ),
        check_vma=False,
    )
```

```python
import functools

import jax
import jax.numpy as jnp
from jax import lax
from jax.experimental import pallas as pl
from jax.experimental.pallas import tpu as pltpu
from jax.sharding import PartitionSpec as P

HEADS = 16
HEAD_DIM = 64
eps = 1e-05
masked = -1e30
log2e = 1.4426950408889634
query_share = 1024
vmem_bytes = 58 * 2**20
low = jnp.bfloat16
full = jnp.float32


def lane_labels(ends_ref, utterances, start, rows, count):
    place = start + lax.broadcasted_iota(jnp.int32, (rows, count), 1)
    label = jnp.zeros((rows, count), jnp.int32)
    for u in range(utterances):
        label = label + (place >= ends_ref[u]).astype(jnp.int32)
    return label


def stage_scores(ends_ref, rows_ref, source, utterances, query_s, key_s, mass=None):
    frames = rows_ref.shape[2]
    label = lane_labels(ends_ref, utterances, source * frames, HEAD_DIM, frames)
    row = lax.broadcasted_iota(jnp.int32, (HEAD_DIM, frames), 0)
    own = jnp.where(row == label, 1.0, 0.0)
    barred = jnp.where((row != label) & (row <= utterances), masked, 0.0)
    if mass is not None:
        first = mass.astype(low).astype(full)
        second = (mass - first).astype(low).astype(full)
        for at, term in enumerate((first, second, mass - first - second)):
            own = jnp.where(row == utterances + 1 + at, -term, own)
        barred = jnp.where((row > utterances) & (row <= utterances + 3), 1.0, barred)
    span = pl.ds(source * frames, frames)
    query = rows_ref[source, 0:HEAD_DIM, :]
    query_s[0:HEAD_DIM, span] = query
    query_s[HEAD_DIM : 2 * HEAD_DIM, span] = query
    query_s[2 * HEAD_DIM : 3 * HEAD_DIM, span] = own.astype(low)
    query_s[3 * HEAD_DIM :, span] = jnp.zeros((HEAD_DIM, frames), low)
    key = rows_ref[source, HEAD_DIM : 2 * HEAD_DIM, :].astype(full) * (HEAD_DIM**-0.5 * log2e)
    main = key.astype(low)
    rest = (key - main.astype(full)).astype(low)
    key_s[span, 0 : 2 * HEAD_DIM] = jnp.concatenate([main, rest], axis=0).T
    key_s[span, 2 * HEAD_DIM :] = jnp.concatenate([barred.astype(low), jnp.zeros((HEAD_DIM, frames), low)], axis=0).T


def causal(scores):
    key_place = lax.broadcasted_iota(jnp.int32, scores.shape, 0)
    query_place = lax.broadcasted_iota(jnp.int32, scores.shape, 1)
    return jnp.where(key_place <= query_place, scores, masked)


def forward_kernel(ends_ref, rows_ref, out_ref, mass_ref, query_s, key_s, value_s, *, block, part, copies):
    sources, _, frames = rows_ref.shape
    utterances = ends_ref.shape[0] - 1
    share = ends_ref[utterances]
    total = sources * frames
    for source in range(sources):
        stage_scores(ends_ref, rows_ref, source, utterances, query_s, key_s)
        span = pl.ds(source * frames, frames)
        value_s[0:HEAD_DIM, span] = rows_ref[source, 2 * HEAD_DIM :, :]
        row = lax.broadcasted_iota(jnp.int32, (value_s.shape[0] - HEAD_DIM, frames), 0)
        value_s[HEAD_DIM:, span] = jnp.where(row == 0, 1.0, 0.0).astype(low)
    if copies > 1:
        out_ref[...] = jnp.zeros_like(out_ref)
        mass_ref[...] = jnp.zeros_like(mass_ref)

    def add_keys(current, query, start, stop, diagonal):
        scores = jnp.dot(key_s[start:stop, :], query, preferred_element_type=full)
        if diagonal:
            scores = causal(scores)
        new_peak = jnp.max(scores, axis=0, keepdims=True)
        if current is not None:
            new_peak = jnp.maximum(current[0], new_peak)
        weights = jnp.exp2(scores - new_peak)
        sums = jnp.dot(value_s[:, start:stop], weights.astype(low), preferred_element_type=full)
        if current is not None:
            sums = sums + current[1] * jnp.exp2(current[0] - new_peak)
        return new_peak, sums

    def query_block(start):
        query = query_s[:, start : start + block]
        whole = add_keys(None, query, 0, start, False) if start else None
        for at in range(0, block, part):
            lanes = slice(at, at + part)
            current = None if whole is None else (whole[0][:, lanes], whole[1][:, lanes])
            if at:
                current = add_keys(current, query[:, lanes], start, start + at, False)
            peak, sums = add_keys(current, query[:, lanes], start + at, start + at + part, True)
            mass = sums[HEAD_DIM : HEAD_DIM + 1]
            label = lane_labels(ends_ref, utterances, start + at, 1, part)
            out = (sums[0:HEAD_DIM] * jnp.where(label < utterances, 1.0 / mass, 0.0)).astype(low)
            mass_ref[:, start + at : start + at + part] = peak + jnp.log2(mass)
            for piece in range(part // frames):
                out_ref[(start + at) // frames + piece] = out[:, piece * frames : (piece + 1) * frames]

    for start in range(0, total, block):
        shared(share, start // query_share, copies, functools.partial(query_block, start))


def shared(share, turn, copies, work):
    if copies == 1:
        work()
    else:
        pl.when(share == turn % copies)(work)


def attn_fwd(ends, rows, copies):
    sources, _, frames = rows.shape
    total = sources * frames
    return pl.pallas_call(
        functools.partial(forward_kernel, block=query_share, part=query_share, copies=copies),
        out_shape=(
            jax.ShapeDtypeStruct((sources, HEAD_DIM, frames), low),
            jax.ShapeDtypeStruct((1, total), full),
        ),
        in_specs=[pl.BlockSpec(memory_space=pltpu.SMEM), pl.BlockSpec(memory_space=pltpu.VMEM)],
        out_specs=[pl.BlockSpec(memory_space=pltpu.VMEM)] * 2,
        scratch_shapes=[
            pltpu.VMEM((4 * HEAD_DIM, total), low),
            pltpu.VMEM((total, 4 * HEAD_DIM), low),
            pltpu.VMEM((HEAD_DIM + 16, total), low),
        ],
        compiler_params=pltpu.CompilerParams(vmem_limit_bytes=vmem_bytes),
        cost_estimate=pl.CostEstimate(
            flops=20 * total * total * HEAD_DIM, bytes_accessed=4 * rows.size, transcendentals=total * total // 2
        ),
        name="attention_forward",
    )(ends, rows)


def backward_kernel(
    ends_ref, rows_ref, grad_ref, out_ref, mass_ref, result_ref,
    query_s, key_s, keyt_s, value_s, grad_s, grad_key_s, grad_value_s, *, block, copies
):
    sources, _, frames = rows_ref.shape
    utterances = ends_ref.shape[0] - 1
    share = ends_ref[utterances]
    scale = HEAD_DIM**-0.5
    total = sources * frames
    row = lax.broadcasted_iota(jnp.int32, (HEAD_DIM, frames), 0)
    for source in range(sources):
        span = pl.ds(source * frames, frames)
        stage_scores(ends_ref, rows_ref, source, utterances, query_s, key_s, mass_ref[:, span])
        keyt_s[:, span] = rows_ref[source, HEAD_DIM : 2 * HEAD_DIM, :]
        grad = grad_ref[source]
        delta = jnp.sum(grad.astype(full) * out_ref[source].astype(full), axis=0, keepdims=True)
        first = delta.astype(low).astype(full)
        second = (delta - first).astype(low).astype(full)
        third = delta - first - second
        more = jnp.where(row == 0, -first, jnp.where(row == 1, -second, jnp.where(row == 2, -third, 0.0)))
        grad_s[0:HEAD_DIM, span] = grad
        grad_s[HEAD_DIM:, span] = more.astype(low)
        ones = jnp.where(row < 3, 1.0, 0.0).astype(low)
        value_s[span, :] = jnp.concatenate([rows_ref[source, 2 * HEAD_DIM :, :], ones], axis=0).T
    across = (((1,), (1,)), ((), ()))
    if copies > 1:
        grad_key_s[...] = jnp.zeros_like(grad_key_s)
        grad_value_s[...] = jnp.zeros_like(grad_value_s)
        result_ref[:, 0:HEAD_DIM, :] = jnp.zeros((sources, HEAD_DIM, frames), low)

    def query_block(start):
        span = slice(start, start + block)

        def add_keys(first, last, diagonal):
            keys = slice(first, last)
            scores = jnp.dot(key_s[keys, :], query_s[:, span], preferred_element_type=full)
            if diagonal:
                scores = causal(scores)
            probs = jnp.exp2(scores)
            shifted = jnp.dot(value_s[keys, :], grad_s[:, span], preferred_element_type=full)
            grad_scores = (probs * shifted).astype(low)
            grad_value = lax.dot_general(
                grad_s[0:HEAD_DIM, span], probs.astype(low), across, preferred_element_type=full
            )
            grad_key = lax.dot_general(query_s[0:HEAD_DIM, span], grad_scores, across, preferred_element_type=full)
            if diagonal and copies == 1:
                grad_value_s[:, keys] = grad_value
                grad_key_s[:, keys] = grad_key
            else:
                grad_value_s[:, keys] += grad_value
                grad_key_s[:, keys] += grad_key
            return jnp.dot(keyt_s[:, keys], grad_scores, preferred_element_type=full)

        grad_query = add_keys(start, start + block, True)
        if start:
            grad_query = grad_query + add_keys(0, start, False)
        grad_query = (grad_query * scale).astype(low)
        for piece in range(block // frames):
            result_ref[start // frames + piece, 0:HEAD_DIM, :] = grad_query[:, piece * frames : (piece + 1) * frames]

    for start in range(0, total, block):
        shared(share, start // query_share, copies, functools.partial(query_block, start))
    for source in range(sources):
        lanes = slice(source * frames, (source + 1) * frames)
        result_ref[source, HEAD_DIM : 2 * HEAD_DIM, :] = (grad_key_s[:, lanes] * scale).astype(low)
        result_ref[source, 2 * HEAD_DIM :, :] = grad_value_s[:, lanes].astype(low)


def attn_bwd(ends, rows, grads, outs, mass, copies):
    sources, _, frames = rows.shape
    total = sources * frames
    return pl.pallas_call(
        functools.partial(backward_kernel, block=max(frames, total // 16), copies=copies),
        out_shape=jax.ShapeDtypeStruct(rows.shape, low),
        in_specs=[pl.BlockSpec(memory_space=pltpu.SMEM)] + [pl.BlockSpec(memory_space=pltpu.VMEM)] * 4,
        out_specs=pl.BlockSpec(memory_space=pltpu.VMEM),
        scratch_shapes=[
            pltpu.VMEM((4 * HEAD_DIM, total), low),
            pltpu.VMEM((total, 4 * HEAD_DIM), low),
            pltpu.VMEM((HEAD_DIM, total), low),
            pltpu.VMEM((total, 2 * HEAD_DIM), low),
            pltpu.VMEM((2 * HEAD_DIM, total), low),
            pltpu.VMEM((HEAD_DIM, total), full),
            pltpu.VMEM((HEAD_DIM, total), full),
        ],
        compiler_params=pltpu.CompilerParams(vmem_limit_bytes=vmem_bytes),
        cost_estimate=pl.CostEstimate(
            flops=35 * total * total * HEAD_DIM, bytes_accessed=8 * rows.size, transcendentals=total * total // 2
        ),
        name="attention_backward",
    )(ends, rows, grads, outs, mass)


def norm_parts(inputs):
    centred = inputs - jnp.mean(inputs, axis=-1, keepdims=True)
    spread = jnp.mean(centred * centred, axis=-1, keepdims=True)
    inverse = lax.rsqrt(spread + eps)
    return centred * inverse, inverse


def norm_back(grad, unit, inverse, gain):
    scaled = grad * gain
    along = jnp.mean(scaled, axis=-1, keepdims=True)
    across = jnp.mean(scaled * unit, axis=-1, keepdims=True)
    return inverse * (scaled - along - unit * across)


def project_kernel(frames_ref, gain_ref, query_ref, key_ref, value_ref, rows_ref, low_ref):
    @pl.when(pl.program_id(0) == 0)
    def _():
        unit, _ = norm_parts(frames_ref[...].astype(full))
        low_ref[...] = (unit * gain_ref[...]).astype(low)

    heads = rows_ref.shape[0]
    for part, weight_ref in enumerate((query_ref, key_ref, value_ref)):
        packed = jnp.dot(low_ref[...], weight_ref[...], preferred_element_type=full).astype(low).T
        for head in range(heads):
            rows_ref[head, part * HEAD_DIM : (part + 1) * HEAD_DIM, :] = packed[
                head * HEAD_DIM : (head + 1) * HEAD_DIM
            ]


def thirds(features, wide):
    count = features // wide
    return [pl.BlockSpec((features, wide), lambda i, part=part: (0, part * count + i)) for part in range(3)]


def project(frames, gain, w_qkv):
    rows, features = frames.shape
    wide = 8 * HEAD_DIM
    return pl.pallas_call(
        project_kernel,
        grid=(features // wide,),
        out_shape=(
            jax.ShapeDtypeStruct((HEADS, 3 * HEAD_DIM, rows), low),
            jax.ShapeDtypeStruct((rows, features), low),
        ),
        in_specs=[
            pl.BlockSpec((rows, features), lambda i: (0, 0)),
            pl.BlockSpec((1, features), lambda i: (0, 0)),
        ]
        + thirds(features, wide),
        out_specs=[
            pl.BlockSpec((8, 3 * HEAD_DIM, rows), lambda i: (i, 0, 0)),
            pl.BlockSpec((rows, features), lambda i: (0, 0)),
        ],
        compiler_params=pltpu.CompilerParams(vmem_limit_bytes=vmem_bytes),
        cost_estimate=pl.CostEstimate(
            flops=6 * rows * features * features, bytes_accessed=8 * features * features, transcendentals=0
        ),
        name="norm_and_project",
    )(frames, gain[None], w_qkv, w_qkv, w_qkv)


def middle_kernel(
    control_ref, frames_ref, att_ref, cot_ref, gain_ref, out_weight_ref, up_ref, down_ref,
    result_ref, grad_middle_ref, branch_ref, branch_away_ref, grad_att_ref, low_two_ref,
    act_0_ref, act_1_ref, act_2_ref, act_3_ref, grad_hidden_ref, grad_hidden_away_ref,
    unit_s, inverse_s, sum_s, back_s, low_two_s, mixed_s, act_s,
):
    step = pl.program_id(0)
    steps = pl.num_programs(0)
    core = control_ref[0]
    valid = control_ref[1]
    rows, features = frames_ref.shape
    root = 0.7978845608028654
    cubic = 0.044715
    across = (((1,), (1,)), ((), ()))
    present = (lax.broadcasted_iota(jnp.int32, (rows, 1), 0) < valid).astype(full)

    def by_core(array, own_ref, away_ref):
        halves = (array[:, : features // 2], array[:, features // 2 :])
        for value in range(2):

            @pl.when(core == value)
            def _():
                own_ref[...] = halves[value]
                away_ref[...] = halves[1 - value]

    @pl.when(step == 0)
    def _():
        middle = frames_ref[...].astype(full) + jnp.dot(
            att_ref[...].T, out_weight_ref[...], preferred_element_type=full
        )
        unit, inverse = norm_parts(middle)
        unit_s[...] = unit
        inverse_s[...] = inverse
        low_two_s[...] = (unit * gain_ref[...]).astype(low)
        low_two_ref[...] = low_two_s[...].T
        mixed_s[...] = (cot_ref[...].astype(full) * present).astype(low)
        sum_s[...] = middle
        back_s[...] = jnp.zeros_like(back_s)

    hidden = jnp.dot(low_two_s[...], up_ref[...], preferred_element_type=full)
    grad_act = lax.dot_general(mixed_s[...], down_ref[...], across, preferred_element_type=full)
    square = hidden * hidden
    bent = jnp.tanh(root * hidden * (1.0 + cubic * square))
    half = 0.5 * (1.0 + bent)
    act = (hidden * half).astype(low)
    slope = half + (0.5 * root) * hidden * (1.0 - bent * bent) * (1.0 + (3.0 * cubic) * square)
    grad_hidden = (slope * grad_act).astype(low)
    turned = act.T
    places, cores, high, piece, _ = act_s.shape
    for at in range(high * places * cores):
        outer, place, half_at = at // (places * cores), at // cores % places, at % cores
        act_s[place, half_at, outer] = turned[at * piece : (at + 1) * piece]
    for other, act_ref in enumerate((act_0_ref, act_1_ref, act_2_ref, act_3_ref)):
        act_ref[...] = act_s[control_ref[2] ^ other]

    @pl.when(step < steps // 2)
    def _():
        grad_hidden_ref[...] = grad_hidden

    @pl.when(step >= steps // 2)
    def _():
        grad_hidden_away_ref[...] = grad_hidden

    sum_s[...] += jnp.dot(act, down_ref[...], preferred_element_type=full)
    back_s[...] += lax.dot_general(grad_hidden, up_ref[...], across, preferred_element_type=full)

    @pl.when(step == steps - 1)
    def _():
        result_ref[...] = (present * sum_s[...]).astype(low)
        grad_middle = mixed_s[...].astype(full) + norm_back(
            back_s[...], unit_s[...], inverse_s[...], gain_ref[...]
        )
        grad_middle_ref[...] = grad_middle
        branch = grad_middle.astype(low)
        by_core(branch, branch_ref, branch_away_ref)
        grad_att = lax.dot_general(out_weight_ref[...], branch, across, preferred_element_type=full)
        lane = (lax.broadcasted_iota(jnp.int32, (1, rows), 1) < valid).astype(full)
        grad_att_ref[...] = (grad_att * lane).astype(low)


def middle_part(core, valid, place, frames, att, cot, gain, w_out, w_up, w_down):
    rows, features = frames.shape
    hidden = w_up.shape[1]
    wide = 1024
    steps = hidden // wide
    size = lax.axis_size("seq")
    piece = hidden // size
    here = lambda i, s: (i + s[0] * (steps // 2)) % steps
    whole = lambda *shape: pl.BlockSpec(shape, lambda i, s: (0,) * len(shape))
    square = (rows, features)
    turned = (features, rows)
    halved = (rows, features // 2)
    outs = [
        (square, low, None),
        (square, full, None),
        (halved, low, None),
        (halved, low, None),
        (turned, low, None),
        (turned, low, None),
        *[
            (
                (2, size // 4, piece // 2, rows),
                low,
                pl.BlockSpec((2, wide // piece // 4, piece // 2, rows), lambda i, s: (0, here(i, s), 0, 0)),
            )
        ]
        * 4,
        ((rows, hidden // 2), low, pl.BlockSpec((rows, wide), lambda i, s: (0, jnp.minimum(i, steps // 2 - 1)))),
        ((rows, hidden // 2), low, pl.BlockSpec((rows, wide), lambda i, s: (0, jnp.maximum(i - steps // 2, 0)))),
    ]
    return pl.pallas_call(
        middle_kernel,
        grid_spec=pltpu.PrefetchScalarGridSpec(
            num_scalar_prefetch=1,
            grid=(steps,),
            in_specs=[
                whole(*square),
                whole(*turned),
                whole(*square),
                whole(1, features),
                whole(features, features),
                pl.BlockSpec((features, wide), lambda i, s: (0, here(i, s))),
                pl.BlockSpec((wide, features), lambda i, s: (here(i, s), 0)),
            ],
            out_specs=[spec or whole(*shape) for shape, _, spec in outs],
            scratch_shapes=[
                pltpu.VMEM(square, full),
                pltpu.VMEM((rows, 1), full),
                pltpu.VMEM(square, full),
                pltpu.VMEM(square, full),
                pltpu.VMEM(square, low),
                pltpu.VMEM(square, low),
                pltpu.VMEM((4, 2, wide // piece // 4, piece // 2, rows), low),
            ],
        ),
        out_shape=[jax.ShapeDtypeStruct(shape, kind) for shape, kind, _ in outs],
        compiler_params=pltpu.CompilerParams(vmem_limit_bytes=vmem_bytes),
        cost_estimate=pl.CostEstimate(
            flops=8 * rows * features * hidden + 4 * rows * features * features,
            bytes_accessed=4 * features * hidden + 2 * features * features,
            transcendentals=rows * hidden,
        ),
        name="middle",
    )(jnp.stack([core, valid, place]), frames, att, cot, gain[None], w_out, w_up, w_down)


def finish_kernel(frames_ref, middle_ref, gain_ref, rows_ref, query_ref, key_ref, value_ref, result_ref, back_s):
    step = pl.program_id(0)
    heads, _, rows = rows_ref.shape

    @pl.when(step == 0)
    def _():
        back_s[...] = jnp.zeros_like(back_s)

    total = back_s[...]
    for part, weight_ref in enumerate((query_ref, key_ref, value_ref)):
        grads = rows_ref[:, part * HEAD_DIM : (part + 1) * HEAD_DIM, :].reshape(heads * HEAD_DIM, rows)
        total = total + jnp.dot(weight_ref[...], grads, preferred_element_type=full)
    back_s[...] = total

    @pl.when(step == pl.num_programs(0) - 1)
    def _():
        unit, inverse = norm_parts(frames_ref[...].astype(full))
        result_ref[...] = middle_ref[...] + norm_back(back_s[...].T, unit, inverse, gain_ref[...])


def finish(frames, grad_middle, gain, grad_rows, w_qkv):
    rows, features = frames.shape
    wide = 4 * HEAD_DIM
    whole = lambda *shape: pl.BlockSpec(shape, lambda i: (0,) * len(shape))
    return pl.pallas_call(
        finish_kernel,
        grid=(features // wide,),
        out_shape=jax.ShapeDtypeStruct((rows, features), full),
        in_specs=[
            whole(rows, features),
            whole(rows, features),
            whole(1, features),
            pl.BlockSpec((4, 3 * HEAD_DIM, rows), lambda i: (i, 0, 0)),
        ]
        + thirds(features, wide),
        out_specs=whole(rows, features),
        scratch_shapes=[pltpu.VMEM((features, rows), full)],
        compiler_params=pltpu.CompilerParams(vmem_limit_bytes=vmem_bytes),
        cost_estimate=pl.CostEstimate(
            flops=6 * rows * features * features, bytes_accessed=8 * features * features, transcendentals=0
        ),
        name="input_gradient",
    )(frames, grad_middle, gain[None], grad_rows, w_qkv, w_qkv, w_qkv)


def terms_kernel(pick_ref, *refs, groups, needs, sets, came_sets):
    step = pl.program_id(0)
    refs = list(refs)
    take = lambda count: [refs.pop(0) for _ in range(count)]
    lefts = [{kind: take(2) for kind in kinds} for kinds in needs]
    rights = [take(2) for _ in range(2)]
    came = take(len(came_sets))
    places = {}
    for came_ref, members in zip(came, came_sets):
        at = 0
        for group in members:
            places[group] = (came_ref, at)
            at += sum(stop - start for _, start, stop in groups[group][3])

    def write(outs):
        for out_ref, members in zip(outs, sets):
            at = 0
            for group in members:
                inner = 0
                for kind, start, stop in groups[group][3]:
                    own_ref, other_ref = lefts[group][kind]
                    rows, frames = own_ref.shape[-2:]
                    left = jnp.concatenate([ref[...].reshape(-1, frames) for ref in (own_ref, other_ref)], axis=1)
                    right = jnp.concatenate([ref[:, start:stop] for ref in rights[kind]], axis=0)
                    terms = jnp.dot(left, right, preferred_element_type=full).reshape(-1, rows, stop - start)
                    if came:
                        came_ref, first = places[group]
                        first += inner
                        terms = terms + came_ref[:, :, first : first + stop - start].astype(full)
                    out_ref[:, :, at : at + stop - start] = terms.astype(low)
                    at += stop - start
                    inner += stop - start

    if not came:
        write(refs)
    else:
        pl.when(step == 0)(functools.partial(write, refs[: len(sets)]))
        pl.when(step == 1)(functools.partial(write, refs[len(sets) :]))


def terms_by_piece(groups, sets, bits, two, att, hidden, branch, came=(), came_sets=()):
    size = lax.axis_size("seq")
    features, frames = two[0].shape
    rows = features // size
    quarter = size // 4
    width_of = lambda members: sum(stop - start for group in members for _, start, stop in groups[group][3])
    needs = [sorted({kind for kind, _, _ in parts}) for *_, parts in groups]
    lefts, specs = [], []
    for (first, after, _, _), kinds in zip(groups, needs):
        upper, lower = max(first, after), min(first, after)
        cut = (size >> (upper + 1), 2, 1 << (upper - lower - 1), 2, 1 << lower)

        def index(i, s, first=first, after=after, upper=upper):
            value = s[first] if came else 1 - s[first]
            beyond = s[after] ^ (1 - i)
            outer, inner = (value, beyond) if upper == first else (beyond, value)
            return (0, outer, 0, inner, 0, 0, 0)

        for kind in kinds:
            lefts += [a.reshape(cut + (rows, frames)) for a in (two, att)[kind]]
            specs += [pl.BlockSpec((cut[0], 1, cut[2], 1, cut[4], rows, frames), index)] * 2
    rights = (*hidden, *branch)
    specs += [pl.BlockSpec(a.shape, lambda i, s: (0, 0)) for a in rights]
    half = lambda members: pl.BlockSpec((None, quarter, rows, width_of(members)), lambda i, s: (i, 0, 0, 0))
    specs += [half(members) for members in came_sets]
    shapes = [(quarter, rows, width_of(members)) for members in sets]
    if came:
        shapes = shapes * 2
        outs = [pl.BlockSpec(shape, lambda i, s: (0, 0, 0)) for shape in shapes]
    else:
        outs = [half(members) for members in sets]
        shapes = [(2,) + shape for shape in shapes]
    return pl.pallas_call(
        functools.partial(terms_kernel, groups=groups, needs=needs, sets=sets, came_sets=came_sets),
        grid_spec=pltpu.PrefetchScalarGridSpec(num_scalar_prefetch=1, grid=(2,), in_specs=specs, out_specs=outs),
        out_shape=[jax.ShapeDtypeStruct(shape, low) for shape in shapes],
        compiler_params=pltpu.CompilerParams(vmem_limit_bytes=vmem_bytes),
        cost_estimate=pl.CostEstimate(
            flops=2 * frames * features * 5 * features // 2, bytes_accessed=5 * features * features, transcendentals=0
        ),
        name="terms_by_piece",
    )(jnp.stack(bits), *lefts, *rights, *came)


def tall_terms_kernel(pick_ref, *refs):
    step = pl.program_id(0)
    acts, mixed, outs = refs[:8], refs[8:16], refs[16:]
    high, rows, frames = acts[0].shape

    def write(out_ref):
        total = None
        for act_ref, mixed_ref in zip(acts, mixed):
            terms = jnp.dot(act_ref[...].reshape(high * rows, frames), mixed_ref[...], preferred_element_type=full)
            total = terms if total is None else total + terms
        out_ref[...] = total.astype(low).reshape(out_ref.shape)

    for value in range(2):
        pl.when(step == value)(functools.partial(write, outs[value]))


def tall_terms(core, bit, act_own, act_other, mixed_own, mixed_other):
    count, high, rows, frames = act_other.shape
    features = mixed_own[0].shape[-1]
    half = high // 2
    cut = lambda a: a.reshape(a.shape[:-3] + (half, 2, rows, frames))
    own = pl.BlockSpec((None, half, None, rows, frames), lambda i, s: (s[0], 0, s[1] ^ (1 - i), 0, 0))
    away = lambda other: pl.BlockSpec((None, half, None, rows, frames), lambda i, s: (other, 0, s[1] ^ (1 - i), 0, 0))
    whole = lambda *shape: pl.BlockSpec(shape, lambda i, s: (0,) * len(shape))
    return pl.pallas_call(
        tall_terms_kernel,
        grid_spec=pltpu.PrefetchScalarGridSpec(
            num_scalar_prefetch=1,
            grid=(2,),
            in_specs=[own] * 4
            + [away(other) for other in range(4)]
            + [whole(frames, features)] * 8,
            out_specs=[whole(half, rows, features)] * 2,
        ),
        out_shape=[jax.ShapeDtypeStruct((half, rows, features), low)] * 2,
        compiler_params=pltpu.CompilerParams(vmem_limit_bytes=vmem_bytes),
        cost_estimate=pl.CostEstimate(
            flops=4 * count * frames * high * rows * features, bytes_accessed=16 * frames * features, transcendentals=0
        ),
        name="tall_terms",
    )(jnp.stack([core, bit]), *[cut(a) for a in act_own], *[cut(act_other)] * 4, *mixed_own, *mixed_other)


def add_split_kernel(pick_ref, *refs, sets, spans):
    step = pl.program_id(0)
    terms, outs = refs[: 2 * len(spans)], refs[2 * len(spans) :]

    def write(outs):
        for out_ref, members in zip(outs, sets):
            at = 0
            for group in members:
                first, second = [ref[:, :, :, spans[group]] for ref in terms[2 * group : 2 * group + 2]]
                width = first.shape[-1]
                out_ref[:, :, :, at : at + width] = (first.astype(full) + second.astype(full)).astype(low)
                at += width

    pl.when(step == 0)(functools.partial(write, outs[: len(sets)]))
    pl.when(step == 1)(functools.partial(write, outs[len(sets) :]))


def add_split(pairs, old_sets, sets, widths, outer, inner, mine):
    rows = pairs[0][0].shape[-2]
    arrays, specs, spans = [], [], []
    for group in range(len(widths)):
        ((which, members),) = [(which, members) for which, members in enumerate(old_sets) if group in members]
        at = sum(widths[other] for other in members[: members.index(group)])
        spans.append(slice(at, at + widths[group]))
        index = lambda i, s, group=group: (0, s[group] ^ (1 - i), 0, 0, 0)
        columns = pairs[which][0].shape[-1]
        arrays += [a.reshape(outer, 2, inner, rows, columns) for a in pairs[which]]
        specs += [pl.BlockSpec((outer, None, inner, rows, columns), index)] * 2
    shapes = [(outer, inner, rows, sum(widths[group] for group in members)) for members in sets]
    sums = pl.pallas_call(
        functools.partial(add_split_kernel, sets=sets, spans=spans),
        grid_spec=pltpu.PrefetchScalarGridSpec(
            num_scalar_prefetch=1,
            grid=(2,),
            in_specs=specs,
            out_specs=[pl.BlockSpec(shape, lambda i, s: (0, 0, 0, 0)) for shape in shapes * 2],
        ),
        out_shape=[jax.ShapeDtypeStruct(shape, low) for shape in shapes * 2],
        compiler_params=pltpu.CompilerParams(vmem_limit_bytes=vmem_bytes),
        name="add_split",
    )(jnp.stack(mine), *arrays)
    sums = [a.reshape((outer * inner,) + a.shape[2:]) for a in sums]
    return sums[: len(sets)], sums[len(sets) :]


def plane_terms_kernel(pick_ref, *refs):
    rows, lows, (keep_ref, send_ref, turn_s) = refs[:4], refs[4:8], refs[8:]
    core = pick_ref[0]
    lines, columns, frames = rows[0].shape
    total = None
    for rows_ref, low_ref in zip(rows, lows):
        terms = jnp.dot(rows_ref[...].reshape(lines * columns, frames), low_ref[...], preferred_element_type=full)
        total = terms if total is None else total + terms
    turn_s[...] = total.T.reshape(turn_s.shape)
    keep_ref[...] = turn_s[:, :, core].reshape(keep_ref.shape)
    send_ref[...] = turn_s[:, :, 1 - core].astype(low).reshape(send_ref.shape)


def plane_terms(core, place, line_rows, lows):
    lines, count, columns, frames = line_rows.shape
    features = lows[0].shape[-1]
    rows = features // lines // count // 2
    shape = (lines, count * rows, lines * columns)
    whole = pl.BlockSpec(shape, lambda i, s: (0, 0, 0))
    source = lambda other: pl.BlockSpec((lines, None, columns, frames), lambda i, s: (0, s[1] ^ other, 0, 0))
    return pl.pallas_call(
        plane_terms_kernel,
        grid_spec=pltpu.PrefetchScalarGridSpec(
            num_scalar_prefetch=1,
            grid=(1,),
            in_specs=[source(other) for other in range(4)]
            + [pl.BlockSpec((frames, features), lambda i, s: (0, 0))] * 4,
            out_specs=[whole, whole],
            scratch_shapes=[pltpu.VMEM((lines, count, 2, rows, lines * columns), full)],
        ),
        out_shape=(jax.ShapeDtypeStruct(shape, full), jax.ShapeDtypeStruct(shape, low)),
        compiler_params=pltpu.CompilerParams(vmem_limit_bytes=vmem_bytes),
        cost_estimate=pl.CostEstimate(
            flops=2 * lines * count * columns * frames * features, bytes_accessed=8 * line_rows.size, transcendentals=0
        ),
        name="plane_terms",
    )(jnp.stack([core, place]), *[line_rows] * 4, *lows)


def gain_sum(weights, grads, gain):
    total = jnp.sum(weights.astype(full) * grads, axis=1, keepdims=True)
    return jnp.broadcast_to(total, (total.shape[0], 128)).T[0:1] / gain


def wide_output_kernel(pick_ref, halves_ref, weight_ref, gain_ref, up_ref, out_ref, sum_ref):
    split, half = up_ref.shape[1] // 2, out_ref.shape[1] // 2
    for side in range(2):
        up_ref[:, side * split : (side + 1) * split] = halves_ref[side, :, 0:split].astype(full)
        out_ref[:, side * half : (side + 1) * half] = halves_ref[side, :, split : split + half].astype(full)
    sum_ref[...] = gain_sum(weight_ref[...], up_ref[...], gain_ref[...])


def tall_output_kernel(pick_ref, halves_ref, weight_ref, gain_ref, qkv_ref, sum_ref):
    rows = qkv_ref.shape[0] // 2
    for side in range(2):
        qkv_ref[side * rows : (side + 1) * rows, :] = halves_ref[side].astype(full)
    sum_ref[...] = gain_sum(weight_ref[...], qkv_ref[...], gain_ref[...])


def write_outputs(kernel, halves, weight, gain, shapes, name):
    size = lax.axis_size("seq")
    rows = weight.shape[0] // size
    whole = lambda *shape: pl.BlockSpec(shape, lambda i, s: (0,) * len(shape))
    shapes = [*shapes, (1, rows)]
    return pl.pallas_call(
        kernel,
        grid_spec=pltpu.PrefetchScalarGridSpec(
            num_scalar_prefetch=1,
            grid=(1,),
            in_specs=[
                whole(*halves.shape),
                pl.BlockSpec((rows, weight.shape[1]), lambda i, s: (s[0], 0)),
                pl.BlockSpec((None, 1, rows), lambda i, s: (s[0], 0, 0)),
            ],
            out_specs=[whole(*shape) for shape in shapes],
        ),
        out_shape=[jax.ShapeDtypeStruct(shape, full) for shape in shapes],
        compiler_params=pltpu.CompilerParams(vmem_limit_bytes=vmem_bytes),
        name=name,
    )(lax.axis_index("seq")[None], halves, weight, gain.reshape(size, 1, rows))


def other_core(array):
    count = lax.axis_size("items")
    return lax.ppermute(array, "items", [(i, i ^ 1) for i in range(count)])


def to_heads(array):
    copies = lax.axis_size("seq") // HEADS
    if copies > 1:
        array = jnp.repeat(array, copies, axis=0)
    return lax.all_to_all(array, "seq", 0, 0, tiled=True)


def by_head(array, axis):
    copies = array.shape[axis] // HEADS
    if copies == 1:
        return array
    shape = array.shape[:axis] + (HEADS, copies) + array.shape[axis + 1 :]
    return jnp.sum(array.reshape(shape).astype(full), axis=axis + 1).astype(low)


def pick(array, index, axis):
    return lax.dynamic_index_in_dim(array, index, axis, keepdims=False)


def swapped(array, bits):
    return lax.ppermute(array, "seq", [(i, i ^ bits) for i in range(lax.axis_size("seq"))])


def flipped(array, bit):
    return swapped(array, 1 << bit)


def split_terms(terms, bit, left):
    axis = left.index(bit)
    mine = (lax.axis_index("seq") >> bit) & 1
    terms = [a.reshape((2,) * len(left) + a.shape[-2:]) for a in terms]

    def part(value):
        chosen = [pick(a, value, axis) for a in terms]
        return chosen[0] if len(chosen) == 1 else (chosen[0].astype(full) + chosen[1].astype(full)).astype(low)

    left.remove(bit)
    return part(1 - mine), part(mine)


def together(first, second):
    return (first.astype(full) + second.astype(full)).astype(low)


def over_items(piece):
    count = lax.axis_size("items")
    if count == 2:
        other = other_core(piece)
        first = lax.axis_index("items") == 0
        return jnp.stack([jnp.where(first, piece, other), jnp.where(first, other, piece)])
    pieces = lax.all_gather(piece, "items", axis=0)
    return jnp.sum(pieces.reshape((count // 2, 2) + piece.shape).astype(full), axis=0)


def on_device(frames, lengths, w_qkv, w_out, w_up, w_down, gain_one, gain_two, cotangent):
    row_count, features = frames.shape[1:]
    hidden_count = w_up.shape[1]
    size = lax.axis_size("seq")
    depth = size.bit_length() - 1
    me = lax.axis_index("seq")
    core = lax.axis_index("items") % 2
    copies = size // HEADS
    ends = jnp.cumsum(lengths[0]).astype(jnp.int32)
    valid = jnp.clip(ends[-1] - me * row_count, 0, row_count)
    control = jnp.concatenate([ends, (me % copies)[None]])
    rows_out = features // size

    lines = size // 4
    fours = [list(range(at, at + 4)) for at in range(0, size, 4)]
    columns = [list(range(at, size, 4)) for at in range(4)]
    across = lambda array, groups: lax.all_to_all(array, "seq", 0, 0, tiled=True, axis_index_groups=groups)
    bits = [(me >> bit) & 1 for bit in range(depth)]

    head_parts, low_one = project(frames[0], gain_one, w_qkv)
    head_rows = to_heads(head_parts)
    mixed = cotangent[0] * (jnp.arange(row_count) < valid).astype(low)[:, None]
    mixed_x, mixed_y = flipped(mixed, 0), flipped(mixed, 1)
    head_rows, low_one, mixed_x, mixed_y = lax.optimization_barrier((head_rows, low_one, mixed_x, mixed_y))
    low_x, mixed_xy = flipped(low_one, 0), flipped(mixed_x, 1)
    head_out, log_mass = attn_fwd(control, head_rows, copies)
    head_out, low_x, mixed_xy = lax.optimization_barrier((head_out, low_x, mixed_xy))
    mixed_own = (mixed, mixed_x, mixed_y, mixed_xy)
    moved = lax.all_to_all(head_out, "seq", 0, 0, tiled=True)
    attended = by_head(moved, 0).reshape(features, row_count)
    attended, low_one, low_x = lax.optimization_barrier((attended, low_one, low_x))
    lows = (low_one, low_x, flipped(low_one, 1), flipped(low_x, 1))
    att = (attended, other_core(attended))

    result, grad_middle, branch, branch_away, grad_attended, two, *acts, hidden, hidden_away = middle_part(
        core, valid, me % 4, frames[0], attended, cotangent[0], gain_two, w_out, w_up, w_down
    )
    grad_attended, two, acts, hidden, hidden_away, branch, branch_away, lows = lax.optimization_barrier(
        (grad_attended, two, acts, hidden, hidden_away, branch, branch_away, lows)
    )
    grad_heads = to_heads(grad_attended.reshape(HEADS, HEAD_DIM, row_count))
    acts = [acts[0]] + [swapped(acts[other], other) for other in range(1, 4)]

    pairs = (
        (two, other_core(two)),
        att,
        (hidden, other_core(hidden_away)),
        (branch, other_core(branch_away)),
    )
    half = features // 2
    split = hidden_count // 2
    groups = (
        (0, 1, 2, ((0, 0, half),)),
        (1, 0, 2, ((0, half, 2 * half),)),
        (2, 0, 1, ((0, 2 * half, 7 * half // 2),)),
        (2, 1, 0, ((0, 7 * half // 2, split), (1, 0, half))),
    )
    widths = [sum(stop - start for _, start, stop in parts) for *_, parts in groups]
    sets = [((0,), (1,), (2, 3)), ((0, 3), (1, 2)), ((0, 1), (2,), (3,)), ((0, 1, 2, 3),)]
    travel = lambda arrays, turn: [flipped(a, groups[members[0]][turn]) for a, members in zip(arrays, sets[turn])]
    away = list(terms_by_piece(groups, sets[0], bits[:3], *pairs))
    grad_heads, away[0] = lax.optimization_barrier((grad_heads, away[0]))
    came = travel(away, 0)
    mixed_other = [other_core(a) for a in mixed_own]
    grad_heads, mixed_other = lax.optimization_barrier((grad_heads, mixed_other))

    grad_rows = attn_bwd(control, head_rows, grad_heads, head_out, log_mass, copies)
    grad_rows, acts, *came = lax.optimization_barrier((grad_rows, acts, *came))
    line_rows = across(grad_rows.reshape(lines, 4, 3 * HEAD_DIM, row_count), columns)

    halves = terms_by_piece(groups, sets[1], bits[:3], *pairs, came, sets[0])
    sends, keeps = halves[:2], halves[2:]
    acts, *sends = lax.optimization_barrier((acts, *sends))
    came = travel(sends, 1)
    acts_other = other_core(jnp.stack([pick(a, 1 - core, 0) for a in acts]))
    tall_send, tall_keep = tall_terms(core, bits[2], acts, acts_other, mixed_own, mixed_other)
    tall_came = flipped(tall_send, 2)
    tall_keep, *came = lax.optimization_barrier((tall_keep, *came))

    sends, keeps = add_split(list(zip(keeps, came)), sets[1], sets[2], widths, lines // 2, 1, [bits[group[2]] for group in groups])
    line_rows, *sends = lax.optimization_barrier((line_rows, *sends))
    came = travel(sends, 2)
    turned = line_rows.transpose(1, 0, 2, 3)
    line_rows, turned = lax.optimization_barrier((line_rows, turned))
    grad_packed = across(turned, fours)
    keep, send = plane_terms(core, me % 4, line_rows, lows)
    keep, send, tall_came, *came = lax.optimization_barrier((keep, send, tall_came, *came))
    both = (keep + other_core(send).astype(full)).astype(low)
    line_left = list(range(depth - 1, 1, -1))
    send, line_keep = split_terms((both,), 2, line_left)
    line_came = flipped(send, 2)
    line_keep, tall_came, *came = lax.optimization_barrier((line_keep, tall_came, *came))
    (wide_send,), (wide_keep,) = add_split(list(zip(keeps, came)), sets[2], sets[3], widths, lines // 4, 1, [bits[3]] * 4)
    tall_left = list(range(depth - 1, 2, -1))
    tall_send, tall_keep = split_terms((tall_keep, tall_came), 3, tall_left)
    wide_terms, wide_left = (wide_keep, flipped(wide_send, 3)), list(range(depth - 1, 3, -1))
    tall_rest = (tall_keep, flipped(tall_send, 3))
    for bit in range(4, depth):
        more, rest = split_terms(wide_terms, bit, wide_left)
        wide_terms = (rest, flipped(more, bit))
        more, rest = split_terms(tall_rest, bit, tall_left)
        tall_rest = (rest, flipped(more, bit))
    line_came, tall_came = lax.optimization_barrier((line_came, tall_rest[1]))
    tall_rest = (tall_rest[0], tall_came)
    line_terms = (line_keep, line_came)
    for bit in range(3, depth):
        send, keep = split_terms(line_terms, bit, line_left)
        grad_packed, send = lax.optimization_barrier((grad_packed, send))
        line_terms = (keep, flipped(send, bit))
    grad_packed = by_head(grad_packed.transpose(1, 0, 2, 3).reshape(size, 3 * HEAD_DIM, row_count), 0)
    grad_inputs = finish(frames[0], grad_middle, gain_one, grad_packed, w_qkv)
    line_came, wide_came, grad_inputs = lax.optimization_barrier((line_terms[1], wide_terms[1], grad_inputs))
    pieces = together(line_terms[0], line_came).reshape(4, rows_out // 2, lines * 3 * HEAD_DIM)
    pieces, wide_came = lax.optimization_barrier((pieces, wide_came))
    pieces = across(pieces, fours)

    sums = over_items(together(wide_terms[0], wide_came).reshape(rows_out, split + half))
    up, out, sum_gain_two = write_outputs(
        wide_output_kernel, sums, w_up, gain_two, [(rows_out, hidden_count), (rows_out, features)], "wide_outputs"
    )
    down = over_items(together(tall_rest[0], tall_came).reshape(-1, features)).astype(full)
    down = down.reshape(hidden_count // size, features)
    pieces, up, out, down, sum_gain_two = lax.optimization_barrier((pieces, up, out, down, sum_gain_two))
    pieces = pieces.reshape(4, rows_out // 2, lines, 3, HEAD_DIM).transpose(1, 3, 2, 0, 4)
    pieces = by_head(pieces.reshape(rows_out // 2, 3, size, HEAD_DIM), 2)
    pieces = over_items(pieces.reshape(rows_out // 2, 3 * features))
    qkv, sum_gain_one = write_outputs(
        tall_output_kernel, pieces, w_qkv, gain_one, [(rows_out, 3 * features)], "tall_outputs"
    )
    return (result[None], grad_inputs[None], qkv, out, up, down, sum_gain_one[0], sum_gain_two[0])


def solution(mesh):
    return jax.shard_map(
        on_device,
        mesh=mesh,
        in_specs=(
            P("items", "seq", None),
            P("items", None),
            P(),
            P(),
            P(),
            P(),
            P(),
            P(),
            P("items", "seq", None),
        ),
        out_specs=(
            P("items", "seq", None),
            P("items", "seq", None),
            P("seq", None),
            P("seq", None),
            P("seq", None),
            P("seq", None),
            P("seq"),
            P("seq"),
        ),
        check_vma=False,
    )
```
